128 devices in a mesh: dp: 8 (over z, x_hi), row: 4 (over y), col: 4 (over x_lo, core).
Axes of the slice: x: 4 (x_hi: 2, x_lo: 2; x = x_hi * 2 + x_lo), y: 4, z: 4, core: 2. Of those that a mesh axis runs over, the one named last changes fastest.
Arguments:
- tokens_in: bfloat16 [16384, 2048], P(('dp', 'row'), 'col'), may hold values from -6 to 6
- segment_ids: int32 [16384], P('dp'), may hold values from 0 to 2, as said below
- attn_gain: float32 [2048], P('col'), may hold values from 0.1 to 1.9
- w_qkv: bfloat16 [2048, 4, 640], P('col', 'row'), may hold values from -0.125 to 0.125
- w_out: bfloat16 [2048, 2048], P('row', 'col'), may hold values from -2 to 2
- mlp_gain: float32 [2048], P('col'), may hold values from 0.1 to 1.9
- w_gate: bfloat16 [2048, 5632], P('col', 'row'), may hold values from -0.125 to 0.125
- w_up: bfloat16 [2048, 5632], P('col', 'row'), may hold values from -0.125 to 0.125
- w_down: bfloat16 [5632, 2048], P('row', 'col'), may hold values from -0.078125 to 0.078125
- cotangent: bfloat16 [16384, 2048], P(('dp', 'row'), 'col'), may hold values from -6 to 6
Outputs:
- out: bfloat16 [16384, 2048], P(('dp', 'row'), 'col')
- grad_in: float32 [16384, 2048], P(('dp', 'row'), 'col')
- grad_attn_gain: float32 [2048], P('col')
- grad_qkv: float32 [2048, 4, 640], P('col', 'row')
- grad_out_proj: float32 [2048, 2048], P('row', 'col')
- grad_mlp_gain: float32 [2048], P('col')
- grad_gate_proj: float32 [2048, 5632], P('col', 'row')
- grad_up_proj: float32 [2048, 5632], P('col', 'row')
- grad_down_proj: float32 [5632, 2048], P('row', 'col')
The draws below stay inside these ranges and needn't reach their ends.
Inputs may be any that keep to these rules, and one draw needn't show every extreme that they name: `segment_ids`: in each group of 2048 tokens the ids are 0, 1, 2 in order, each present; document 1 starts within the group's first eighth and ends within its last eighth.
All inputs are finite; a program needn't handle non-finite values.
Results may differ from the reference program's by a relative error of at most 0.024.
Values may be sent and summed in bfloat16 or wider, within the bound.
No kernel may reach another device: no remote copies, remote signals or barrier semaphores. Data moves between devices by JAX's collectives and lax.ppermute only.
A program may use at most 192 MiB of HBM per device.

```python
import math
import jax
import jax.numpy as jnp
from jax import lax

D = 2048
HD = 64
KVH = 4
QPG = 8
FF = 5632
GROUP_TOK = 2048
HEADS = 32
TOKENS = 16384


def draw_segment_ids(key, part):
    key = jax.random.fold_in(key, 7)
    first_key, last_key = jax.random.split(key)
    groups = TOKENS // GROUP_TOK
    firsts = jax.random.randint(first_key, (groups, 1), 1, GROUP_TOK // 8 + 1)
    lasts = jax.random.randint(last_key, (groups, 1), GROUP_TOK - GROUP_TOK // 8, GROUP_TOK)
    indices = jnp.arange(GROUP_TOK, dtype=jnp.int32)[None, :]
    labels = (indices >= firsts).astype(jnp.int32) + (indices >= lasts).astype(jnp.int32)
    return labels.reshape(TOKENS)


def level_of(rng, shape, cuts, least, top_value):
    def one(axis_at, blocks):
        steps = jax.random.uniform(jax.random.fold_in(jax.random.fold_in(rng, 6), axis_at), (blocks,), jnp.float32, least / len(cuts), top_value / len(cuts))
        return jnp.repeat(jnp.exp(steps), shape[axis_at] // blocks).reshape((-1,) + (1,) * (len(shape) - axis_at - 1))

    level = one(*cuts[0])
    for cut in cuts[1:]:
        level = level * one(*cut)
    return level


def noise(own_key, shape, spread, reach, pieces=(), kind=jnp.bfloat16):
    array = spread * jax.random.normal(own_key, shape, jnp.float32)
    if pieces:
        array = array * level_of(own_key, shape, pieces, -0.22, 0.18)
    return jnp.clip(array, -reach, reach).astype(kind)


def setup_inputs(seed: int = 0) -> dict:
    keys = jax.random.split(jax.random.key(seed), 11)
    tokens_in = noise(keys[0], (TOKENS, D), 1.0, 6.0, ((0, 32), (1, 4)))
    segment_ids = draw_segment_ids(jax.random.fold_in(keys[10], 71), 0)
    attn_gain = jnp.clip(1.0 + 0.18 * jax.random.normal(keys[2], (D,), jnp.float32), 0.1, 1.9)
    w_qkv = noise(keys[3], (D, KVH, (QPG + 2) * HD), D ** -0.5, 0.125, ((0, 4), (1, 4)))
    w_out = noise(keys[4], (HEADS * HD, D), (max(HEADS * HD // 256, 1)) ** -0.5, 2.0, ((0, 4), (1, 4)))
    mlp_gain = jnp.clip(1.0 + 0.18 * jax.random.normal(keys[5], (D,), jnp.float32), 0.1, 1.9)
    w_gate = noise(keys[6], (D, FF), D ** -0.5, 0.125, ((0, 4), (1, 4)))
    w_up = noise(keys[7], (D, FF), D ** -0.5, 0.125, ((0, 4), (1, 4)))
    w_down = noise(keys[8], (FF, D), FF ** -0.5, 0.078125, ((0, 4), (1, 4)))
    cotangent = noise(keys[9], (TOKENS, D), 1.0, 6.0, ((0, 32), (1, 4)))
    return dict(tokens_in=tokens_in, segment_ids=segment_ids, attn_gain=attn_gain, w_qkv=w_qkv, w_out=w_out, mlp_gain=mlp_gain, w_gate=w_gate, w_up=w_up, w_down=w_down, cotangent=cotangent)


highest = lax.Precision.HIGHEST
norm_eps = 1e-05
rope_base = 10000.0

@jax.custom_vjp
def low(v):
    return lax.optimization_barrier(v.astype(jnp.bfloat16)).astype(jnp.float32)

@jax.custom_vjp
def low_back(v):
    return v

def low_keep(v):
    return (low(v), None)

def low_pass(kept, grad):
    return (grad,)

def back_keep(v):
    return (v, None)

def back_low(kept, grad):
    return (low(grad),)
low.defvjp(low_keep, low_pass)
low_back.defvjp(back_keep, back_low)

def matmul(left, right):
    return jnp.dot(left, right, precision=highest)

def rms_scale(values):
    return lax.rsqrt(lax.optimization_barrier(jnp.mean(values * values, axis=-1, keepdims=True)) + norm_eps)

def positions_of(seg_group):
    indices = jnp.arange(seg_group.shape[0], dtype=jnp.int32)
    previous = jnp.concatenate([seg_group[:1] - 1, seg_group[:-1]])
    starts = lax.cummax(jnp.where(seg_group != previous, indices, 0), axis=0)
    return indices - starts

def rotary(positions):
    half_dim = HD // 2
    inverse_freq = rope_base ** (-jnp.arange(half_dim, dtype=jnp.float32) * 2.0 / HD)
    angles = positions.astype(jnp.float32)[:, None] * inverse_freq[None, :]
    cosine = jnp.concatenate([jnp.cos(angles), jnp.cos(angles)], axis=-1)
    sine_tab = jnp.concatenate([jnp.sin(angles), jnp.sin(angles)], axis=-1)
    return (cosine, sine_tab)

def rotate(values, cosine, sine_tab):
    half_dim = values.shape[-1] // 2
    turned = jnp.concatenate([-values[..., half_dim:], values[..., :half_dim]], axis=-1)
    return values * cosine + turned * sine_tab

def attention(query, key_all, value_all, seg_group):
    length = seg_group.shape[0]
    span = math.gcd(length, 512)
    indices = jnp.arange(length, dtype=jnp.int32)
    score_scale = HD ** (-0.5)

    def one_block(first_row):
        query_rows = lax.dynamic_slice_in_dim(query, first_row, span, 0)
        query_seg = lax.dynamic_slice_in_dim(seg_group, first_row, span, 0)
        query_place = first_row + jnp.arange(span, dtype=jnp.int32)
        scores = low_back(jnp.einsum('tgqd,kgd->gqtk', query_rows, key_all, precision=highest) * score_scale)
        allowed = (query_seg[:, None] == seg_group[None, :]) & (indices[None, :] <= query_place[:, None])
        scores = jnp.where(allowed, scores, -1e+30)
        running_top = lax.optimization_barrier(jnp.max(scores, axis=-1, keepdims=True))
        weights = jnp.exp(scores - running_top)
        probabilities = low(weights / lax.optimization_barrier(jnp.sum(weights, axis=-1, keepdims=True)))
        return jnp.einsum('gqtk,kgd->tgqd', probabilities, value_all, precision=highest)
    firsts = jnp.arange(0, length, span, dtype=jnp.int32)
    blocks = lax.map(jax.checkpoint(one_block), firsts)
    return blocks.reshape(query.shape)

def layer(inputs, attn_gain, w_qkv, w_out, mlp_gain, w_gate, w_up, w_down, seg_group):
    length = inputs.shape[0]
    cosine, sine_tab = rotary(positions_of(seg_group))
    normed_one = low(inputs * rms_scale(inputs) * attn_gain)
    qkv = low_back(matmul(normed_one, w_qkv.reshape(D, -1))).reshape(length, KVH, QPG + 2, HD)
    query = low(rotate(qkv[:, :, :QPG], cosine[:, None, None], sine_tab[:, None, None]))
    key_all = low(rotate(qkv[:, :, QPG], cosine[:, None], sine_tab[:, None]))
    value_all = low(qkv[:, :, QPG + 1])
    mixed = attention(query, key_all, value_all, seg_group)
    heads_flat = low_back(low(mixed)).reshape(length, KVH * QPG * HD)
    hidden = inputs + low_back(matmul(heads_flat, w_out))
    normed_two = low(hidden * rms_scale(hidden) * mlp_gain)
    gate_vals = low_back(matmul(normed_two, w_gate))
    up_vals = low_back(matmul(normed_two, w_up))
    inner = low(jax.nn.silu(gate_vals) * up_vals)
    return hidden + low_back(matmul(inner, w_down))

def reference(tokens_in, segment_ids, attn_gain, w_qkv, w_out, mlp_gain, w_gate, w_up, w_down, cotangent):
    params = tuple((p.astype(jnp.float32) for p in (attn_gain, w_qkv, w_out, mlp_gain, w_gate, w_up, w_down)))
    groups = tokens_in.shape[0] // GROUP_TOK
    inputs_all = tokens_in.astype(jnp.float32).reshape(groups, GROUP_TOK, D)
    cots_all = cotangent.astype(jnp.float32).reshape(groups, GROUP_TOK, D)
    segs_all = segment_ids.reshape(groups, GROUP_TOK)

    def step(totals, item):
        inputs, cot_group, seg_group = item

        def forward(inputs, gain_a, weight_qkv, weight_out, gain_m, weight_gate, weight_up, weight_down):
            return layer(inputs, gain_a, weight_qkv, weight_out, gain_m, weight_gate, weight_up, weight_down, seg_group)
        result, pull = jax.vjp(forward, inputs, *params)
        grads = pull(cot_group)
        totals = tuple((a + b for a, b in zip(totals, grads[1:])))
        return (totals, (result, grads[0]))
    zeros = tuple((jnp.zeros_like(p) for p in params))
    totals, (results, grad_inputs) = lax.scan(step, zeros, (inputs_all, cots_all, segs_all))
    return (results.reshape(-1, D).astype(jnp.bfloat16), grad_inputs.reshape(-1, D), totals[0], totals[1], totals[2], totals[3], totals[4], totals[5], totals[6])
```

```python
import functools

import jax
import jax.numpy as jnp
from jax import lax
from jax.experimental import pallas as pl
from jax.experimental.pallas import tpu as pltpu
from jax.sharding import Mesh
from jax.sharding import PartitionSpec as P

HD = 64
norm_eps = 1e-05
rope_base = 10000.0
masked = -1e30

COL = ("xl", "k")
RING = ("xh", "xl")
BF16 = jnp.bfloat16
F32 = jnp.float32


def trade(values, axes, mask, size=4):
    return lax.ppermute(values, axes, [(i, i ^ mask) for i in range(size)])


def trade_row(values, mask):
    return trade(values, "y", mask)


def trade_col(values, mask):
    return trade(values, COL, mask)


def trade_core(values):
    return trade(values, "k", 1, 2)


def trade_ring(values, mask):
    return trade(values, RING, mask)


def gather_row(values):
    return jnp.concatenate([values] + [trade_row(values, j) for j in (1, 2, 3)], axis=0)


def sum_row(partial):
    size = partial.shape[0] // 4
    own = partial[:size].astype(F32)
    for j in (2, 1, 3):
        own = own + trade_row(partial[j * size : (j + 1) * size], j).astype(F32)
    return own


def to_full_width(values, col):
    size = values.shape[0] // 4
    parts = [lax.dynamic_slice_in_dim(values, (col ^ m) * size, size, 0) for m in range(4)]
    return jnp.concatenate([parts[0]] + [trade_col(parts[m], m) for m in (1, 2, 3)], axis=1)


def to_blocks(values, core, low):
    width = values.shape[1] // 4
    parts = [values[:, :width]]
    parts += [trade_col(values[:, m * width : (m + 1) * width], m) for m in (1, 2, 3)]
    a, b, c, d = parts
    a, b = jnp.where(core == 0, a, b), jnp.where(core == 0, b, a)
    c, d = jnp.where(core == 0, c, d), jnp.where(core == 0, d, c)
    first, second = jnp.concatenate([a, b], 0), jnp.concatenate([c, d], 0)
    return jnp.concatenate(
        [jnp.where(low == 0, first, second), jnp.where(low == 0, second, first)], 0
    )


def gather_weight(shard, axis):
    half = shard.shape[0] // 2
    other = jnp.concatenate([trade_ring(shard[:half], 1), trade_ring(shard[half:], 3)], axis=0)
    return jnp.concatenate([shard, trade_core(shard), other, trade_core(other)], axis=axis)


def add_low(*terms):
    total = terms[0].astype(F32)
    for term in terms[1:]:
        total = total + term.astype(F32)
    return total.astype(BF16)


def sum_core(parts):
    return (
        add_low(parts[0], trade_core(parts[1])),
        add_low(parts[2], trade_core(parts[3])),
    )


def ring_scatter(mine, theirs, high):
    half = mine.shape[0] // 2
    take = lambda values, which: lax.dynamic_slice_in_dim(values, which * half, half, 0)
    return add_low(
        take(mine, high),
        trade_ring(take(theirs, high), 1),
        trade_ring(take(theirs, 1 - high), 3),
        trade_ring(take(mine, 1 - high), 2),
    )


def ring_gather(values, high):
    other = trade_ring(values, 2)
    return jnp.concatenate(
        [jnp.where(high == 0, values, other), jnp.where(high == 0, other, values)], axis=0
    )


def reduce_z_first(parts, high):
    mine, theirs = sum_core(parts)
    both = lax.psum_scatter(jnp.stack([mine, theirs]), "z", scatter_dimension=1, tiled=True)
    total = ring_gather(ring_scatter(both[0], both[1], high), high)
    return lax.all_gather(total, "z", axis=0, tiled=True).astype(F32)


def reduce_ring_first(parts, high):
    mine, theirs = sum_core(parts)
    part = ring_scatter(mine, theirs, high)
    total = lax.psum_scatter(part, "z", scatter_dimension=0, tiled=True)
    total = lax.all_gather(total, "z", axis=0, tiled=True)
    return ring_gather(total, high).astype(F32)


def reduce_gain(values):
    total = values
    for m in (1, 3, 2):
        total = total + trade_row(values, m)
    width = total.shape[1] // 4
    own = total[:, :width]
    for m in (1, 2, 3):
        own = own + trade_col(total[:, m * width : (m + 1) * width], m)
    whole = own
    for m in (1, 3, 2):
        whole = whole + trade(own, "z", m)
    return (whole + trade(whole, "xh", 1, 2))[0]


def product(left, right, dims, kind=F32):
    return lax.dot_general(left, right, (dims, ((), ())), preferred_element_type=F32).astype(kind)


def scale_of(values):
    return lax.rsqrt(jnp.mean(values * values, axis=1, keepdims=True) + norm_eps)


def norm_back(values, scale, gain, upstream):
    weighted = upstream * gain
    inner = jnp.mean(weighted * values, axis=1, keepdims=True)
    return scale * weighted - values * (scale**3 * inner)


def attend(place_ref, q_ref, kn_ref, vt_ref, koff_ref, qpos_ref, qstart_ref, o_ref, low_ref, lse_ref):
    row = place_ref[0]
    span = kn_ref.shape[1]
    size = span // 4
    pairs = q_ref.shape[0] // (2 * HD)

    def one_block(block, carry):
        at = pl.multiple_of(block * size, size)
        mine = block ^ row
        qpos = qpos_ref[:, pl.ds(at, size)]
        qstart = qstart_ref[:, pl.ds(at, size)]
        for pair in range(pairs):
            first = pair * 2 * HD
            query = jnp.concatenate(
                [
                    q_ref[first : first + HD, pl.ds(at, size)],
                    q_ref[first + HD : first + 2 * HD, pl.ds(at, size)],
                ],
                axis=1,
            )

            def chunk(number, state, diagonal):
                top, total, accum = state
                where = number ^ row
                scores = jnp.dot(kn_ref[where], query, preferred_element_type=F32)
                keys = koff_ref[...] + number * span
                allowed = keys >= qstart
                if diagonal:
                    allowed = allowed & (keys <= qpos)
                allowed = jnp.concatenate([allowed, allowed], axis=1)
                scores = jnp.where(allowed, scores, masked)
                new_top = jnp.maximum(top, jnp.max(scores, axis=0, keepdims=True))
                weights = jnp.exp(scores - new_top)
                shrink = jnp.exp(top - new_top)
                total = total * shrink + jnp.sum(weights, axis=0, keepdims=True)
                accum = accum * shrink + jnp.dot(
                    vt_ref[where], weights.astype(BF16), preferred_element_type=F32
                )
                return new_top, total, accum

            state = (
                jnp.full((1, 2 * size), masked, F32),
                jnp.zeros((1, 2 * size), F32),
                jnp.zeros((HD, 2 * size), F32),
            )
            state = chunk(mine, state, True)
            top, total, accum = lax.fori_loop(
                0, mine, lambda number, state: chunk(number, state, False), state
            )
            result = accum / total
            lse = top + jnp.log(total)
            for part in range(2):
                spot = first + part * HD
                piece = result[:, part * size : (part + 1) * size]
                o_ref[spot : spot + HD, pl.ds(at, size)] = piece
                low_ref[spot : spot + HD, pl.ds(at, size)] = piece.astype(BF16)
                lse_ref[pair * 2 + part : pair * 2 + part + 1, pl.ds(at, size)] = lse[
                    :, part * size : (part + 1) * size
                ]
        return carry

    lax.fori_loop(0, 4, one_block, 0)


def attend_back(
    place_ref, q_ref, kn_ref, kt_ref, vn_ref, koff_ref, qpos_ref, qstart_ref, o_ref, lse_ref, go_ref,
    gq_ref, gk_ref, gv_ref,
):
    row = place_ref[0]
    span = kn_ref.shape[1]
    size = span // 4
    pairs = q_ref.shape[0] // (2 * HD)
    gk_ref[...] = jnp.zeros_like(gk_ref)
    gv_ref[...] = jnp.zeros_like(gv_ref)
    last = (((1,), (1,)), ((), ()))

    def one_block(block, carry):
        at = pl.multiple_of(block * size, size)
        mine = block ^ row
        qpos = qpos_ref[:, pl.ds(at, size)]
        qstart = qstart_ref[:, pl.ds(at, size)]
        for pair in range(pairs):
            first = pair * 2 * HD
            both = lambda ref: jnp.concatenate(
                [
                    ref[first : first + HD, pl.ds(at, size)],
                    ref[first + HD : first + 2 * HD, pl.ds(at, size)],
                ],
                axis=1,
            )
            query, grad_out = both(q_ref), both(go_ref)
            delta = jnp.sum(grad_out.astype(F32) * both(o_ref), axis=0, keepdims=True)
            lse = jnp.concatenate(
                [
                    lse_ref[2 * pair : 2 * pair + 1, pl.ds(at, size)],
                    lse_ref[2 * pair + 1 : 2 * pair + 2, pl.ds(at, size)],
                ],
                axis=1,
            )

            def chunk(number, grad_query, diagonal):
                where = number ^ row
                scores = jnp.dot(kn_ref[where], query, preferred_element_type=F32)
                keys = koff_ref[...] + number * span
                allowed = keys >= qstart
                if diagonal:
                    allowed = allowed & (keys <= qpos)
                allowed = jnp.concatenate([allowed, allowed], axis=1)
                probs = jnp.exp(jnp.where(allowed, scores - lse, masked))
                grad_probs = jnp.dot(vn_ref[where], grad_out, preferred_element_type=F32)
                grad_scores = (probs * (grad_probs - delta)).astype(BF16)
                gv_ref[where] += lax.dot_general(
                    grad_out, probs.astype(BF16), last, preferred_element_type=F32
                )
                gk_ref[where] += lax.dot_general(
                    query, grad_scores, last, preferred_element_type=F32
                )
                return grad_query + jnp.dot(
                    kt_ref[where], grad_scores, preferred_element_type=F32
                )

            grad_query = chunk(mine, jnp.zeros((HD, 2 * size), F32), True)
            grad_query = lax.fori_loop(
                0, mine, lambda number, total: chunk(number, total, False), grad_query
            )
            for part in range(2):
                spot = first + part * HD
                gq_ref[spot : spot + HD, pl.ds(at, size)] = (
                    grad_query[:, part * size : (part + 1) * size] * HD**-0.5
                )
        return carry

    lax.fori_loop(0, 4, one_block, 0)


def kernel_call(body, out_shape, operands, flops):
    moved = sum(x.size * x.dtype.itemsize for x in operands)
    return pl.pallas_call(
        body,
        out_shape=out_shape,
        in_specs=[pl.BlockSpec(memory_space=pltpu.SMEM)]
        + [pl.BlockSpec(memory_space=pltpu.VMEM)] * (len(operands) - 1),
        out_specs=jax.tree.map(lambda _: pl.BlockSpec(memory_space=pltpu.VMEM), out_shape),
        compiler_params=pltpu.CompilerParams(vmem_limit_bytes=40 * 1024 * 1024),
        cost_estimate=pl.CostEstimate(flops=flops, bytes_accessed=moved, transcendentals=0),
    )(*operands)


def turn(pairs, cosine, sine):
    first, second = pairs[:, 0], pairs[:, 1]
    return jnp.stack([first * cosine - second * sine, second * cosine + first * sine], axis=1)


def turn_back(pairs, cosine, sine):
    first, second = pairs[:, 0], pairs[:, 1]
    return jnp.stack([first * cosine + second * sine, second * cosine - first * sine], axis=1)


def on_device(
    tokens_in, segment_ids, attn_gain, w_qkv, w_out, mlp_gain, w_gate, w_up, w_down, cotangent
):
    group = segment_ids.shape[0]
    span = group // 4
    size = span // 4
    units = w_gate.shape[1]
    slots = w_qkv.shape[2] // HD
    heads = slots - 2
    high, row = lax.axis_index("xh"), lax.axis_index("y")
    low, core = lax.axis_index("xl"), lax.axis_index("k")
    col = low * 2 + core

    gains = jnp.stack([attn_gain, mlp_gain])
    gains = jnp.concatenate([gains] + [trade_col(gains, m) for m in (1, 2, 3)], axis=1)
    inputs = to_full_width(tokens_in, col).astype(F32)
    scale_one = scale_of(inputs)
    rows_one = gather_row((inputs * scale_one * gains[0]).astype(BF16))
    full_qkv = gather_weight(w_qkv.reshape(w_qkv.shape[0], -1), 0)
    full_out = gather_weight(w_out, 1)
    full_gu = gather_weight(jnp.concatenate([w_gate, w_up], axis=1), 0)
    full_down = gather_weight(w_down, 1)
    grad_rows = gather_row(to_full_width(cotangent, col))

    indices = jnp.arange(group, dtype=jnp.int32)
    previous = jnp.concatenate([segment_ids[:1] - 1, segment_ids[:-1]])
    starts = lax.cummax(jnp.where(segment_ids != previous, indices, 0), axis=0)
    bases = [(row ^ place) * span + col * size for place in range(4)]
    my_starts = jnp.concatenate([lax.dynamic_slice_in_dim(starts, b, size, 0) for b in bases])
    lanes = jnp.arange(size, dtype=jnp.int32)
    my_index = jnp.concatenate([lanes + b for b in bases])
    half_dim = HD // 2
    inverse_freq = rope_base ** (-jnp.arange(half_dim, dtype=F32) * 2.0 / HD)
    angles = inverse_freq[:, None] * (my_index - my_starts).astype(F32)[None, :]
    cosine, sine = jnp.cos(angles), jnp.sin(angles)
    key_offset = jnp.concatenate([lanes + (col ^ m) * size for m in range(4)])
    key_offset = jnp.broadcast_to(key_offset[:, None], (span, size))
    place = jnp.stack([row, col]).astype(jnp.int32)
    qpos, qstart = my_index[None, :], my_starts[None, :]

    qkv = product(full_qkv, rows_one, ((0,), (1,)))
    turned = turn(qkv[: (heads + 1) * HD].reshape(heads + 1, 2, half_dim, span), cosine, sine)
    turned = turned.reshape(-1, span)
    query = (turned[: heads * HD] * HD**-0.5).astype(BF16)
    pairs = jnp.concatenate([turned[heads * HD :], qkv[(heads + 1) * HD :]], axis=0).astype(BF16)
    all_pairs = jnp.stack([pairs] + [trade_col(pairs, m) for m in (1, 2, 3)])
    all_pairs = all_pairs.reshape(4, 2, HD, 4, size).transpose(1, 3, 2, 0, 4)
    all_pairs = all_pairs.reshape(2, 4, HD, span)
    natural = all_pairs.swapaxes(2, 3)
    kt, vt, kn, vn = all_pairs[0], all_pairs[1], natural[0], natural[1]
    shape = lambda kind, *dims: jax.ShapeDtypeStruct(dims, kind)
    flops = 2 * 2 * heads * HD * span * group
    mixed, mixed_low, lse = kernel_call(
        attend,
        (shape(F32, heads * HD, span), shape(BF16, heads * HD, span), shape(F32, heads, span)),
        (place, query, kn, vt, key_offset, qpos, qstart),
        flops,
    )
    branch = product(mixed_low, full_out, ((0,), (0,)), BF16)
    hidden = inputs + sum_row(branch)
    scale_two = scale_of(hidden)
    rows_two = gather_row((hidden * scale_two * gains[1]).astype(BF16))
    gate_up = product(rows_two, full_gu, ((1,), (0,)))
    gate, up = gate_up[:, :units], gate_up[:, units:]
    grad_inner = product(grad_rows, full_down, ((1,), (1,)))
    sig = jax.nn.sigmoid(gate)
    inner = (gate * sig * up).astype(BF16)
    grad_gate = grad_inner * up * sig * (1.0 + gate * (1.0 - sig))
    grad_up = grad_inner * gate * sig
    grad_pair = jnp.concatenate([grad_gate, grad_up], axis=1).astype(BF16)
    part_two = product(grad_pair, full_gu, ((1,), (1,)), BF16)
    grad_n2 = sum_row(part_two)
    gain_two = jnp.sum(grad_n2 * hidden * scale_two, axis=0, keepdims=True)
    grad_hidden = grad_rows[:size].astype(F32) + norm_back(
        hidden, scale_two, gains[1], grad_n2
    )
    branch_rows = gather_row(grad_hidden.astype(BF16))
    grad_heads = product(full_out, branch_rows, ((1,), (1,)), BF16)
    gq, gk, gv = kernel_call(
        attend_back,
        (shape(F32, heads * HD, span), shape(F32, 4, HD, span), shape(F32, 4, HD, span)),
        (place, query, kn, kt, vn, key_offset, qpos, qstart, mixed, lse, grad_heads),
        flops * 5 // 2,
    )
    grad_pairs = jnp.stack([gk, gv]).astype(BF16).reshape(2, 4, HD, 4, size)
    own_pairs = grad_pairs[:, :, :, 0].astype(F32)
    for m in (1, 2, 3):
        own_pairs = own_pairs + trade_col(grad_pairs[:, :, :, m], m).astype(F32)
    own_pairs = own_pairs.transpose(0, 2, 1, 3).reshape(2, HD, span)
    grad_turned = jnp.concatenate([gq.reshape(heads, HD, span), own_pairs[:1]])
    grad_turned = turn_back(
        grad_turned.reshape(heads + 1, 2, half_dim, span), cosine, sine
    ).reshape(-1, span)
    grad_qkv = jnp.concatenate([grad_turned, own_pairs[1]], axis=0).astype(BF16)
    part_one = product(grad_qkv, full_qkv, ((0,), (1,)), BF16)
    grad_n1 = sum_row(part_one)
    gain_one = jnp.sum(grad_n1 * inputs * scale_one, axis=0, keepdims=True)
    grad_in = grad_hidden + norm_back(inputs, scale_one, gains[0], grad_n1)
    grad_in = to_blocks(grad_in, core, low)
    result = (hidden + sum_row(product(inner, full_down, ((1,), (0,)), BF16))).astype(BF16)
    result = to_blocks(result, core, low)

    width = rows_one.shape[1] // 4
    cut_d = lambda v: [v[:, m * width : (m + 1) * width] for m in range(4)]
    token_sum = lambda a, b: product(a, b, ((0,), (0,)), BF16)
    down_parts = [token_sum(inner, piece) for piece in cut_d(grad_rows)]
    gate_parts = [token_sum(piece, grad_pair[:, :units]) for piece in cut_d(rows_two)]
    up_parts = [token_sum(piece, grad_pair[:, units:]) for piece in cut_d(rows_two)]
    out_parts = [product(mixed_low, piece, ((1,), (0,)), BF16) for piece in cut_d(branch_rows)]
    qkv_parts = [product(piece, grad_qkv, ((0,), (1,)), BF16) for piece in cut_d(rows_one)]
    return (
        result,
        grad_in,
        reduce_gain(gain_one),
        reduce_z_first(qkv_parts, high).reshape(w_qkv.shape),
        reduce_ring_first(out_parts, high),
        reduce_gain(gain_two),
        reduce_z_first(gate_parts, high),
        reduce_ring_first(up_parts, high),
        reduce_z_first(down_parts, high),
    )


def solution(mesh):
    dp, rows, cols = mesh.devices.shape
    fine = Mesh(
        mesh.devices.reshape(dp // 2, 2, rows, cols // 2, 2), ("z", "xh", "y", "xl", "k")
    )
    tokens = P(("z", "xh", "y"), COL)
    in_specs = (
        tokens, P(("z", "xh")), P(COL), P(COL, "y", None), P("y", COL), P(COL),
        P(COL, "y"), P(COL, "y"), P("y", COL), tokens,
    )
    out_specs = (
        tokens, tokens, P(COL), P(COL, "y", None), P("y", COL), P(COL),
        P(COL, "y"), P(COL, "y"), P("y", COL),
    )
    return jax.shard_map(
        on_device, mesh=fine, in_specs=in_specs, out_specs=out_specs, check_vma=False
    )
```

```python
import functools

import jax
import jax.numpy as jnp
from jax import lax
from jax.experimental import pallas as pl
from jax.experimental.pallas import tpu as pltpu
from jax.sharding import Mesh
from jax.sharding import PartitionSpec as P

HD = 64
norm_eps = 1e-05
rope_base = 10000.0
masked = -1e30

COL = ("xl", "k")
RING = ("xh", "xl")
BF16 = jnp.bfloat16
F32 = jnp.float32


def trade(values, axes, mask, size=4):
    return lax.ppermute(values, axes, [(i, i ^ mask) for i in range(size)])


def trade_row(values, mask):
    return trade(values, "y", mask)


def trade_col(values, mask):
    return trade(values, COL, mask)


def trade_core(values):
    return trade(values, "k", 1, 2)


def trade_ring(values, mask):
    return trade(values, RING, mask)


def trade_deep(values, mask):
    return trade(values, "z", mask)


def after(values, *earlier):
    return lax.optimization_barrier((values, earlier))[0]


def pick(bit, zero, one):
    return jnp.where(bit == 0, zero, one)


def in_order(parts, index):
    low, high = index % 2, index // 2
    a, b, c, d = parts
    a, b = pick(low, a, b), pick(low, b, a)
    c, d = pick(low, c, d), pick(low, d, c)
    return [pick(high, a, c), pick(high, b, d), pick(high, c, a), pick(high, d, b)]


def cut(values, count, axis):
    return jnp.split(values, count, axis)


def gather_row(values):
    return lax.all_gather(values, "y", axis=0, tiled=True)


def sum_row(partial):
    return lax.psum_scatter(partial, "y", scatter_dimension=0, tiled=True)


def spread_row(values):
    return [values] + [trade_row(values, j) for j in (1, 2, 3)]


def row_parts(partial, row):
    size = partial.shape[0] // 4
    return [lax.dynamic_slice_in_dim(partial, (row ^ j) * size, size, 0) for j in range(4)]


def collect_row(parts):
    return [parts[0]] + [trade_row(parts[j], j) for j in (1, 2, 3)]


def by_width(parts, low):
    return [
        pick(low, parts[core + 2 * place], parts[core + 2 * (1 - place)])
        for core in range(2)
        for place in range(2)
    ]


def of_width(values, low):
    blocks = cut(values, 4, 1)
    return [
        pick(low, blocks[2 * core + place], blocks[2 * core + 1 - place])
        for place in range(2)
        for core in range(2)
    ]


def to_full_width(values, col, *alongside):
    size = values[0].shape[0] // 4
    send = lambda m: jnp.concatenate(
        [lax.dynamic_slice_in_dim(v, (col ^ m) * size, size, 0) for v in values], axis=1
    )
    parts = [send(0)] + [trade_col(send(m), m) for m in (1, 2, 3)]
    parts, alongside = lax.optimization_barrier((parts, alongside))
    parts = [cut(part, len(values), 1) for part in parts]
    rows = [
        jnp.concatenate(by_width([part[i] for part in parts], col // 2), axis=1)
        for i in range(len(values))
    ]
    return rows, alongside


def to_blocks(values, col):
    parts = of_width(values, col // 2)
    kind = values.dtype
    parts = [parts[0]] + [trade_col(parts[m].astype(BF16), m).astype(kind) for m in (1, 2, 3)]
    return jnp.concatenate(in_order(parts, col), axis=0)


def ring_halves(first, second, low, axis, *earlier):
    shard = jnp.concatenate([first, second])
    other = [trade_ring(first, 1), trade_ring(second, 3)]
    other = jnp.concatenate(after(other, *earlier))
    both = [pick(low, shard, other), pick(low, other, shard)]
    return jnp.concatenate(both, axis=axis)


def add_low(*terms):
    total = terms[0].astype(F32)
    for term in terms[1:]:
        total = total + term.astype(F32)
    return total.astype(BF16)


def at(values, index):
    return lax.dynamic_index_in_dim(values, index, 0, keepdims=False)


def ring_parts(blocks, low, high):
    half = blocks[0].shape[1] // 2
    take = lambda place, which: jnp.concatenate(
        [
            lax.dynamic_slice(v, (place, which * half, 0), (1, half, v.shape[2]))[0]
            for v in blocks
        ],
        axis=1,
    )
    return [take(low, high), take(1 - low, high), take(low, 1 - high), take(1 - low, 1 - high)]


def deep_parts(blocks, deep):
    size = blocks.shape[-2] // 4
    return [
        lax.dynamic_slice_in_dim(blocks, (deep ^ j) * size, size, blocks.ndim - 2) for j in range(4)
    ]


def trade_near(parts, trader):
    return [trader(parts[1], 1), trader(parts[3], 3)]


def exchange(parts, trader):
    return add_low(parts[0], *lax.optimization_barrier([trader(parts[j], j) for j in (1, 2, 3)]))


def ring_gather(values, high):
    other = trade_ring(values, 2)
    return jnp.concatenate([pick(high, values, other), pick(high, other, values)], axis=0)


def deep_gather(values, deep):
    parts = lax.optimization_barrier([values] + [trade_deep(values, j) for j in (1, 2, 3)])
    return jnp.concatenate(in_order(parts, deep), axis=0)


def product(left, right, dims, kind=F32):
    return lax.dot_general(left, right, (dims, ((), ())), preferred_element_type=F32).astype(kind)


def scale_of(values):
    return lax.rsqrt(jnp.mean(values * values, axis=1, keepdims=True) + norm_eps)


def add_and_norm(base_ref, part_ref, hidden_ref, normed_ref):
    hidden = base_ref[...] + part_ref[...].astype(F32)
    hidden_ref[...] = hidden
    normed_ref[...] = (hidden * scale_of(hidden)).astype(BF16)


def norm_back(values, weighted, passed):
    scale = scale_of(values)
    inner = jnp.mean(weighted * values, axis=1, keepdims=True)
    return passed + (scale * weighted - values * (scale**3 * inner))


def norm_back_low(values_ref, part_ref, passed_ref, grad_ref, low_ref):
    grad = norm_back(values_ref[...], part_ref[...].astype(F32), passed_ref[...].astype(F32))
    grad_ref[...] = grad
    low_ref[...] = grad.astype(BF16)


def norm_back_sum(values_ref, p0, p1, p2, p3, passed_ref, grad_ref):
    weighted = (p0[...].astype(F32) + p1[...].astype(F32)) + (p2[...].astype(F32) + p3[...].astype(F32))
    grad_ref[...] = norm_back(values_ref[...], weighted, passed_ref[...])


def turn(first, second, cosine, sine):
    return first * cosine - second * sine, second * cosine + first * sine


def project(x_ref, mine_ref, theirs_ref, cos_ref, sin_ref, q_ref, kv_ref):
    width = mine_ref.shape[1]
    slots = kv_ref.shape[0] + q_ref.shape[0]
    total = None
    for core, weights in enumerate((mine_ref, theirs_ref)):
        for place in range(2):
            spot = (2 * core + place) * width
            term = jnp.dot(
                x_ref[:, spot : spot + width], weights[place, :, :slots], preferred_element_type=F32
            )
            total = term if total is None else total + term
    turned = total.T
    cosine, sine = cos_ref[...], sin_ref[...]
    half = HD // 2
    heads = q_ref.shape[0] // HD
    for head in range(heads + 1):
        spot = head * HD
        first, second = turn(
            turned[spot : spot + half], turned[spot + half : spot + HD], cosine, sine
        )
        if head < heads:
            q_ref[spot : spot + half, :] = (first * HD**-0.5).astype(BF16)
            q_ref[spot + half : spot + HD, :] = (second * HD**-0.5).astype(BF16)
        else:
            kv_ref[:half, :] = first.astype(BF16)
            kv_ref[half:HD, :] = second.astype(BF16)
    kv_ref[HD:, :] = turned[(heads + 1) * HD :].astype(BF16)


def lay_keys(pairs, kt_ref, vt_ref, kn_ref, vn_ref):
    size = pairs[0].shape[1] // 4
    for block in range(4):
        for m, pair in enumerate(pairs):
            piece = pair[:, block * size : (block + 1) * size]
            spot = slice(m * size, (m + 1) * size)
            kt_ref[block, :, spot] = piece[:HD]
            if vt_ref is not None:
                vt_ref[block, :, spot] = piece[HD:]
            natural = piece.astype(F32).T.astype(BF16)
            kn_ref[block, spot, :] = natural[:, :HD]
            vn_ref[block, spot, :] = natural[:, HD:]


def two_heads(ref, first, spot, size):
    return jnp.concatenate(
        [ref[first : first + HD, pl.ds(spot, size)], ref[first + HD : first + 2 * HD, pl.ds(spot, size)]],
        axis=1,
    )


def admitted(koff_ref, start, qpos, qstart, diagonal):
    keys = koff_ref[...] + start
    allowed = keys >= qstart
    if diagonal:
        allowed = allowed & (keys <= qpos)
    return jnp.concatenate([allowed, allowed], axis=1)


def attend(
    q_ref, p0, p1, p2, p3, koff_ref, qpos_ref, qstart_ref,
    o_ref, low_ref, lse_ref, kt_ref, vt_ref, kn_ref, vn_ref,
):
    span = kn_ref.shape[1]
    size = span // 4
    pairs = q_ref.shape[0] // (2 * HD)
    lay_keys((p0, p1, p2, p3), kt_ref, vt_ref, kn_ref, vn_ref)

    def one_block(block, carry):
        spot = pl.multiple_of(block * size, size)
        qpos = qpos_ref[:, pl.ds(spot, size)]
        qstart = qstart_ref[:, pl.ds(spot, size)]
        queries = [two_heads(q_ref, pair * 2 * HD, spot, size) for pair in range(pairs)]

        def chunk(number, state, diagonal):
            keys, values = kn_ref[number], vt_ref[number]
            allowed = admitted(koff_ref, number * span, qpos, qstart, diagonal)
            fresh = []
            for query, (top, total, accum) in zip(queries, state):
                scores = jnp.dot(keys, query, preferred_element_type=F32)
                scores = jnp.where(allowed, scores, masked)
                new_top = jnp.maximum(top, jnp.max(scores, axis=0, keepdims=True))
                weights = jnp.exp(scores - new_top)
                shrink = jnp.exp(top - new_top)
                total = total * shrink + jnp.sum(weights, axis=0, keepdims=True)
                accum = accum * shrink + jnp.dot(
                    values, weights.astype(BF16), preferred_element_type=F32
                )
                fresh.append((new_top, total, accum))
            return tuple(fresh)

        empty = (
            jnp.full((1, 2 * size), masked, F32),
            jnp.zeros((1, 2 * size), F32),
            jnp.zeros((HD, 2 * size), F32),
        )
        state = chunk(block, (empty,) * pairs, True)
        state = lax.fori_loop(0, block, lambda number, state: chunk(number, state, False), state)
        for pair, (top, total, accum) in enumerate(state):
            result = accum / total
            lse = top + jnp.log(total)
            for part in range(2):
                first = (2 * pair + part) * HD
                piece = result[:, part * size : (part + 1) * size]
                o_ref[first : first + HD, pl.ds(spot, size)] = piece
                low_ref[first : first + HD, pl.ds(spot, size)] = piece.astype(BF16)
                lse_ref[2 * pair + part : 2 * pair + part + 1, pl.ds(spot, size)] = lse[
                    :, part * size : (part + 1) * size
                ]
        return carry

    lax.fori_loop(0, 4, one_block, 0)


def attend_back(
    q_ref, p0, p1, p2, p3, koff_ref, qpos_ref, qstart_ref, o_ref, lse_ref, go_ref, cos_ref, sin_ref, *refs,
    first_pair, pairs, last_call,
):
    if last_call:
        gk_in, gv_in, gq_ref, g0, g1, g2, g3, kt_ref, kn_ref, vn_ref, gk_ref, gv_ref = refs
    else:
        gq_ref, gk_ref, gv_ref, kt_ref, kn_ref, vn_ref = refs
    span = kn_ref.shape[1]
    size = span // 4
    lay_keys((p0, p1, p2, p3), kt_ref, None, kn_ref, vn_ref)
    gk_ref[...] = gk_in[...] if last_call else jnp.zeros_like(gk_ref)
    gv_ref[...] = gv_in[...] if last_call else jnp.zeros_like(gv_ref)
    last = (((1,), (1,)), ((), ()))

    def one_block(block, carry):
        spot = pl.multiple_of(block * size, size)
        qpos = qpos_ref[:, pl.ds(spot, size)]
        qstart = qstart_ref[:, pl.ds(spot, size)]
        cosine, sine = cos_ref[:, pl.ds(spot, size)], sin_ref[:, pl.ds(spot, size)]
        known = []
        for pair in range(first_pair, first_pair + pairs):
            first = pair * 2 * HD
            query, grad_out = two_heads(q_ref, first, spot, size), two_heads(go_ref, first, spot, size)
            mixed = two_heads(o_ref, first, spot, size)
            delta = jnp.sum(grad_out.astype(F32) * mixed, axis=0, keepdims=True)
            lse = jnp.concatenate(
                [lse_ref[2 * pair + part : 2 * pair + part + 1, pl.ds(spot, size)] for part in range(2)],
                axis=1,
            )
            known.append((query, grad_out, delta, lse))

        def chunk(number, state, diagonal):
            keys, values, turned_keys = kn_ref[number], vn_ref[number], kt_ref[number]
            allowed = admitted(koff_ref, number * span, qpos, qstart, diagonal)
            fresh = []
            grad_keys, grad_values = gk_ref[number], gv_ref[number]
            for (query, grad_out, delta, lse), grad_query in zip(known, state):
                scores = jnp.dot(keys, query, preferred_element_type=F32)
                probs = jnp.exp(jnp.where(allowed, scores - lse, masked))
                grad_probs = jnp.dot(values, grad_out, preferred_element_type=F32)
                grad_scores = (probs * (grad_probs - delta)).astype(BF16)
                grad_values = grad_values + lax.dot_general(
                    grad_out, probs.astype(BF16), last, preferred_element_type=F32
                )
                grad_keys = grad_keys + lax.dot_general(
                    query, grad_scores, last, preferred_element_type=F32
                )
                fresh.append(
                    grad_query + jnp.dot(turned_keys, grad_scores, preferred_element_type=F32)
                )
            gk_ref[number] = grad_keys
            gv_ref[number] = grad_values
            return tuple(fresh)

        state = chunk(block, (jnp.zeros((HD, 2 * size), F32),) * pairs, True)
        state = lax.fori_loop(0, block, lambda number, state: chunk(number, state, False), state)
        for head in range(2 * pairs):
            grad = state[head // 2][:, head % 2 * size : (head % 2 + 1) * size] * HD**-0.5
            half = HD // 2
            first, second = turn(grad[:half], grad[half:], cosine, -sine)
            gq_ref[head * HD : head * HD + half, pl.ds(spot, size)] = first.astype(BF16)
            gq_ref[head * HD + half : (head + 1) * HD, pl.ds(spot, size)] = second.astype(BF16)
        return carry

    lax.fori_loop(0, 4, one_block, 0)
    if last_call:
        for block in range(4):
            for m, ref in enumerate((g0, g1, g2, g3)):
                spot, out = slice(m * size, (m + 1) * size), slice(block * size, (block + 1) * size)
                ref[:HD, out] = gk_ref[block, :, spot].astype(BF16)
                ref[HD:, out] = gv_ref[block, :, spot].astype(BF16)


def project_back(
    gq0, gq1, g0, g1, g2, g3, cos_ref, sin_ref, mine_ref, theirs_ref, gqkv_ref, part_ref
):
    pair = g0[...].astype(F32) + g1[...].astype(F32) + (g2[...].astype(F32) + g3[...].astype(F32))
    half = HD // 2
    first, second = turn(pair[:half], pair[half:HD], cos_ref[...], -sin_ref[...])
    turned = jnp.concatenate(
        [gq0[...].astype(F32), gq1[...].astype(F32), first, second, pair[HD:]], axis=0
    )
    gqkv_ref[...] = turned.astype(BF16)
    natural = turned.T.astype(BF16)
    width = mine_ref.shape[1]
    slots = turned.shape[0]
    for core, weights in enumerate((mine_ref, theirs_ref)):
        for place in range(2):
            spot = (2 * core + place) * width
            part = lax.dot_general(
                natural, weights[place, :, :slots], (((1,), (1,)), ((), ())), preferred_element_type=F32
            )
            part_ref[:, spot : spot + width] = part.astype(BF16)


def feed(h_ref, gi_ref, own_ref, other_ref, inner_ref, pair_ref, part_ref, w_ref, sems):
    units = gi_ref.shape[1]
    depth = own_ref.shape[0]
    groups = feed_groups(units)
    copies = []
    for group, (begin, end) in enumerate(groups):
        mine = []
        for core, ref in enumerate((own_ref, other_ref)):
            for start in (0, units):
                columns = pl.ds(start + begin, end - begin)
                copy = pltpu.make_async_copy(
                    ref.at[:, columns],
                    w_ref.at[pl.ds(core * depth, depth), columns],
                    sems.at[group, len(mine)],
                )
                copy.start()
                mine.append(copy)
        copies.append(mine)
    for (begin, end), mine in zip(groups, copies):
        for copy in mine:
            copy.wait()
        gate = jnp.dot(h_ref[...], w_ref[:, begin:end], preferred_element_type=F32)
        up = jnp.dot(h_ref[...], w_ref[:, units + begin : units + end], preferred_element_type=F32)
        grad_inner = gi_ref[:, begin:end]
        sig = 1.0 / (1.0 + jnp.exp(-gate))
        act = gate * sig
        inner_ref[:, begin:end] = (act * up).astype(BF16)
        grad_gate = grad_inner * up * (sig * (1.0 + gate * (1.0 - sig)))
        pair_ref[:, begin:end] = grad_gate.astype(BF16)
        pair_ref[:, units + begin : units + end] = (grad_inner * act).astype(BF16)
    for begin in range(0, 2 * depth, 512):
        part = lax.dot_general(
            pair_ref[...], w_ref[begin : begin + 512, :], (((1,), (1,)), ((), ())),
            preferred_element_type=F32,
        )
        part_ref[:, begin : begin + 512] = part.astype(BF16)


def feed_groups(units):
    ends = [128, 384] + list(range(896, units, 512)) + [units]
    return list(zip([0] + ends[:-1], ends))


def spread_heads(row_ref, w_ref, b0, b1, b2, b3, out_ref):
    size = b0.shape[0]
    for j, part in enumerate((b0, b1, b2, b3)):
        spot = pl.multiple_of((row_ref[0] ^ j) * size, size)
        piece = lax.dot_general(
            w_ref[...], part[...], (((1,), (1,)), ((), ())), preferred_element_type=F32
        )
        out_ref[:, pl.ds(spot, size)] = piece.astype(BF16)


def kernel_call(body, out_shape, operands, flops, scratch=(), scalars=0, outside=()):
    moved = sum(x.size * x.dtype.itemsize for x in operands)
    spaces = [
        pltpu.SMEM if i < scalars else pl.ANY if i in outside else pltpu.VMEM
        for i in range(len(operands))
    ]
    return pl.pallas_call(
        body,
        out_shape=out_shape,
        in_specs=[pl.BlockSpec(memory_space=space) for space in spaces],
        out_specs=jax.tree.map(lambda _: pl.BlockSpec(memory_space=pltpu.VMEM), out_shape),
        scratch_shapes=list(scratch),
        compiler_params=pltpu.CompilerParams(vmem_limit_bytes=48 * 1024 * 1024),
        cost_estimate=pl.CostEstimate(flops=flops, bytes_accessed=moved, transcendentals=0),
    )(*operands)


def on_device(
    tokens_in, segment_ids, attn_gain, w_qkv, w_out, mlp_gain, w_gate, w_up, w_down, cotangent
):
    group = segment_ids.shape[0]
    span = group // 4
    size = span // 4
    units = w_gate.shape[1]
    slots = w_qkv.shape[2] // HD
    heads = slots - 2
    deep, high, row = lax.axis_index("z"), lax.axis_index("xh"), lax.axis_index("y")
    low, core = lax.axis_index("xl"), lax.axis_index("k")
    col = low * 2 + core

    indices = jnp.arange(group, dtype=jnp.int32)
    previous = jnp.concatenate([segment_ids[:1] - 1, segment_ids[:-1]])
    starts = lax.cummax(jnp.where(segment_ids != previous, indices, 0), axis=0)
    bases = [j * span + col * size for j in range(4)]
    my_starts = jnp.concatenate([lax.dynamic_slice_in_dim(starts, b, size, 0) for b in bases])
    lanes = jnp.arange(size, dtype=jnp.int32)
    my_index = jnp.concatenate([lanes + b for b in bases])
    half_dim = HD // 2
    inverse_freq = rope_base ** (-jnp.arange(half_dim, dtype=F32) * 2.0 / HD)
    angles = inverse_freq[:, None] * (my_index - my_starts).astype(F32)[None, :]
    cosine, sine = jnp.cos(angles), jnp.sin(angles)
    key_offset = jnp.concatenate([lanes + (col ^ m) * size for m in range(4)])
    key_offset = jnp.broadcast_to(key_offset[:, None], (span, size))
    qpos, qstart = my_index[None, :], my_starts[None, :]
    cut_at = slots * HD

    flat_qkv = w_qkv.reshape(w_qkv.shape[0], -1)
    qkv_out = jnp.concatenate([(flat_qkv * attn_gain[:, None]).astype(BF16), w_out], axis=1)
    (inputs, cot_rows), alongside = to_full_width(
        [tokens_in, cotangent], col, cosine, sine, key_offset, qpos, qstart, *cut(qkv_out, 2, 0)
    )
    cosine, sine, key_offset, qpos, qstart, qkv_out_first, qkv_out_second = alongside
    inputs = inputs.astype(F32)
    normed_one = (inputs * scale_of(inputs)).astype(BF16)
    rows_one = gather_row(normed_one)

    mine = ring_halves(qkv_out_first, qkv_out_second, low, 0).reshape(2, *qkv_out.shape)
    theirs = trade_core(mine)
    down_halves = [after(v, normed_one) for v in cut(w_down, 2, 0)]
    scaled = lambda v: (v * mlp_gain[:, None]).astype(BF16)
    gate_up = jnp.concatenate([scaled(w_gate), scaled(w_up)], axis=1)
    gu_halves = [after(v, mine) for v in cut(gate_up, 2, 0)]
    full_out = jnp.concatenate(
        [mine[0, :, cut_at:], mine[1, :, cut_at:], theirs[0, :, cut_at:], theirs[1, :, cut_at:]],
        axis=1,
    )
    rows_one, gu_halves, full_out = lax.optimization_barrier((rows_one, gu_halves, full_out))
    grad_rows = gather_row(after(cot_rows, rows_one))
    down_mine = ring_halves(*down_halves, low, 1, rows_one)
    gu_mine = ring_halves(*gu_halves, low, 0)

    shape = lambda kind, *dims: jax.ShapeDtypeStruct(dims, kind)
    scratch = lambda kind, *dims: pltpu.VMEM(dims, kind)
    width = inputs.shape[1]
    matmul = lambda rows, depth, columns: 2 * rows * depth * columns
    query, pairs = kernel_call(
        project,
        (shape(BF16, heads * HD, span), shape(BF16, 2 * HD, span)),
        (rows_one, mine, theirs, cosine, sine),
        matmul(span, width, cut_at),
    )
    all_pairs = [pairs] + [trade_col(pairs, m) for m in (1, 2, 3)]
    all_pairs = lax.optimization_barrier((all_pairs, down_mine))[0]
    down_theirs = trade_core(after(down_mine, all_pairs))

    flops = 2 * matmul(heads * span, HD, group)
    keys_shape = (4, HD, span), (4, span, HD)
    mixed, mixed_low, lse = kernel_call(
        attend,
        (shape(F32, heads * HD, span), shape(BF16, heads * HD, span), shape(F32, heads, span)),
        (query, *all_pairs, key_offset, qpos, qstart),
        flops,
        scratch=[scratch(BF16, *keys_shape[i]) for i in (0, 0, 1, 1)],
    )
    mixed_low = after(mixed_low, down_theirs)
    full_down = jnp.concatenate([down_mine, down_theirs], axis=1)
    branch = product(mixed_low, full_out, ((0,), (0,)), BF16)
    grad_inner = product(grad_rows, full_down, ((1,), (1,)))
    hidden, normed_two = kernel_call(
        add_and_norm,
        (shape(F32, *inputs.shape), shape(BF16, *inputs.shape)),
        (inputs, after(sum_row(branch), grad_inner, gu_mine)),
        0,
    )
    gu_theirs = trade_core(after(gu_mine, hidden))
    rows_two = gather_row(normed_two)

    side = lambda v, which: v[:, which * width // 2 : (which + 1) * width // 2]
    both_cores = lambda v, axis=0: jnp.concatenate([v, trade_core(v)], axis=axis)
    half_of = lambda v: jnp.concatenate([side(v, 0), trade_core(side(v, 1))])

    def half_by_ring(v):
        blocks = [cut(v, 8, 1)[i] for i in (0, 2, 1, 3, 4, 6, 5, 7)]
        sides = [jnp.concatenate(blocks[:4], axis=1), jnp.concatenate(blocks[4:], axis=1)]
        return jnp.concatenate([sides[0], trade_core(sides[1])])

    token_sum = lambda a, b: product(a, b, ((0,), (0,)), BF16)
    cot_half, heads_both = half_by_ring(after(grad_rows, hidden)), both_cores(after(mixed_low, hidden), 1)
    one_half = half_of(after(rows_one, hidden))
    rows_two, cot_half, heads_both, one_half = lax.optimization_barrier(
        (rows_two, cot_half, heads_both, one_half)
    )
    two_half = half_by_ring(rows_two)
    inner, grad_pair, part_two = kernel_call(
        feed,
        (shape(BF16, span, units), shape(BF16, span, 2 * units), shape(BF16, span, width)),
        (rows_two, grad_inner, gu_mine, gu_theirs),
        2 * matmul(span, width, 2 * units),
        scratch=(scratch(BF16, width, 2 * units), pltpu.SemaphoreType.DMA((len(feed_groups(units)), 4))),
        outside=(2, 3),
    )
    inner_both = both_cores(inner)
    pair_both = both_cores(grad_pair)
    mlp_sums = jnp.concatenate([token_sum(two_half, pair_both), token_sum(cot_half, inner_both)], axis=1)
    grad_n2, mlp_sums = lax.optimization_barrier((sum_row(part_two), mlp_sums))
    mlp_sums = lax.psum_scatter(mlp_sums, ("xh", "xl", "z"), scatter_dimension=0, tiled=True)
    grad_hidden, grad_low = kernel_call(
        norm_back_low,
        (shape(F32, *hidden.shape), shape(BF16, *hidden.shape)),
        (hidden, grad_n2, cot_rows),
        0,
    )
    branch_parts = spread_row(grad_low)
    result_parts = row_parts(product(inner, full_down, ((1,), (0,)), BF16), row)
    branch_parts, result_parts = lax.optimization_barrier((branch_parts, result_parts))
    grad_heads = kernel_call(
        spread_heads,
        shape(BF16, heads * HD, span),
        (row.astype(jnp.int32)[None], full_out, *branch_parts),
        matmul(span, width, heads * HD),
        scalars=1,
    )
    pair_shape = shape(BF16, 2 * HD, span)
    known = (query, *all_pairs, key_offset, qpos, qstart, mixed, lse, grad_heads, cosine, sine)
    half_heads = shape(BF16, heads * HD // 2, span)
    keys_scratch = [scratch(BF16, *keys_shape[i]) for i in (0, 1, 1)]
    key_sums = (shape(F32, *keys_shape[0]),) * 2
    split = functools.partial(attend_back, pairs=heads // 4)
    result_near = trade_near(result_parts, trade_row)
    gq_first, *key_grads = kernel_call(
        functools.partial(split, first_pair=0, last_call=False),
        (half_heads,) + key_sums,
        known,
        flops * 5 // 4,
        scratch=keys_scratch,
    )
    key_grads, result_near = lax.optimization_barrier((key_grads, result_near))
    result_far = trade_row(after(result_parts[2], result_near), 2)
    gq_last, *grad_pairs = kernel_call(
        functools.partial(split, first_pair=heads // 4, last_call=True),
        (half_heads,) + (pair_shape,) * 4,
        (*known, *key_grads),
        flops * 5 // 4,
        scratch=keys_scratch + [scratch(F32, *keys_shape[0])] * 2,
    )
    grad_pairs, result_far = lax.optimization_barrier((grad_pairs, result_far))
    grad_pairs = [grad_pairs[0]] + [trade_col(grad_pairs[m], m) for m in (1, 2, 3)]
    grad_qkv, part_one = kernel_call(
        project_back,
        (shape(BF16, cut_at, span), shape(BF16, span, width)),
        (gq_first, gq_last, *grad_pairs, cosine, sine, mine, theirs),
        matmul(span, width, cut_at),
    )
    one_parts = collect_row(row_parts(part_one, row))
    branch_rows = jnp.concatenate(in_order(after(branch_parts, grad_qkv), row))
    branch_half = half_of(branch_rows)
    qkv_both = both_cores(grad_qkv, 1)
    qkv_sum = product(one_half, qkv_both, ((0,), (1,)), BF16).reshape(2, width // 4, -1)
    qkv_parts, mlp_sums = after((ring_parts([qkv_sum], low, high), mlp_sums), one_parts[1])
    qkv_near = trade_near(qkv_parts, trade_ring)
    mlp_total = lax.all_gather(mlp_sums, ("xh", "z"), axis=0, tiled=True).astype(F32)
    one_parts, qkv_near, branch_half = lax.optimization_barrier((one_parts, qkv_near, branch_half))

    grad_in = kernel_call(
        norm_back_sum, shape(F32, *inputs.shape), (inputs, *one_parts, grad_hidden), 0
    )
    out_sum = product(branch_half, heads_both, ((0,), (1,)), BF16).reshape(2, width // 4, -1)
    qkv_far = trade_ring(after(qkv_parts[2], qkv_near), 2)
    grad_in, qkv_far, out_sum = lax.optimization_barrier((to_blocks(grad_in, col), qkv_far, out_sum))
    qkv_total = add_low(qkv_parts[0], *qkv_near, qkv_far)
    out_parts = ring_parts([out_sum], low, high)
    out_near = trade_near(out_parts, trade_ring)
    qkv_total = exchange([qkv_total] * 4, trade_deep)
    qkv_total, out_near = lax.optimization_barrier((qkv_total, out_near))
    out_far = trade_ring(after(out_parts[2], out_near), 2)
    qkv_total = ring_gather(qkv_total, high).astype(F32)
    result = (hidden + result_parts[0].astype(F32)) + result_far.astype(F32)
    result = result + sum(part.astype(F32) for part in result_near)
    result = to_blocks(after(result.astype(BF16), grad_in), col)
    out_far, qkv_total, result = lax.optimization_barrier((out_far, qkv_total, result))
    out_total = exchange([add_low(out_parts[0], *out_near, out_far)] * 4, trade_deep)
    out_total = ring_gather(out_total, high).astype(F32)
    gu_total, down_total = mlp_total[:, : 2 * units], mlp_total[:, 2 * units :]

    gate_total, up_total = gu_total[:, :units], gu_total[:, units:]
    gain_sums = jnp.stack(
        [
            jnp.sum(flat_qkv * qkv_total, axis=1),
            jnp.sum(w_gate * gate_total + w_up * up_total, axis=1),
        ]
    )
    gain_sums = sum([trade_row(gain_sums, j) for j in (1, 2, 3)], gain_sums)
    return (
        result,
        grad_in,
        gain_sums[0],
        (qkv_total * attn_gain[:, None]).reshape(w_qkv.shape),
        out_total.T,
        gain_sums[1],
        gate_total * mlp_gain[:, None],
        up_total * mlp_gain[:, None],
        down_total.T,
    )


def solution(mesh):
    dp, rows, cols = mesh.devices.shape
    fine = Mesh(
        mesh.devices.reshape(dp // 2, 2, rows, cols // 2, 2), ("z", "xh", "y", "xl", "k")
    )
    tokens = P(("z", "xh", "y"), COL)
    in_specs = (
        tokens, P(("z", "xh")), P(COL), P(COL, "y", None), P("y", COL), P(COL),
        P(COL, "y"), P(COL, "y"), P("y", COL), tokens,
    )
    out_specs = (
        tokens, tokens, P(COL), P(COL, "y", None), P("y", COL), P(COL),
        P(COL, "y"), P(COL, "y"), P("y", COL),
    )
    return jax.shard_map(
        on_device, mesh=fine, in_specs=in_specs, out_specs=out_specs, check_vma=False
    )
```

```python
import functools

import jax
import jax.numpy as jnp
from jax import lax
from jax.experimental import pallas as pl
from jax.experimental.pallas import tpu as pltpu
from jax.sharding import Mesh
from jax.sharding import PartitionSpec as P

HD = 64
norm_eps = 1e-05
rope_base = 10000.0
masked = -1e30

COL = ("xl", "k")
RING = ("xh", "xl")
BF16 = jnp.bfloat16
F32 = jnp.float32


def trade(values, axes, mask, size=4):
    return lax.ppermute(values, axes, [(i, i ^ mask) for i in range(size)])


def trade_row(values, mask):
    return trade(values, "y", mask)


def trade_col(values, mask):
    return trade(values, COL, mask)


def trade_core(values):
    return trade(values, "k", 1, 2)


def trade_ring(values, mask):
    return trade(values, RING, mask)


def trade_deep(values, mask):
    return trade(values, "z", mask)


def after(values, *earlier):
    return lax.optimization_barrier((values, earlier))[0]


def pick(bit, zero, one):
    return jnp.where(bit == 0, zero, one)


def in_order(parts, index):
    low, high = index % 2, index // 2
    a, b, c, d = parts
    a, b = pick(low, a, b), pick(low, b, a)
    c, d = pick(low, c, d), pick(low, d, c)
    return [pick(high, a, c), pick(high, b, d), pick(high, c, a), pick(high, d, b)]


def cut(values, count, axis):
    return jnp.split(values, count, axis)


def gather_row(values):
    return lax.all_gather(values, "y", axis=0, tiled=True)


def sum_row(partial):
    return lax.psum_scatter(partial, "y", scatter_dimension=0, tiled=True)


def spread_row(values):
    return [values] + [trade_row(values, j) for j in (1, 2, 3)]


def row_parts(partial, row):
    size = partial.shape[0] // 4
    return [lax.dynamic_slice_in_dim(partial, (row ^ j) * size, size, 0) for j in range(4)]


def collect_row(parts):
    return [parts[0]] + [trade_row(parts[j], j) for j in (1, 2, 3)]


def by_width(parts, low):
    return [
        pick(low, parts[core + 2 * place], parts[core + 2 * (1 - place)])
        for core in range(2)
        for place in range(2)
    ]


def of_width(values, low):
    blocks = cut(values, 4, 1)
    return [
        pick(low, blocks[2 * core + place], blocks[2 * core + 1 - place])
        for place in range(2)
        for core in range(2)
    ]


def to_full_width(values, col, *alongside):
    size = values[0].shape[0] // 4
    send = lambda m: jnp.concatenate(
        [lax.dynamic_slice_in_dim(v, (col ^ m) * size, size, 0) for v in values], axis=1
    )
    parts = [send(0)] + [trade_col(send(m), m) for m in (1, 2, 3)]
    parts, alongside = lax.optimization_barrier((parts, alongside))
    parts = [cut(part, len(values), 1) for part in parts]
    rows = [
        jnp.concatenate(by_width([part[i] for part in parts], col // 2), axis=1)
        for i in range(len(values))
    ]
    return rows, alongside


def to_blocks(values, col):
    parts = of_width(values, col // 2)
    kind = values.dtype
    parts = [parts[0]] + [trade_col(parts[m].astype(BF16), m).astype(kind) for m in (1, 2, 3)]
    return jnp.concatenate(in_order(parts, col), axis=0)


def ring_send(halves):
    return [trade_ring(halves[0], 1), trade_ring(halves[1], 3)]


def ring_join(halves, got, low, axis):
    shard, other = jnp.concatenate(halves), jnp.concatenate(got)
    return jnp.concatenate([pick(low, shard, other), pick(low, other, shard)], axis=axis)


def add_low(*terms):
    total = terms[0].astype(F32)
    for term in terms[1:]:
        total = total + term.astype(F32)
    return total.astype(BF16)


def at(values, index):
    return lax.dynamic_index_in_dim(values, index, 0, keepdims=False)


def ring_parts(blocks, low, high):
    half = blocks[0].shape[1] // 2
    take = lambda place, which: jnp.concatenate(
        [
            lax.dynamic_slice(v, (place, which * half, 0), (1, half, v.shape[2]))[0]
            for v in blocks
        ],
        axis=1,
    )
    return [take(low, high), take(1 - low, high), take(low, 1 - high), take(1 - low, 1 - high)]


def deep_parts(blocks, deep):
    size = blocks.shape[-2] // 4
    return [
        lax.dynamic_slice_in_dim(blocks, (deep ^ j) * size, size, blocks.ndim - 2) for j in range(4)
    ]


def trade_near(parts, trader):
    return [trader(parts[1], 1), trader(parts[3], 3)]


def exchange(parts, trader):
    return add_low(parts[0], *lax.optimization_barrier([trader(parts[j], j) for j in (1, 2, 3)]))


def ring_gather(values, high):
    other = trade_ring(values, 2)
    return jnp.concatenate([pick(high, values, other), pick(high, other, values)], axis=0)


def deep_gather(values, deep):
    parts = lax.optimization_barrier([values] + [trade_deep(values, j) for j in (1, 2, 3)])
    return jnp.concatenate(in_order(parts, deep), axis=0)


def product(left, right, dims, kind=F32):
    return lax.dot_general(left, right, (dims, ((), ())), preferred_element_type=F32).astype(kind)


def scale_of(values):
    return lax.rsqrt(jnp.mean(values * values, axis=1, keepdims=True) + norm_eps)


def add_and_norm(base_ref, p0, p1, p2, p3, hidden_ref, normed_ref):
    hidden = (p0[...].astype(F32) + p1[...].astype(F32)) + (p2[...].astype(F32) + p3[...].astype(F32))
    hidden = base_ref[...] + hidden
    hidden_ref[...] = hidden
    normed_ref[...] = (hidden * scale_of(hidden)).astype(BF16)


def norm_back(values, weighted, passed):
    scale = scale_of(values)
    inner = jnp.mean(weighted * values, axis=1, keepdims=True)
    return passed + (scale * weighted - values * (scale**3 * inner))


def norm_back_low(values_ref, part_ref, passed_ref, grad_ref, low_ref):
    grad = norm_back(values_ref[...], part_ref[...].astype(F32), passed_ref[...].astype(F32))
    grad_ref[...] = grad
    low_ref[...] = grad.astype(BF16)


def norm_back_high(values_ref, part_ref, passed_ref, grad_ref):
    grad_ref[...] = norm_back(values_ref[...], part_ref[...].astype(F32), passed_ref[...])


def turn(first, second, cosine, sine):
    return first * cosine - second * sine, second * cosine + first * sine


def project(x_ref, mine_ref, theirs_ref, cos_ref, sin_ref, q_ref, kv_ref):
    width = mine_ref.shape[1]
    slots = kv_ref.shape[0] + q_ref.shape[0]
    total = None
    for core, weights in enumerate((mine_ref, theirs_ref)):
        for place in range(2):
            spot = (2 * core + place) * width
            term = jnp.dot(
                x_ref[:, spot : spot + width], weights[place, :, :slots], preferred_element_type=F32
            )
            total = term if total is None else total + term
    turned = total.T
    cosine, sine = cos_ref[...], sin_ref[...]
    half = HD // 2
    heads = q_ref.shape[0] // HD
    for head in range(heads + 1):
        spot = head * HD
        first, second = turn(
            turned[spot : spot + half], turned[spot + half : spot + HD], cosine, sine
        )
        if head < heads:
            q_ref[spot : spot + half, :] = (first * HD**-0.5).astype(BF16)
            q_ref[spot + half : spot + HD, :] = (second * HD**-0.5).astype(BF16)
        else:
            kv_ref[:half, :] = first.astype(BF16)
            kv_ref[half:HD, :] = second.astype(BF16)
    kv_ref[HD:, :] = turned[(heads + 1) * HD :].astype(BF16)


def lay_keys(pairs, kt_ref, vt_ref, kn_ref, vn_ref):
    size = pairs.shape[2] // 4
    for block in range(4):
        for m in range(4):
            piece = pairs[m, :, block * size : (block + 1) * size]
            spot = slice(m * size, (m + 1) * size)
            kt_ref[block, :, spot] = piece[:HD]
            if vt_ref is not None:
                vt_ref[block, :, spot] = piece[HD:]
            natural = piece.astype(F32).T.astype(BF16)
            kn_ref[block, spot, :] = natural[:, :HD]
            vn_ref[block, spot, :] = natural[:, HD:]


def side_by_side(ref, first, count, depth, spot, size):
    return jnp.concatenate(
        [ref[head * depth : (head + 1) * depth, spot : spot + size] for head in range(first, first + count)],
        axis=1,
    )


def admitted(koff_ref, start, qpos, qstart, diagonal, count):
    keys = koff_ref[...] + start
    allowed = keys >= qstart
    if diagonal:
        allowed = allowed & (keys <= qpos)
    return jnp.concatenate([allowed] * count, axis=1)


def attend(
    q_ref, pairs_ref, koff_ref, qpos_ref, qstart_ref, o_ref, low_ref, lse_ref, kt_ref, vt_ref, kn_ref, vn_ref
):
    span = kn_ref.shape[1]
    size = span // 4
    heads = q_ref.shape[0] // HD
    lay_keys(pairs_ref, kt_ref, vt_ref, kn_ref, vn_ref)
    for block in range(4):
        spot = block * size
        qpos, qstart = qpos_ref[:, spot : spot + size], qstart_ref[:, spot : spot + size]
        query = side_by_side(q_ref, 0, heads, HD, spot, size)
        top = jnp.full((1, heads * size), masked, F32)
        total = jnp.zeros((1, heads * size), F32)
        accum = jnp.zeros((HD, heads * size), F32)
        for number in (block, *range(block)):
            scores = jnp.dot(kn_ref[number], query, preferred_element_type=F32)
            allowed = admitted(koff_ref, number * span, qpos, qstart, number == block, heads)
            scores = jnp.where(allowed, scores, masked)
            new_top = jnp.maximum(top, jnp.max(scores, axis=0, keepdims=True))
            weights = jnp.exp(scores - new_top)
            shrink = jnp.exp(top - new_top)
            total = total * shrink + jnp.sum(weights, axis=0, keepdims=True)
            accum = accum * shrink + jnp.dot(
                vt_ref[number], weights.astype(BF16), preferred_element_type=F32
            )
            top = new_top
        result = accum / total
        lse = top + jnp.log(total)
        for head in range(heads):
            piece = result[:, head * size : (head + 1) * size]
            rows = slice(head * HD, (head + 1) * HD)
            o_ref[rows, spot : spot + size] = piece
            low_ref[rows, spot : spot + size] = piece.astype(BF16)
            lse_ref[head : head + 1, spot : spot + size] = lse[:, head * size : (head + 1) * size]


def attend_back(
    q_ref, pairs_ref, koff_ref, qpos_ref, qstart_ref, o_ref, lse_ref, go_ref, cos_ref, sin_ref, *refs,
    first, count, last_call,
):
    if last_call:
        gk_in, gv_in, gq_ref, g0, g1, g2, g3, kt_ref, kn_ref, vn_ref, gk_ref, gv_ref = refs
    else:
        gq_ref, gk_ref, gv_ref, kt_ref, kn_ref, vn_ref = refs
    span = kn_ref.shape[1]
    size = span // 4
    lay_keys(pairs_ref, kt_ref, None, kn_ref, vn_ref)
    gk_ref[...] = gk_in[...] if last_call else jnp.zeros_like(gk_ref)
    gv_ref[...] = gv_in[...] if last_call else jnp.zeros_like(gv_ref)
    last = (((1,), (1,)), ((), ()))
    for block in range(4):
        spot = block * size
        here = slice(spot, spot + size)
        qpos, qstart = qpos_ref[:, here], qstart_ref[:, here]
        cosine, sine = cos_ref[:, here], sin_ref[:, here]
        pick_heads = lambda ref, depth: side_by_side(ref, first, count, depth, spot, size)
        query, grad_out = pick_heads(q_ref, HD), pick_heads(go_ref, HD)
        lse = pick_heads(lse_ref, 1)
        delta = jnp.sum(grad_out.astype(F32) * pick_heads(o_ref, HD), axis=0, keepdims=True)
        grad_query = jnp.zeros((HD, count * size), F32)
        for number in (block, *range(block)):
            scores = jnp.dot(kn_ref[number], query, preferred_element_type=F32)
            allowed = admitted(koff_ref, number * span, qpos, qstart, number == block, count)
            probs = jnp.exp(jnp.where(allowed, scores - lse, masked))
            grad_probs = jnp.dot(vn_ref[number], grad_out, preferred_element_type=F32)
            grad_scores = (probs * (grad_probs - delta)).astype(BF16)
            gv_ref[number] += lax.dot_general(
                grad_out, probs.astype(BF16), last, preferred_element_type=F32
            )
            gk_ref[number] += lax.dot_general(query, grad_scores, last, preferred_element_type=F32)
            grad_query = grad_query + jnp.dot(
                kt_ref[number], grad_scores, preferred_element_type=F32
            )
        half = HD // 2
        for head in range(count):
            grad = grad_query[:, head * size : (head + 1) * size] * HD**-0.5
            upper, lower = turn(grad[:half], grad[half:], cosine, -sine)
            gq_ref[head * HD : head * HD + half, here] = upper.astype(BF16)
            gq_ref[head * HD + half : (head + 1) * HD, here] = lower.astype(BF16)
    if last_call:
        for block in range(4):
            for m, ref in enumerate((g0, g1, g2, g3)):
                spot, out = slice(m * size, (m + 1) * size), slice(block * size, (block + 1) * size)
                ref[:HD, out] = gk_ref[block, :, spot].astype(BF16)
                ref[HD:, out] = gv_ref[block, :, spot].astype(BF16)


def project_back(
    gq0, gq1, g0, g1, g2, g3, cos_ref, sin_ref, mine_ref, theirs_ref, gqkv_ref, part_ref
):
    pair = g0[...].astype(F32) + g1[...].astype(F32) + (g2[...].astype(F32) + g3[...].astype(F32))
    half = HD // 2
    first, second = turn(pair[:half], pair[half:HD], cos_ref[...], -sin_ref[...])
    turned = jnp.concatenate(
        [gq0[...].astype(F32), gq1[...].astype(F32), first, second, pair[HD:]], axis=0
    )
    gqkv_ref[...] = turned.astype(BF16)
    natural = turned.T.astype(BF16)
    width = mine_ref.shape[1]
    slots = turned.shape[0]
    for core, weights in enumerate((mine_ref, theirs_ref)):
        for place in range(2):
            spot = (2 * core + place) * width
            part = lax.dot_general(
                natural, weights[place, :, :slots], (((1,), (1,)), ((), ())), preferred_element_type=F32
            )
            part_ref[:, spot : spot + width] = part.astype(BF16)


def feed(h_ref, gi_ref, own_ref, other_ref, inner_ref, pair_ref, part_ref, w_ref, sems):
    units = gi_ref.shape[1]
    depth = own_ref.shape[0]
    groups = feed_groups(units)
    copies = []
    for group, (begin, end) in enumerate(groups):
        mine = []
        for core, ref in enumerate((own_ref, other_ref)):
            for start in (0, units):
                columns = pl.ds(start + begin, end - begin)
                copy = pltpu.make_async_copy(
                    ref.at[:, columns],
                    w_ref.at[pl.ds(core * depth, depth), columns],
                    sems.at[group, len(mine)],
                )
                copy.start()
                mine.append(copy)
        copies.append(mine)
    for (begin, end), mine in zip(groups, copies):
        for copy in mine:
            copy.wait()
        gate = jnp.dot(h_ref[...], w_ref[:, begin:end], preferred_element_type=F32)
        up = jnp.dot(h_ref[...], w_ref[:, units + begin : units + end], preferred_element_type=F32)
        grad_inner = gi_ref[:, begin:end]
        sig = 1.0 / (1.0 + jnp.exp(-gate))
        act = gate * sig
        inner_ref[:, begin:end] = (act * up).astype(BF16)
        grad_gate = grad_inner * up * (sig * (1.0 + gate * (1.0 - sig)))
        pair_ref[:, begin:end] = grad_gate.astype(BF16)
        pair_ref[:, units + begin : units + end] = (grad_inner * act).astype(BF16)
    for begin in range(0, 2 * depth, 512):
        part = lax.dot_general(
            pair_ref[...], w_ref[begin : begin + 512, :], (((1,), (1,)), ((), ())),
            preferred_element_type=F32,
        )
        part_ref[:, begin : begin + 512] = part.astype(BF16)


def feed_groups(units):
    ends = [128, 384] + list(range(896, units, 512)) + [units]
    return list(zip([0] + ends[:-1], ends))


def spread_heads(row_ref, w_ref, b0, b1, b2, b3, out_ref):
    size = b0.shape[0]
    for j, part in enumerate((b0, b1, b2, b3)):
        spot = pl.multiple_of((row_ref[0] ^ j) * size, size)
        piece = lax.dot_general(
            w_ref[...], part[...], (((1,), (1,)), ((), ())), preferred_element_type=F32
        )
        out_ref[:, pl.ds(spot, size)] = piece.astype(BF16)


def kernel_call(body, out_shape, operands, flops, scratch=(), scalars=0, outside=(), staged=(), mib=48):
    moved = sum(x.size * x.dtype.itemsize for x in operands)
    count = len(operands)
    spaces = [
        pltpu.SMEM if i < scalars else pl.ANY if i in outside or i in staged else pltpu.VMEM
        for i in range(count)
    ]
    if staged:
        held = [pltpu.VMEM(operands[i].shape, operands[i].dtype) for i in staged]
        scratch = [*scratch, *held, pltpu.SemaphoreType.DMA((len(staged),))]

        def whole(*refs):
            refs, buffers, sems = list(refs[: -len(staged) - 1]), refs[-len(staged) - 1 : -1], refs[-1]
            copies = [
                pltpu.make_async_copy(refs[i], buffer, sems.at[n])
                for n, (i, buffer) in enumerate(zip(staged, buffers))
            ]
            for copy in copies:
                copy.start()
            for copy in copies:
                copy.wait()
            for i, buffer in zip(staged, buffers):
                refs[i] = buffer
            body(*refs)
    else:
        whole = body
    out_specs = jax.tree.map(lambda _: pl.BlockSpec(memory_space=pltpu.VMEM), out_shape)
    return pl.pallas_call(
        whole,
        out_shape=out_shape,
        in_specs=[pl.BlockSpec(memory_space=space) for space in spaces],
        out_specs=out_specs,
        scratch_shapes=list(scratch),
        compiler_params=pltpu.CompilerParams(vmem_limit_bytes=mib * 1024 * 1024),
        cost_estimate=pl.CostEstimate(flops=flops, bytes_accessed=moved, transcendentals=0),
    )(*operands)


def rows_call(body, kinds, operands, steps=2):
    rows, width = operands[0].shape
    block = pl.BlockSpec((rows // steps, width), lambda i: (i, 0))
    out_shape = tuple(jax.ShapeDtypeStruct((rows, width), kind) for kind in kinds)
    moved = sum(x.size * x.dtype.itemsize for x in operands)
    return pl.pallas_call(
        body,
        out_shape=out_shape,
        grid=(steps,),
        in_specs=[block] * len(operands),
        out_specs=(block,) * len(kinds),
        cost_estimate=pl.CostEstimate(flops=0, bytes_accessed=moved, transcendentals=0),
    )(*operands)


def on_device(
    tokens_in, segment_ids, attn_gain, w_qkv, w_out, mlp_gain, w_gate, w_up, w_down, cotangent
):
    group = segment_ids.shape[0]
    span = group // 4
    size = span // 4
    units = w_gate.shape[1]
    slots = w_qkv.shape[2] // HD
    heads = slots - 2
    deep, high, row = lax.axis_index("z"), lax.axis_index("xh"), lax.axis_index("y")
    low, core = lax.axis_index("xl"), lax.axis_index("k")
    col = low * 2 + core

    indices = jnp.arange(group, dtype=jnp.int32)
    previous = jnp.concatenate([segment_ids[:1] - 1, segment_ids[:-1]])
    starts = lax.cummax(jnp.where(segment_ids != previous, indices, 0), axis=0)
    bases = [j * span + col * size for j in range(4)]
    my_starts = jnp.concatenate([lax.dynamic_slice_in_dim(starts, b, size, 0) for b in bases])
    lanes = jnp.arange(size, dtype=jnp.int32)
    my_index = jnp.concatenate([lanes + b for b in bases])
    half_dim = HD // 2
    inverse_freq = rope_base ** (-jnp.arange(half_dim, dtype=F32) * 2.0 / HD)
    angles = inverse_freq[:, None] * (my_index - my_starts).astype(F32)[None, :]
    cosine, sine = jnp.cos(angles), jnp.sin(angles)
    key_offset = jnp.concatenate([lanes + (col ^ m) * size for m in range(4)])
    key_offset = jnp.broadcast_to(key_offset[:, None], (span, size))
    qpos, qstart = my_index[None, :], my_starts[None, :]
    cut_at = slots * HD

    flat_qkv = w_qkv.reshape(w_qkv.shape[0], -1)
    qkv_out = jnp.concatenate([(flat_qkv * attn_gain[:, None]).astype(BF16), w_out], axis=1)
    (inputs,), alongside = to_full_width(
        [tokens_in], col, cosine, sine, key_offset, qpos, qstart, *cut(qkv_out, 2, 0)
    )
    cosine, sine, key_offset, qpos, qstart, qkv_out_first, qkv_out_second = alongside
    inputs = inputs.astype(F32)
    normed_one = (inputs * scale_of(inputs)).astype(BF16)
    rows_one = gather_row(normed_one)

    qkv_out_halves = [qkv_out_first, qkv_out_second]
    mine = ring_join(qkv_out_halves, lax.optimization_barrier(ring_send(qkv_out_halves)), low, 0)
    mine = mine.reshape(2, *qkv_out.shape)
    theirs = trade_core(mine)
    (cot_rows,), _ = to_full_width([after(cotangent, mine)], col)
    scaled = lambda v: (v * mlp_gain[:, None]).astype(BF16)
    gate_up = jnp.concatenate([scaled(w_gate), scaled(w_up)], axis=1)
    gu_halves = [after(v, normed_one) for v in cut(gate_up, 2, 0)]
    full_out = jnp.concatenate(
        [mine[0, :, cut_at:], mine[1, :, cut_at:], theirs[0, :, cut_at:], theirs[1, :, cut_at:]],
        axis=1,
    )
    rows_one, gu_halves, full_out, cot_rows = lax.optimization_barrier(
        (rows_one, gu_halves, full_out, cot_rows)
    )
    gu_got = ring_send(gu_halves)

    shape = lambda kind, *dims: jax.ShapeDtypeStruct(dims, kind)
    scratch = lambda kind, *dims: pltpu.VMEM(dims, kind)
    width = inputs.shape[1]
    matmul = lambda rows, depth, columns: 2 * rows * depth * columns
    query, pairs = kernel_call(
        project,
        (shape(BF16, heads * HD, span), shape(BF16, 2 * HD, span)),
        (rows_one, mine, theirs, cosine, sine),
        matmul(span, width, cut_at),
        staged=(0,),
    )
    grad_rows = gather_row(after(cot_rows, query))
    all_pairs = jnp.stack([pairs] + [trade_col(pairs, m) for m in (1, 2, 3)])

    flops = 2 * matmul(heads * span, HD, group)
    keys_shape = (4, HD, span), (4, span, HD)
    mixed, mixed_low, lse = kernel_call(
        attend,
        (shape(F32, heads * HD, span), shape(BF16, heads * HD, span), shape(F32, heads, span)),
        (query, all_pairs, key_offset, qpos, qstart),
        flops,
        scratch=[scratch(BF16, *keys_shape[i]) for i in (0, 0, 1, 1)],
    )
    branch = product(mixed_low, full_out, ((0,), (0,)), BF16)
    gu_mine = ring_join(gu_halves, after(gu_got, branch), low, 0)
    down_halves = [after(v, branch, gu_got) for v in cut(w_down, 2, 0)]
    down_got = ring_send(down_halves)
    branch_parts = after(collect_row(row_parts(branch, row)), gu_mine, down_got)
    hidden, normed_two = rows_call(add_and_norm, (F32, BF16), (inputs, *branch_parts))
    down_mine = ring_join(down_halves, after(down_got, hidden), low, 1)
    full_down = jnp.concatenate([down_mine, trade_core(down_mine)], axis=1)
    grad_inner = product(grad_rows, full_down, ((1,), (1,)))
    gu_theirs = trade_core(after(gu_mine, hidden))
    rows_two = gather_row(normed_two)

    side = lambda v, which: v[:, which * width // 2 : (which + 1) * width // 2]
    both_cores = lambda v, axis=0: jnp.concatenate([v, trade_core(v)], axis=axis)
    half_of = lambda v: jnp.concatenate([side(v, 0), trade_core(side(v, 1))])

    def half_by_ring(v):
        blocks = [cut(v, 8, 1)[i] for i in (0, 2, 1, 3, 4, 6, 5, 7)]
        sides = [jnp.concatenate(blocks[:4], axis=1), jnp.concatenate(blocks[4:], axis=1)]
        return jnp.concatenate([sides[0], trade_core(sides[1])])

    token_sum = lambda a, b: product(a, b, ((0,), (0,)), BF16)
    cot_half, heads_both = half_by_ring(after(grad_rows, hidden)), both_cores(after(mixed_low, hidden), 1)
    one_half = half_of(after(rows_one, hidden))
    rows_two, cot_half, heads_both, one_half = lax.optimization_barrier(
        (rows_two, cot_half, heads_both, one_half)
    )
    two_half = half_by_ring(rows_two)
    inner, grad_pair, part_two = kernel_call(
        feed,
        (shape(BF16, span, units), shape(BF16, span, 2 * units), shape(BF16, span, width)),
        (rows_two, grad_inner, gu_mine, gu_theirs),
        2 * matmul(span, width, 2 * units),
        scratch=(scratch(BF16, width, 2 * units), pltpu.SemaphoreType.DMA((len(feed_groups(units)), 4))),
        outside=(2, 3),
    )
    inner_both = both_cores(inner)
    pair_both = both_cores(grad_pair)
    mlp_sums = jnp.concatenate([token_sum(two_half, pair_both), token_sum(cot_half, inner_both)], axis=1)
    grad_n2, mlp_sums = lax.optimization_barrier((sum_row(part_two), mlp_sums))
    mlp_sums = lax.psum_scatter(mlp_sums, ("xh", "xl", "z"), scatter_dimension=0, tiled=True)
    grad_hidden, grad_low = rows_call(norm_back_low, (F32, BF16), (hidden, grad_n2, cot_rows))
    branch_parts = spread_row(grad_low)
    result_parts = row_parts(product(inner, full_down, ((1,), (0,)), BF16), row)
    branch_parts, result_parts = lax.optimization_barrier((branch_parts, result_parts))
    grad_heads = kernel_call(
        spread_heads,
        shape(BF16, heads * HD, span),
        (row.astype(jnp.int32)[None], full_out, *branch_parts),
        matmul(span, width, heads * HD),
        scalars=1,
    )
    pair_shape = shape(BF16, 2 * HD, span)
    known = (query, all_pairs, key_offset, qpos, qstart, mixed, lse, grad_heads, cosine, sine)
    half_heads = shape(BF16, heads * HD // 2, span)
    keys_scratch = [scratch(BF16, *keys_shape[i]) for i in (0, 1, 1)]
    key_sums = (shape(F32, *keys_shape[0]),) * 2
    split = functools.partial(attend_back, count=heads // 2)
    result_near = trade_near(result_parts, trade_row)
    gq_first, *key_grads = kernel_call(
        functools.partial(split, first=0, last_call=False),
        (half_heads,) + key_sums,
        known,
        flops * 5 // 4,
        scratch=keys_scratch,
        staged=(1,),
    )
    key_grads, result_near = lax.optimization_barrier((key_grads, result_near))
    result_far = trade_row(after(result_parts[2], result_near), 2)
    gq_last, *grad_pairs = kernel_call(
        functools.partial(split, first=heads // 2, last_call=True),
        (half_heads,) + (pair_shape,) * 4,
        (*known, *key_grads),
        flops * 5 // 4,
        scratch=keys_scratch + [scratch(F32, *keys_shape[0])] * 2,
        staged=(1,),
    )
    grad_pairs = [grad_pairs[0]] + [trade_col(grad_pairs[m], m) for m in (1, 2, 3)]
    grad_pairs = lax.optimization_barrier(grad_pairs)
    grad_qkv, part_one = kernel_call(
        project_back,
        (shape(BF16, cut_at, span), shape(BF16, span, width)),
        (gq_first, gq_last, *grad_pairs, cosine, sine, mine, theirs),
        matmul(span, width, cut_at),
    )
    qkv_both = both_cores(grad_qkv, 1)
    branch_rows = jnp.concatenate(in_order(after(branch_parts, grad_qkv), row))
    branch_half = half_of(branch_rows)
    qkv_sum = product(one_half, qkv_both, ((0,), (1,)), BF16).reshape(2, width // 4, -1)
    out_sum = product(branch_half, heads_both, ((0,), (1,)), BF16).reshape(2, width // 4, -1)
    both_parts = deep_parts(jnp.concatenate([qkv_sum, out_sum], axis=2), deep)
    both_parts, mlp_sums = lax.optimization_barrier((both_parts, mlp_sums))
    both_sums = exchange(both_parts, trade_deep)
    rows_here = mlp_sums.shape[0]
    grad_n1 = sum_row(part_one)
    (grad_in,) = rows_call(norm_back_high, (F32,), (inputs, grad_n1, grad_hidden))
    both_sums, grad_in, result_far = lax.optimization_barrier((both_sums, to_blocks(grad_in, col), result_far))
    both_total = exchange(ring_parts([both_sums], low, high), trade_ring)
    own_rows = lambda w: lax.dynamic_slice_in_dim(w, (high * 4 + deep) * rows_here, rows_here, 0)
    own_gain = jnp.sum(own_rows(w_gate) * mlp_sums[:, :units].astype(F32), axis=1, keepdims=True)
    own_gain += jnp.sum(own_rows(w_up) * mlp_sums[:, units : 2 * units].astype(F32), axis=1, keepdims=True)
    own_gain = jnp.broadcast_to(own_gain, (rows_here, 128))
    own_gain = sum([trade_row(own_gain, j) for j in (1, 2, 3)], own_gain).astype(BF16)
    mlp_total = ring_gather(jnp.concatenate([mlp_sums, own_gain], axis=1), high)
    mlp_total = lax.all_gather(mlp_total, "z", axis=0, tiled=True)
    both_total = ring_gather(both_total, high)
    both_total = deep_gather(both_total, deep).astype(F32)
    result = (hidden + result_parts[0].astype(F32)) + result_far.astype(F32)
    result = (result + sum(part.astype(F32) for part in result_near)).astype(BF16)
    result = to_blocks(after(result, grad_in), col)
    both_total, result = lax.optimization_barrier((both_total, result))
    qkv_total, out_total = both_total[:, :cut_at], both_total[:, cut_at:]
    qkv_gain = jnp.sum(flat_qkv * qkv_total, axis=1)[None]
    qkv_gain = sum([trade_row(qkv_gain, j) for j in (1, 2, 3)], qkv_gain)[0]
    mlp_total, qkv_gain = lax.optimization_barrier((mlp_total, qkv_gain))
    mlp_total = mlp_total.reshape(4, 2, rows_here, -1).swapaxes(0, 1).reshape(mlp_total.shape)
    piece = lambda first: mlp_total[:, first : first + units].astype(F32)
    return (
        result,
        grad_in,
        qkv_gain,
        (qkv_total * attn_gain[:, None]).reshape(w_qkv.shape),
        out_total.T,
        mlp_total[:, 3 * units].astype(F32),
        piece(0) * mlp_gain[:, None],
        piece(units) * mlp_gain[:, None],
        piece(2 * units).T,
    )


def solution(mesh):
    dp, rows, cols = mesh.devices.shape
    fine = Mesh(
        mesh.devices.reshape(dp // 2, 2, rows, cols // 2, 2), ("z", "xh", "y", "xl", "k")
    )
    tokens = P(("z", "xh", "y"), COL)
    in_specs = (
        tokens, P(("z", "xh")), P(COL), P(COL, "y", None), P("y", COL), P(COL),
        P(COL, "y"), P(COL, "y"), P("y", COL), tokens,
    )
    out_specs = (
        tokens, tokens, P(COL), P(COL, "y", None), P("y", COL), P(COL),
        P(COL, "y"), P(COL, "y"), P("y", COL),
    )
    return jax.shard_map(
        on_device, mesh=fine, in_specs=in_specs, out_specs=out_specs, check_vma=False
    )
```

```python
import functools

import jax
import jax.numpy as jnp
from jax import lax
from jax.experimental import pallas as pl
from jax.experimental.pallas import tpu as pltpu
from jax.sharding import Mesh
from jax.sharding import PartitionSpec as P

HD = 64
norm_eps = 1e-05
rope_base = 10000.0
masked = -1e30

COL = ("xl", "k")
RING = ("xh", "xl")
BF16 = jnp.bfloat16
F32 = jnp.float32


def trade(values, axes, mask, size=4):
    return lax.ppermute(values, axes, [(i, i ^ mask) for i in range(size)])


def trade_row(values, mask):
    return trade(values, "y", mask)


def trade_col(values, mask):
    return trade(values, COL, mask)


def trade_core(values):
    return trade(values, "k", 1, 2)


def trade_ring(values, mask):
    return trade(values, RING, mask)


def trade_deep(values, mask):
    return trade(values, "z", mask)


def after(values, *earlier):
    return lax.optimization_barrier((values, earlier))[0]


def pick(bit, zero, one):
    return jnp.where(bit == 0, zero, one)


def in_order(parts, index):
    low, high = index % 2, index // 2
    a, b, c, d = parts
    a, b = pick(low, a, b), pick(low, b, a)
    c, d = pick(low, c, d), pick(low, d, c)
    return [pick(high, a, c), pick(high, b, d), pick(high, c, a), pick(high, d, b)]


def cut(values, count, axis):
    return jnp.split(values, count, axis)


def gather_row(values):
    return lax.all_gather(values, "y", axis=0, tiled=True)


def sum_row(partial):
    return lax.psum_scatter(partial, "y", scatter_dimension=0, tiled=True)


def spread_row(values):
    return [values] + [trade_row(values, j) for j in (1, 2, 3)]


def row_parts(partial, row):
    size = partial.shape[0] // 4
    return [lax.dynamic_slice_in_dim(partial, (row ^ j) * size, size, 0) for j in range(4)]


def collect_row(parts):
    return [parts[0]] + [trade_row(parts[j], j) for j in (1, 2, 3)]


def by_width(parts, low):
    return [
        pick(low, parts[core + 2 * place], parts[core + 2 * (1 - place)])
        for core in range(2)
        for place in range(2)
    ]


def of_width(values, low):
    blocks = cut(values, 4, 1)
    return [
        pick(low, blocks[2 * core + place], blocks[2 * core + 1 - place])
        for place in range(2)
        for core in range(2)
    ]


def to_full_width(values, col, *alongside):
    size = values[0].shape[0] // 4
    send = lambda m: jnp.concatenate(
        [lax.dynamic_slice_in_dim(v, (col ^ m) * size, size, 0) for v in values], axis=1
    )
    parts = [send(0)] + [trade_col(send(m), m) for m in (1, 2, 3)]
    parts, alongside = lax.optimization_barrier((parts, alongside))
    parts = [cut(part, len(values), 1) for part in parts]
    rows = [
        jnp.concatenate(by_width([part[i] for part in parts], col // 2), axis=1)
        for i in range(len(values))
    ]
    return rows, alongside


def to_blocks(values, col):
    parts = of_width(values, col // 2)
    kind = values.dtype
    parts = [parts[0]] + [trade_col(parts[m].astype(BF16), m).astype(kind) for m in (1, 2, 3)]
    return jnp.concatenate(in_order(parts, col), axis=0)


def ring_send(halves):
    return [trade_ring(halves[0], 1), trade_ring(halves[1], 3)]


def ring_join(halves, got, low, axis):
    shard, other = jnp.concatenate(halves), jnp.concatenate(got)
    return jnp.concatenate([pick(low, shard, other), pick(low, other, shard)], axis=axis)


def add_low(*terms):
    total = terms[0].astype(F32)
    for term in terms[1:]:
        total = total + term.astype(F32)
    return total.astype(BF16)


def at(values, index):
    return lax.dynamic_index_in_dim(values, index, 0, keepdims=False)


def ring_parts(blocks, low, high):
    half = blocks[0].shape[1] // 2
    take = lambda place, which: jnp.concatenate(
        [
            lax.dynamic_slice(v, (place, which * half, 0), (1, half, v.shape[2]))[0]
            for v in blocks
        ],
        axis=1,
    )
    return [take(low, high), take(1 - low, high), take(low, 1 - high), take(1 - low, 1 - high)]


def deep_parts(blocks, deep):
    size = blocks.shape[-2] // 4
    return [
        lax.dynamic_slice_in_dim(blocks, (deep ^ j) * size, size, blocks.ndim - 2) for j in range(4)
    ]


def trade_near(parts, trader):
    return [trader(parts[1], 1), trader(parts[3], 3)]


def exchange(parts, trader):
    return add_low(parts[0], *lax.optimization_barrier([trader(parts[j], j) for j in (1, 2, 3)]))


def ring_gather(values, high):
    other = trade_ring(values, 2)
    return jnp.concatenate([pick(high, values, other), pick(high, other, values)], axis=0)


def deep_gather(values, deep):
    parts = lax.optimization_barrier([values] + [trade_deep(values, j) for j in (1, 2, 3)])
    return jnp.concatenate(in_order(parts, deep), axis=0)


def product(left, right, dims, kind=F32):
    return lax.dot_general(left, right, (dims, ((), ())), preferred_element_type=F32).astype(kind)


def scale_of(values):
    return lax.rsqrt(jnp.mean(values * values, axis=1, keepdims=True) + norm_eps)


def add_and_norm(base_ref, p0, p1, p2, p3, hidden_ref, normed_ref):
    hidden = (p0[...].astype(F32) + p1[...].astype(F32)) + (p2[...].astype(F32) + p3[...].astype(F32))
    hidden = base_ref[...] + hidden
    hidden_ref[...] = hidden
    normed_ref[...] = (hidden * scale_of(hidden)).astype(BF16)


def norm_back(values, weighted, passed):
    scale = scale_of(values)
    inner = jnp.mean(weighted * values, axis=1, keepdims=True)
    return passed + (scale * weighted - values * (scale**3 * inner))


def norm_back_low(values_ref, part_ref, passed_ref, grad_ref, low_ref):
    grad = norm_back(values_ref[...], part_ref[...].astype(F32), passed_ref[...].astype(F32))
    grad_ref[...] = grad
    low_ref[...] = grad.astype(BF16)


def norm_back_high(values_ref, part_ref, passed_ref, grad_ref):
    grad_ref[...] = norm_back(values_ref[...], part_ref[...].astype(F32), passed_ref[...])


def turn(first, second, cosine, sine):
    return first * cosine - second * sine, second * cosine + first * sine


def project(x_ref, mine_ref, theirs_ref, cos_ref, sin_ref, q_ref, kv_ref):
    width = mine_ref.shape[1]
    slots = kv_ref.shape[0] + q_ref.shape[0]
    total = None
    for core, weights in enumerate((mine_ref, theirs_ref)):
        for place in range(2):
            spot = (2 * core + place) * width
            term = jnp.dot(
                x_ref[:, spot : spot + width], weights[place, :, :slots], preferred_element_type=F32
            )
            total = term if total is None else total + term
    turned = total.T
    cosine, sine = cos_ref[...], sin_ref[...]
    half = HD // 2
    heads = q_ref.shape[0] // HD
    for head in range(heads + 1):
        spot = head * HD
        first, second = turn(
            turned[spot : spot + half], turned[spot + half : spot + HD], cosine, sine
        )
        if head < heads:
            q_ref[spot : spot + half, :] = (first * HD**-0.5).astype(BF16)
            q_ref[spot + half : spot + HD, :] = (second * HD**-0.5).astype(BF16)
        else:
            kv_ref[:half, :] = first.astype(BF16)
            kv_ref[half:HD, :] = second.astype(BF16)
    kv_ref[HD:, :] = turned[(heads + 1) * HD :].astype(BF16)


def lay_keys(pairs, kt_ref, vt_ref, kn_ref, vn_ref):
    size = pairs.shape[2] // 4
    for block in range(4):
        for m in range(4):
            piece = pairs[m, :, block * size : (block + 1) * size]
            spot = slice(m * size, (m + 1) * size)
            kt_ref[block, :, spot] = piece[:HD]
            if vt_ref is not None:
                vt_ref[block, :, spot] = piece[HD:]
            natural = piece.astype(F32).T.astype(BF16)
            kn_ref[block, spot, :] = natural[:, :HD]
            vn_ref[block, spot, :] = natural[:, HD:]


def side_by_side(ref, first, count, depth, spot, size):
    return jnp.concatenate(
        [ref[head * depth : (head + 1) * depth, spot : spot + size] for head in range(first, first + count)],
        axis=1,
    )


def admitted(koff_ref, start, qpos, qstart, diagonal, count):
    keys = koff_ref[...] + start
    allowed = keys >= qstart
    if diagonal:
        allowed = allowed & (keys <= qpos)
    return jnp.concatenate([allowed] * count, axis=1)


def attend(
    q_ref, pairs_ref, koff_ref, qpos_ref, qstart_ref, o_ref, low_ref, lse_ref, kt_ref, vt_ref, kn_ref, vn_ref
):
    span = kn_ref.shape[1]
    size = span // 4
    heads = q_ref.shape[0] // HD
    lay_keys(pairs_ref, kt_ref, vt_ref, kn_ref, vn_ref)
    for block in range(4):
        spot = block * size
        qpos, qstart = qpos_ref[:, spot : spot + size], qstart_ref[:, spot : spot + size]
        query = side_by_side(q_ref, 0, heads, HD, spot, size)
        top = jnp.full((1, heads * size), masked, F32)
        total = jnp.zeros((1, heads * size), F32)
        accum = jnp.zeros((HD, heads * size), F32)
        for number in (block, *range(block)):
            scores = jnp.dot(kn_ref[number], query, preferred_element_type=F32)
            allowed = admitted(koff_ref, number * span, qpos, qstart, number == block, heads)
            scores = jnp.where(allowed, scores, masked)
            new_top = jnp.maximum(top, jnp.max(scores, axis=0, keepdims=True))
            weights = jnp.exp(scores - new_top)
            shrink = jnp.exp(top - new_top)
            total = total * shrink + jnp.sum(weights, axis=0, keepdims=True)
            accum = accum * shrink + jnp.dot(
                vt_ref[number], weights.astype(BF16), preferred_element_type=F32
            )
            top = new_top
        result = accum / total
        lse = top + jnp.log(total)
        for head in range(heads):
            piece = result[:, head * size : (head + 1) * size]
            rows = slice(head * HD, (head + 1) * HD)
            o_ref[rows, spot : spot + size] = piece
            low_ref[rows, spot : spot + size] = piece.astype(BF16)
            lse_ref[head : head + 1, spot : spot + size] = lse[:, head * size : (head + 1) * size]


def attend_back(
    q_ref, pairs_ref, koff_ref, qpos_ref, qstart_ref, o_ref, lse_ref, go_ref, cos_ref, sin_ref, *refs,
    first, count, last_call,
):
    if last_call:
        gk_in, gv_in, gq_ref, g0, g1, g2, g3, kt_ref, kn_ref, vn_ref, gk_ref, gv_ref = refs
    else:
        gq_ref, gk_ref, gv_ref, kt_ref, kn_ref, vn_ref = refs
    span = kn_ref.shape[1]
    size = span // 4
    lay_keys(pairs_ref, kt_ref, None, kn_ref, vn_ref)
    gk_ref[...] = gk_in[...] if last_call else jnp.zeros_like(gk_ref)
    gv_ref[...] = gv_in[...] if last_call else jnp.zeros_like(gv_ref)
    last = (((1,), (1,)), ((), ()))
    for block in range(4):
        spot = block * size
        here = slice(spot, spot + size)
        qpos, qstart = qpos_ref[:, here], qstart_ref[:, here]
        cosine, sine = cos_ref[:, here], sin_ref[:, here]
        pick_heads = lambda ref, depth: side_by_side(ref, first, count, depth, spot, size)
        query, grad_out = pick_heads(q_ref, HD), pick_heads(go_ref, HD)
        lse = pick_heads(lse_ref, 1)
        delta = jnp.sum(grad_out.astype(F32) * pick_heads(o_ref, HD), axis=0, keepdims=True)
        grad_query = jnp.zeros((HD, count * size), F32)
        for number in (block, *range(block)):
            scores = jnp.dot(kn_ref[number], query, preferred_element_type=F32)
            allowed = admitted(koff_ref, number * span, qpos, qstart, number == block, count)
            probs = jnp.exp(jnp.where(allowed, scores - lse, masked))
            grad_probs = jnp.dot(vn_ref[number], grad_out, preferred_element_type=F32)
            grad_scores = (probs * (grad_probs - delta)).astype(BF16)
            gv_ref[number] += lax.dot_general(
                grad_out, probs.astype(BF16), last, preferred_element_type=F32
            )
            gk_ref[number] += lax.dot_general(query, grad_scores, last, preferred_element_type=F32)
            grad_query = grad_query + jnp.dot(
                kt_ref[number], grad_scores, preferred_element_type=F32
            )
        half = HD // 2
        for head in range(count):
            grad = grad_query[:, head * size : (head + 1) * size] * HD**-0.5
            upper, lower = turn(grad[:half], grad[half:], cosine, -sine)
            gq_ref[head * HD : head * HD + half, here] = upper.astype(BF16)
            gq_ref[head * HD + half : (head + 1) * HD, here] = lower.astype(BF16)
    if last_call:
        for block in range(4):
            for m, ref in enumerate((g0, g1, g2, g3)):
                spot, out = slice(m * size, (m + 1) * size), slice(block * size, (block + 1) * size)
                ref[:HD, out] = gk_ref[block, :, spot].astype(BF16)
                ref[HD:, out] = gv_ref[block, :, spot].astype(BF16)


def project_back(
    gq0, gq1, g0, g1, g2, g3, cos_ref, sin_ref, mine_ref, theirs_ref, gqkv_ref, part_ref
):
    pair = g0[...].astype(F32) + g1[...].astype(F32) + (g2[...].astype(F32) + g3[...].astype(F32))
    half = HD // 2
    first, second = turn(pair[:half], pair[half:HD], cos_ref[...], -sin_ref[...])
    turned = jnp.concatenate(
        [gq0[...].astype(F32), gq1[...].astype(F32), first, second, pair[HD:]], axis=0
    )
    gqkv_ref[...] = turned.astype(BF16)
    natural = turned.T.astype(BF16)
    width = mine_ref.shape[1]
    slots = turned.shape[0]
    for core, weights in enumerate((mine_ref, theirs_ref)):
        for place in range(2):
            spot = (2 * core + place) * width
            part = lax.dot_general(
                natural, weights[place, :, :slots], (((1,), (1,)), ((), ())), preferred_element_type=F32
            )
            part_ref[:, spot : spot + width] = part.astype(BF16)


def feed(h_ref, gi_ref, own_ref, other_ref, inner_ref, pair_ref, part_ref, w_ref, sems):
    units = gi_ref.shape[1]
    depth = own_ref.shape[0]
    groups = feed_groups(units)
    copies = []
    for group, (begin, end) in enumerate(groups):
        mine = []
        for core, ref in enumerate((own_ref, other_ref)):
            for start in (0, units):
                columns = pl.ds(start + begin, end - begin)
                copy = pltpu.make_async_copy(
                    ref.at[:, columns],
                    w_ref.at[pl.ds(core * depth, depth), columns],
                    sems.at[group, len(mine)],
                )
                copy.start()
                mine.append(copy)
        copies.append(mine)
    for (begin, end), mine in zip(groups, copies):
        for copy in mine:
            copy.wait()
        gate = jnp.dot(h_ref[...], w_ref[:, begin:end], preferred_element_type=F32)
        up = jnp.dot(h_ref[...], w_ref[:, units + begin : units + end], preferred_element_type=F32)
        grad_inner = gi_ref[:, begin:end]
        sig = 1.0 / (1.0 + jnp.exp(-gate))
        act = gate * sig
        inner_ref[:, begin:end] = (act * up).astype(BF16)
        grad_gate = grad_inner * up * (sig * (1.0 + gate * (1.0 - sig)))
        pair_ref[:, begin:end] = grad_gate.astype(BF16)
        pair_ref[:, units + begin : units + end] = (grad_inner * act).astype(BF16)
    for begin in range(0, 2 * depth, 512):
        part = lax.dot_general(
            pair_ref[...], w_ref[begin : begin + 512, :], (((1,), (1,)), ((), ())),
            preferred_element_type=F32,
        )
        part_ref[:, begin : begin + 512] = part.astype(BF16)


def feed_groups(units):
    ends = [128, 384] + list(range(896, units, 512)) + [units]
    return list(zip([0] + ends[:-1], ends))


def spread_heads(row_ref, w_ref, b0, b1, b2, b3, out_ref):
    size = b0.shape[0]
    for j, part in enumerate((b0, b1, b2, b3)):
        spot = pl.multiple_of((row_ref[0] ^ j) * size, size)
        piece = lax.dot_general(
            w_ref[...], part[...], (((1,), (1,)), ((), ())), preferred_element_type=F32
        )
        out_ref[:, pl.ds(spot, size)] = piece.astype(BF16)


def kernel_call(body, out_shape, operands, flops, scratch=(), scalars=0, outside=(), staged=(), mib=48):
    moved = sum(x.size * x.dtype.itemsize for x in operands)
    count = len(operands)
    spaces = [
        pltpu.SMEM if i < scalars else pl.ANY if i in outside or i in staged else pltpu.VMEM
        for i in range(count)
    ]
    if staged:
        held = [pltpu.VMEM(operands[i].shape, operands[i].dtype) for i in staged]
        scratch = [*scratch, *held, pltpu.SemaphoreType.DMA((len(staged),))]

        def whole(*refs):
            refs, buffers, sems = list(refs[: -len(staged) - 1]), refs[-len(staged) - 1 : -1], refs[-1]
            copies = [
                pltpu.make_async_copy(refs[i], buffer, sems.at[n])
                for n, (i, buffer) in enumerate(zip(staged, buffers))
            ]
            for copy in copies:
                copy.start()
            for copy in copies:
                copy.wait()
            for i, buffer in zip(staged, buffers):
                refs[i] = buffer
            body(*refs)
    else:
        whole = body
    out_specs = jax.tree.map(lambda _: pl.BlockSpec(memory_space=pltpu.VMEM), out_shape)
    return pl.pallas_call(
        whole,
        out_shape=out_shape,
        in_specs=[pl.BlockSpec(memory_space=space) for space in spaces],
        out_specs=out_specs,
        scratch_shapes=list(scratch),
        compiler_params=pltpu.CompilerParams(vmem_limit_bytes=mib * 1024 * 1024),
        cost_estimate=pl.CostEstimate(flops=flops, bytes_accessed=moved, transcendentals=0),
    )(*operands)


def rows_call(body, kinds, operands, steps=2):
    rows, width = operands[0].shape
    block = pl.BlockSpec((rows // steps, width), lambda i: (i, 0))
    out_shape = tuple(jax.ShapeDtypeStruct((rows, width), kind) for kind in kinds)
    moved = sum(x.size * x.dtype.itemsize for x in operands)
    return pl.pallas_call(
        body,
        out_shape=out_shape,
        grid=(steps,),
        in_specs=[block] * len(operands),
        out_specs=(block,) * len(kinds),
        cost_estimate=pl.CostEstimate(flops=0, bytes_accessed=moved, transcendentals=0),
    )(*operands)


def on_device(
    tokens_in, segment_ids, attn_gain, w_qkv, w_out, mlp_gain, w_gate, w_up, w_down, cotangent
):
    group = segment_ids.shape[0]
    span = group // 4
    size = span // 4
    units = w_gate.shape[1]
    slots = w_qkv.shape[2] // HD
    heads = slots - 2
    deep, high, row = lax.axis_index("z"), lax.axis_index("xh"), lax.axis_index("y")
    low, core = lax.axis_index("xl"), lax.axis_index("k")
    col = low * 2 + core

    indices = jnp.arange(group, dtype=jnp.int32)
    previous = jnp.concatenate([segment_ids[:1] - 1, segment_ids[:-1]])
    starts = lax.cummax(jnp.where(segment_ids != previous, indices, 0), axis=0)
    bases = [j * span + col * size for j in range(4)]
    my_starts = jnp.concatenate([lax.dynamic_slice_in_dim(starts, b, size, 0) for b in bases])
    lanes = jnp.arange(size, dtype=jnp.int32)
    my_index = jnp.concatenate([lanes + b for b in bases])
    half_dim = HD // 2
    inverse_freq = rope_base ** (-jnp.arange(half_dim, dtype=F32) * 2.0 / HD)
    angles = inverse_freq[:, None] * (my_index - my_starts).astype(F32)[None, :]
    cosine, sine = jnp.cos(angles), jnp.sin(angles)
    key_offset = jnp.concatenate([lanes + (col ^ m) * size for m in range(4)])
    key_offset = jnp.broadcast_to(key_offset[:, None], (span, size))
    qpos, qstart = my_index[None, :], my_starts[None, :]
    cut_at = slots * HD

    flat_qkv = w_qkv.reshape(w_qkv.shape[0], -1)
    qkv_out = jnp.concatenate([(flat_qkv * attn_gain[:, None]).astype(BF16), w_out], axis=1)
    (inputs,), alongside = to_full_width(
        [tokens_in], col, cosine, sine, key_offset, qpos, qstart, *cut(qkv_out, 2, 0)
    )
    cosine, sine, key_offset, qpos, qstart, qkv_out_first, qkv_out_second = alongside
    inputs = inputs.astype(F32)
    normed_one = (inputs * scale_of(inputs)).astype(BF16)
    rows_one = gather_row(normed_one)

    qkv_out_halves = [qkv_out_first, qkv_out_second]
    mine = ring_join(qkv_out_halves, lax.optimization_barrier(ring_send(qkv_out_halves)), low, 0)
    mine = mine.reshape(2, *qkv_out.shape)
    theirs = trade_core(mine)
    (cot_rows,), _ = to_full_width([after(cotangent, mine)], col)
    scaled = lambda v: (v * mlp_gain[:, None]).astype(BF16)
    gate_up = jnp.concatenate([scaled(w_gate), scaled(w_up)], axis=1)
    gu_halves = [after(v, normed_one) for v in cut(gate_up, 2, 0)]
    full_out = jnp.concatenate(
        [mine[0, :, cut_at:], mine[1, :, cut_at:], theirs[0, :, cut_at:], theirs[1, :, cut_at:]],
        axis=1,
    )
    rows_one, gu_halves, full_out, cot_rows = lax.optimization_barrier(
        (rows_one, gu_halves, full_out, cot_rows)
    )
    gu_got = ring_send(gu_halves)

    shape = lambda kind, *dims: jax.ShapeDtypeStruct(dims, kind)
    scratch = lambda kind, *dims: pltpu.VMEM(dims, kind)
    width = inputs.shape[1]
    matmul = lambda rows, depth, columns: 2 * rows * depth * columns
    query, pairs = kernel_call(
        project,
        (shape(BF16, heads * HD, span), shape(BF16, 2 * HD, span)),
        (rows_one, mine, theirs, cosine, sine),
        matmul(span, width, cut_at),
        staged=(0,),
    )
    grad_rows = gather_row(after(cot_rows, query))
    all_pairs = jnp.stack([pairs] + [trade_col(pairs, m) for m in (1, 2, 3)])

    flops = 2 * matmul(heads * span, HD, group)
    keys_shape = (4, HD, span), (4, span, HD)
    mixed, mixed_low, lse = kernel_call(
        attend,
        (shape(F32, heads * HD, span), shape(BF16, heads * HD, span), shape(F32, heads, span)),
        (query, all_pairs, key_offset, qpos, qstart),
        flops,
        scratch=[scratch(BF16, *keys_shape[i]) for i in (0, 0, 1, 1)],
    )
    branch = product(mixed_low, full_out, ((0,), (0,)), BF16)
    gu_mine = ring_join(gu_halves, after(gu_got, branch), low, 0)
    down_halves = [after(v, branch, gu_got) for v in cut(w_down, 2, 0)]
    down_got = ring_send(down_halves)
    branch_parts = after(collect_row(row_parts(branch, row)), gu_mine, down_got)
    hidden, normed_two = rows_call(add_and_norm, (F32, BF16), (inputs, *branch_parts))
    down_mine = ring_join(down_halves, after(down_got, hidden), low, 1)
    full_down = jnp.concatenate([down_mine, trade_core(down_mine)], axis=1)
    grad_inner = product(grad_rows, full_down, ((1,), (1,)))
    gu_theirs = trade_core(after(gu_mine, hidden))
    rows_two = gather_row(normed_two)

    side = lambda v, which: v[:, which * width // 2 : (which + 1) * width // 2]
    both_cores = lambda v, axis=0: jnp.concatenate([v, trade_core(v)], axis=axis)
    half_of = lambda v: jnp.concatenate([side(v, 0), trade_core(side(v, 1))])

    def half_by_ring(v):
        blocks = [cut(v, 8, 1)[i] for i in (0, 2, 1, 3, 4, 6, 5, 7)]
        sides = [jnp.concatenate(blocks[:4], axis=1), jnp.concatenate(blocks[4:], axis=1)]
        return jnp.concatenate([sides[0], trade_core(sides[1])])

    token_sum = lambda a, b: product(a, b, ((0,), (0,)), BF16)
    cot_half, heads_both = half_by_ring(after(grad_rows, hidden)), both_cores(after(mixed_low, hidden), 1)
    one_half = half_of(after(rows_one, hidden))
    rows_two, cot_half, heads_both, one_half = lax.optimization_barrier(
        (rows_two, cot_half, heads_both, one_half)
    )
    two_half = half_by_ring(rows_two)
    inner, grad_pair, part_two = kernel_call(
        feed,
        (shape(BF16, span, units), shape(BF16, span, 2 * units), shape(BF16, span, width)),
        (rows_two, grad_inner, gu_mine, gu_theirs),
        2 * matmul(span, width, 2 * units),
        scratch=(scratch(BF16, width, 2 * units), pltpu.SemaphoreType.DMA((len(feed_groups(units)), 4))),
        outside=(2, 3),
    )
    inner_both = both_cores(inner)
    pair_both = both_cores(grad_pair)
    mlp_sums = jnp.concatenate([token_sum(two_half, pair_both), token_sum(cot_half, inner_both)], axis=1)
    grad_n2, mlp_sums = lax.optimization_barrier((sum_row(part_two), mlp_sums))
    mlp_sums = lax.psum_scatter(mlp_sums, ("xh", "xl", "z"), scatter_dimension=0, tiled=True)
    grad_hidden, grad_low = rows_call(norm_back_low, (F32, BF16), (hidden, grad_n2, cot_rows))
    branch_parts = spread_row(grad_low)
    result_parts = row_parts(product(inner, full_down, ((1,), (0,)), BF16), row)
    branch_parts, result_parts = lax.optimization_barrier((branch_parts, result_parts))
    grad_heads = kernel_call(
        spread_heads,
        shape(BF16, heads * HD, span),
        (row.astype(jnp.int32)[None], full_out, *branch_parts),
        matmul(span, width, heads * HD),
        scalars=1,
    )
    pair_shape = shape(BF16, 2 * HD, span)
    known = (query, all_pairs, key_offset, qpos, qstart, mixed, lse, grad_heads, cosine, sine)
    half_heads = shape(BF16, heads * HD // 2, span)
    keys_scratch = [scratch(BF16, *keys_shape[i]) for i in (0, 1, 1)]
    key_sums = (shape(F32, *keys_shape[0]),) * 2
    split = functools.partial(attend_back, count=heads // 2)
    result_near = trade_near(result_parts, trade_row)
    gq_first, *key_grads = kernel_call(
        functools.partial(split, first=0, last_call=False),
        (half_heads,) + key_sums,
        known,
        flops * 5 // 4,
        scratch=keys_scratch,
        staged=(1,),
    )
    key_grads, result_near = lax.optimization_barrier((key_grads, result_near))
    result_far = trade_row(after(result_parts[2], result_near), 2)
    gq_last, *grad_pairs = kernel_call(
        functools.partial(split, first=heads // 2, last_call=True),
        (half_heads,) + (pair_shape,) * 4,
        (*known, *key_grads),
        flops * 5 // 4,
        scratch=keys_scratch + [scratch(F32, *keys_shape[0])] * 2,
        staged=(1,),
    )
    grad_pairs = [grad_pairs[0]] + [trade_col(grad_pairs[m], m) for m in (1, 2, 3)]
    grad_pairs = lax.optimization_barrier(grad_pairs)
    grad_qkv, part_one = kernel_call(
        project_back,
        (shape(BF16, cut_at, span), shape(BF16, span, width)),
        (gq_first, gq_last, *grad_pairs, cosine, sine, mine, theirs),
        matmul(span, width, cut_at),
    )
    qkv_both = both_cores(grad_qkv, 1)
    branch_rows = jnp.concatenate(in_order(after(branch_parts, grad_qkv), row))
    branch_half = half_of(branch_rows)
    qkv_sum = product(one_half, qkv_both, ((0,), (1,)), BF16).reshape(2, width // 4, -1)
    out_sum = product(branch_half, heads_both, ((0,), (1,)), BF16).reshape(2, width // 4, -1)
    both_parts = deep_parts(jnp.concatenate([qkv_sum, out_sum], axis=2), deep)
    both_sums = exchange(both_parts, trade_deep)
    rows_here = mlp_sums.shape[0]
    rows_here = mlp_sums.shape[0]
    own_rows = lambda w: lax.dynamic_slice_in_dim(w, (high * 4 + deep) * rows_here, rows_here, 0)
    own_gain = jnp.sum(own_rows(w_gate) * mlp_sums[:, :units].astype(F32), axis=1, keepdims=True)
    own_gain += jnp.sum(own_rows(w_up) * mlp_sums[:, units : 2 * units].astype(F32), axis=1, keepdims=True)
    own_gain = jnp.broadcast_to(own_gain, (rows_here, 128))
    own_gain = own_gain + trade_row(own_gain, 1)
    own_gain = (own_gain + trade_row(own_gain, 2)).astype(BF16)
    mlp_sums = jnp.concatenate([mlp_sums, own_gain], axis=1)
    mlp_sums, both_sums = lax.optimization_barrier((mlp_sums, both_sums))
    mlp_total = ring_gather(mlp_sums, high)
    both_total = exchange(ring_parts([both_sums], low, high), trade_ring)
    mlp_total, both_total = lax.optimization_barrier((mlp_total, both_total))
    mlp_total = lax.all_gather(mlp_total, "z", axis=0, tiled=True)
    both_total = ring_gather(both_total, high)
    grad_n1 = sum_row(part_one)
    (grad_in,) = rows_call(norm_back_high, (F32,), (inputs, grad_n1, grad_hidden))
    both_total, grad_in, result_far = lax.optimization_barrier((both_total, to_blocks(grad_in, col), result_far))
    both_total = deep_gather(both_total, deep).astype(F32)
    result = (hidden + result_parts[0].astype(F32)) + result_far.astype(F32)
    result = (result + sum(part.astype(F32) for part in result_near)).astype(BF16)
    result = to_blocks(result, col)
    both_total, result = lax.optimization_barrier((both_total, result))
    qkv_total, out_total = both_total[:, :cut_at], both_total[:, cut_at:]
    qkv_gain = jnp.sum(flat_qkv * qkv_total, axis=1)[None]
    qkv_gain = sum([trade_row(qkv_gain, j) for j in (1, 2, 3)], qkv_gain)[0]
    mlp_total = mlp_total.reshape(4, 2, rows_here, -1).swapaxes(0, 1).reshape(mlp_total.shape)
    piece = lambda first: mlp_total[:, first : first + units].astype(F32)
    return (
        result,
        grad_in,
        qkv_gain,
        (qkv_total * attn_gain[:, None]).reshape(w_qkv.shape),
        out_total.T,
        mlp_total[:, 3 * units].astype(F32),
        piece(0) * mlp_gain[:, None],
        piece(units) * mlp_gain[:, None],
        piece(2 * units).T,
    )


def solution(mesh):
    dp, rows, cols = mesh.devices.shape
    fine = Mesh(
        mesh.devices.reshape(dp // 2, 2, rows, cols // 2, 2), ("z", "xh", "y", "xl", "k")
    )
    tokens = P(("z", "xh", "y"), COL)
    in_specs = (
        tokens, P(("z", "xh")), P(COL), P(COL, "y", None), P("y", COL), P(COL),
        P(COL, "y"), P(COL, "y"), P("y", COL), tokens,
    )
    out_specs = (
        tokens, tokens, P(COL), P(COL, "y", None), P("y", COL), P(COL),
        P(COL, "y"), P(COL, "y"), P("y", COL),
    )
    return jax.shard_map(
        on_device, mesh=fine, in_specs=in_specs, out_specs=out_specs, check_vma=False
    )
```

```python
import functools

import jax
import jax.numpy as jnp
from jax import lax
from jax.experimental import pallas as pl
from jax.experimental.pallas import tpu as pltpu
from jax.sharding import Mesh
from jax.sharding import PartitionSpec as P

HD = 64
norm_eps = 1e-05
rope_base = 10000.0
masked = -1e30

COL = ("xl", "k")
RING = ("xh", "xl")
BF16 = jnp.bfloat16
F32 = jnp.float32


def trade(values, axes, mask, size=4):
    return lax.ppermute(values, axes, [(i, i ^ mask) for i in range(size)])


def trade_row(values, mask):
    return trade(values, "y", mask)


def trade_col(values, mask):
    return trade(values, COL, mask)


def trade_core(values):
    return trade(values, "k", 1, 2)


def trade_ring(values, mask):
    return trade(values, RING, mask)


def trade_deep(values, mask):
    return trade(values, "z", mask)


def after(values, *earlier):
    return lax.optimization_barrier((values, earlier))[0]


def pick(bit, zero, one):
    return jnp.where(bit == 0, zero, one)


def in_order(parts, index):
    low, high = index % 2, index // 2
    a, b, c, d = parts
    a, b = pick(low, a, b), pick(low, b, a)
    c, d = pick(low, c, d), pick(low, d, c)
    return [pick(high, a, c), pick(high, b, d), pick(high, c, a), pick(high, d, b)]


def cut(values, count, axis):
    return jnp.split(values, count, axis)


def gather_row(values):
    return lax.all_gather(values, "y", axis=0, tiled=True)


def sum_row(partial):
    return lax.psum_scatter(partial, "y", scatter_dimension=0, tiled=True)


def spread_row(values):
    return [values] + [trade_row(values, j) for j in (1, 2, 3)]


def row_parts(partial, row):
    size = partial.shape[0] // 4
    return [lax.dynamic_slice_in_dim(partial, (row ^ j) * size, size, 0) for j in range(4)]


def collect_row(parts):
    return [parts[0]] + [trade_row(parts[j], j) for j in (1, 2, 3)]


def by_width(parts, low):
    return [
        pick(low, parts[core + 2 * place], parts[core + 2 * (1 - place)])
        for core in range(2)
        for place in range(2)
    ]


def of_width(values, low):
    blocks = cut(values, 4, 1)
    return [
        pick(low, blocks[2 * core + place], blocks[2 * core + 1 - place])
        for place in range(2)
        for core in range(2)
    ]


def to_full_width(values, col, *alongside):
    size = values[0].shape[0] // 4
    send = lambda m: jnp.concatenate(
        [lax.dynamic_slice_in_dim(v, (col ^ m) * size, size, 0) for v in values], axis=1
    )
    parts = [send(0)] + [trade_col(send(m), m) for m in (1, 2, 3)]
    parts, alongside = lax.optimization_barrier((parts, alongside))
    parts = [cut(part, len(values), 1) for part in parts]
    rows = [
        jnp.concatenate(by_width([part[i] for part in parts], col // 2), axis=1)
        for i in range(len(values))
    ]
    return rows, alongside


def to_blocks(values, col):
    parts = of_width(values, col // 2)
    kind = values.dtype
    parts = [parts[0]] + [trade_col(parts[m].astype(BF16), m).astype(kind) for m in (1, 2, 3)]
    return jnp.concatenate(in_order(parts, col), axis=0)


def ring_send(halves):
    return [trade_ring(halves[0], 1), trade_ring(halves[1], 3)]


def ring_join(halves, got, low, axis):
    shard, other = jnp.concatenate(halves), jnp.concatenate(got)
    return jnp.concatenate([pick(low, shard, other), pick(low, other, shard)], axis=axis)


def add_low(*terms):
    total = terms[0].astype(F32)
    for term in terms[1:]:
        total = total + term.astype(F32)
    return total.astype(BF16)


def at(values, index):
    return lax.dynamic_index_in_dim(values, index, 0, keepdims=False)


def ring_parts(blocks, low, high):
    half = blocks[0].shape[1] // 2
    take = lambda place, which: jnp.concatenate(
        [
            lax.dynamic_slice(v, (place, which * half, 0), (1, half, v.shape[2]))[0]
            for v in blocks
        ],
        axis=1,
    )
    return [take(low, high), take(1 - low, high), take(low, 1 - high), take(1 - low, 1 - high)]


def deep_parts(blocks, deep):
    size = blocks.shape[-2] // 4
    return [
        lax.dynamic_slice_in_dim(blocks, (deep ^ j) * size, size, blocks.ndim - 2) for j in range(4)
    ]


def trade_near(parts, trader):
    return [trader(parts[1], 1), trader(parts[3], 3)]


def exchange(parts, trader):
    return add_low(parts[0], *lax.optimization_barrier([trader(parts[j], j) for j in (1, 2, 3)]))


def ring_gather(values, high):
    other = trade_ring(values, 2)
    return jnp.concatenate([pick(high, values, other), pick(high, other, values)], axis=0)


def deep_gather(values, deep):
    parts = lax.optimization_barrier([values] + [trade_deep(values, j) for j in (1, 2, 3)])
    return jnp.concatenate(in_order(parts, deep), axis=0)


def product(left, right, dims, kind=F32):
    return lax.dot_general(left, right, (dims, ((), ())), preferred_element_type=F32).astype(kind)


def scale_of(values):
    return lax.rsqrt(jnp.mean(values * values, axis=1, keepdims=True) + norm_eps)


def add_and_norm(base_ref, p0, p1, p2, p3, hidden_ref, normed_ref):
    hidden = (p0[...].astype(F32) + p1[...].astype(F32)) + (p2[...].astype(F32) + p3[...].astype(F32))
    hidden = base_ref[...] + hidden
    hidden_ref[...] = hidden
    normed_ref[...] = (hidden * scale_of(hidden)).astype(BF16)


def norm_back(values, weighted, passed):
    scale = scale_of(values)
    inner = jnp.mean(weighted * values, axis=1, keepdims=True)
    return passed + (scale * weighted - values * (scale**3 * inner))


def norm_back_low(values_ref, part_ref, passed_ref, grad_ref, low_ref):
    grad = norm_back(values_ref[...], part_ref[...].astype(F32), passed_ref[...].astype(F32))
    grad_ref[...] = grad
    low_ref[...] = grad.astype(BF16)


def norm_back_high(values_ref, part_ref, passed_ref, grad_ref):
    grad_ref[...] = norm_back(values_ref[...], part_ref[...].astype(F32), passed_ref[...])


def turn(first, second, cosine, sine):
    return first * cosine - second * sine, second * cosine + first * sine


def project(x_ref, mine_ref, theirs_ref, cos_ref, sin_ref, q_ref, kv_ref):
    width = mine_ref.shape[1]
    slots = kv_ref.shape[0] + q_ref.shape[0]
    total = None
    for core, weights in enumerate((mine_ref, theirs_ref)):
        for place in range(2):
            spot = (2 * core + place) * width
            term = jnp.dot(
                x_ref[:, spot : spot + width], weights[place, :, :slots], preferred_element_type=F32
            )
            total = term if total is None else total + term
    turned = total.T
    cosine, sine = cos_ref[...], sin_ref[...]
    half = HD // 2
    heads = q_ref.shape[0] // HD
    for head in range(heads + 1):
        spot = head * HD
        first, second = turn(
            turned[spot : spot + half], turned[spot + half : spot + HD], cosine, sine
        )
        if head < heads:
            q_ref[spot : spot + half, :] = (first * HD**-0.5).astype(BF16)
            q_ref[spot + half : spot + HD, :] = (second * HD**-0.5).astype(BF16)
        else:
            kv_ref[:half, :] = first.astype(BF16)
            kv_ref[half:HD, :] = second.astype(BF16)
    kv_ref[HD:, :] = turned[(heads + 1) * HD :].astype(BF16)


def lay_keys(pairs, kt_ref, vt_ref, kn_ref, vn_ref):
    size = pairs.shape[2] // 4
    for block in range(4):
        for m in range(4):
            piece = pairs[m, :, block * size : (block + 1) * size]
            spot = slice(m * size, (m + 1) * size)
            kt_ref[block, :, spot] = piece[:HD]
            if vt_ref is not None:
                vt_ref[block, :, spot] = piece[HD:]
            natural = piece.astype(F32).T.astype(BF16)
            kn_ref[block, spot, :] = natural[:, :HD]
            vn_ref[block, spot, :] = natural[:, HD:]


def side_by_side(ref, first, count, depth, spot, size):
    return jnp.concatenate(
        [ref[head * depth : (head + 1) * depth, spot : spot + size] for head in range(first, first + count)],
        axis=1,
    )


def admitted(koff_ref, start, qpos, qstart, diagonal, count):
    keys = koff_ref[...] + start
    allowed = keys >= qstart
    if diagonal:
        allowed = allowed & (keys <= qpos)
    return jnp.concatenate([allowed] * count, axis=1)


def attend(
    q_ref, pairs_ref, koff_ref, qpos_ref, qstart_ref, o_ref, low_ref, lse_ref, kt_ref, vt_ref, kn_ref, vn_ref
):
    span = kn_ref.shape[1]
    size = span // 4
    heads = q_ref.shape[0] // HD
    lay_keys(pairs_ref, kt_ref, vt_ref, kn_ref, vn_ref)
    for block in range(4):
        spot = block * size
        qpos, qstart = qpos_ref[:, spot : spot + size], qstart_ref[:, spot : spot + size]
        query = side_by_side(q_ref, 0, heads, HD, spot, size)
        top = jnp.full((1, heads * size), masked, F32)
        total = jnp.zeros((1, heads * size), F32)
        accum = jnp.zeros((HD, heads * size), F32)
        for number in (block, *range(block)):
            scores = jnp.dot(kn_ref[number], query, preferred_element_type=F32)
            allowed = admitted(koff_ref, number * span, qpos, qstart, number == block, heads)
            scores = jnp.where(allowed, scores, masked)
            new_top = jnp.maximum(top, jnp.max(scores, axis=0, keepdims=True))
            weights = jnp.exp(scores - new_top)
            shrink = jnp.exp(top - new_top)
            total = total * shrink + jnp.sum(weights, axis=0, keepdims=True)
            accum = accum * shrink + jnp.dot(
                vt_ref[number], weights.astype(BF16), preferred_element_type=F32
            )
            top = new_top
        result = accum / total
        lse = top + jnp.log(total)
        for head in range(heads):
            piece = result[:, head * size : (head + 1) * size]
            rows = slice(head * HD, (head + 1) * HD)
            o_ref[rows, spot : spot + size] = piece
            low_ref[rows, spot : spot + size] = piece.astype(BF16)
            lse_ref[head : head + 1, spot : spot + size] = lse[:, head * size : (head + 1) * size]


def attend_back(
    q_ref, pairs_ref, koff_ref, qpos_ref, qstart_ref, o_ref, lse_ref, go_ref, cos_ref, sin_ref, *refs,
    first, count, last_call,
):
    if last_call:
        gk_in, gv_in, gq_ref, g0, g1, g2, g3, kt_ref, kn_ref, vn_ref, gk_ref, gv_ref = refs
    else:
        gq_ref, gk_ref, gv_ref, kt_ref, kn_ref, vn_ref = refs
    span = kn_ref.shape[1]
    size = span // 4
    lay_keys(pairs_ref, kt_ref, None, kn_ref, vn_ref)
    gk_ref[...] = gk_in[...] if last_call else jnp.zeros_like(gk_ref)
    gv_ref[...] = gv_in[...] if last_call else jnp.zeros_like(gv_ref)
    last = (((1,), (1,)), ((), ()))
    for block in range(4):
        spot = block * size
        here = slice(spot, spot + size)
        qpos, qstart = qpos_ref[:, here], qstart_ref[:, here]
        cosine, sine = cos_ref[:, here], sin_ref[:, here]
        pick_heads = lambda ref, depth: side_by_side(ref, first, count, depth, spot, size)
        query, grad_out = pick_heads(q_ref, HD), pick_heads(go_ref, HD)
        lse = pick_heads(lse_ref, 1)
        delta = jnp.sum(grad_out.astype(F32) * pick_heads(o_ref, HD), axis=0, keepdims=True)
        grad_query = jnp.zeros((HD, count * size), F32)
        for number in (block, *range(block)):
            scores = jnp.dot(kn_ref[number], query, preferred_element_type=F32)
            allowed = admitted(koff_ref, number * span, qpos, qstart, number == block, count)
            probs = jnp.exp(jnp.where(allowed, scores - lse, masked))
            grad_probs = jnp.dot(vn_ref[number], grad_out, preferred_element_type=F32)
            grad_scores = (probs * (grad_probs - delta)).astype(BF16)
            gv_ref[number] += lax.dot_general(
                grad_out, probs.astype(BF16), last, preferred_element_type=F32
            )
            gk_ref[number] += lax.dot_general(query, grad_scores, last, preferred_element_type=F32)
            grad_query = grad_query + jnp.dot(
                kt_ref[number], grad_scores, preferred_element_type=F32
            )
        half = HD // 2
        for head in range(count):
            grad = grad_query[:, head * size : (head + 1) * size] * HD**-0.5
            upper, lower = turn(grad[:half], grad[half:], cosine, -sine)
            gq_ref[head * HD : head * HD + half, here] = upper.astype(BF16)
            gq_ref[head * HD + half : (head + 1) * HD, here] = lower.astype(BF16)
    if last_call:
        for block in range(4):
            for m, ref in enumerate((g0, g1, g2, g3)):
                spot, out = slice(m * size, (m + 1) * size), slice(block * size, (block + 1) * size)
                ref[:HD, out] = gk_ref[block, :, spot].astype(BF16)
                ref[HD:, out] = gv_ref[block, :, spot].astype(BF16)


def project_back(
    gq0, gq1, g0, g1, g2, g3, cos_ref, sin_ref, mine_ref, theirs_ref, gqkv_ref, part_ref
):
    pair = g0[...].astype(F32) + g1[...].astype(F32) + (g2[...].astype(F32) + g3[...].astype(F32))
    half = HD // 2
    first, second = turn(pair[:half], pair[half:HD], cos_ref[...], -sin_ref[...])
    turned = jnp.concatenate(
        [gq0[...].astype(F32), gq1[...].astype(F32), first, second, pair[HD:]], axis=0
    )
    gqkv_ref[...] = turned.astype(BF16)
    natural = turned.T.astype(BF16)
    width = mine_ref.shape[1]
    slots = turned.shape[0]
    for core, weights in enumerate((mine_ref, theirs_ref)):
        for place in range(2):
            spot = (2 * core + place) * width
            part = lax.dot_general(
                natural, weights[place, :, :slots], (((1,), (1,)), ((), ())), preferred_element_type=F32
            )
            part_ref[:, spot : spot + width] = part.astype(BF16)


def feed(h_ref, gi_ref, own_ref, other_ref, inner_ref, pair_ref, part_ref, w_ref, sems):
    units = gi_ref.shape[1]
    depth = own_ref.shape[0]
    groups = feed_groups(units)
    copies = []
    for group, (begin, end) in enumerate(groups):
        mine = []
        for core, ref in enumerate((own_ref, other_ref)):
            for start in (0, units):
                columns = pl.ds(start + begin, end - begin)
                copy = pltpu.make_async_copy(
                    ref.at[:, columns],
                    w_ref.at[pl.ds(core * depth, depth), columns],
                    sems.at[group, len(mine)],
                )
                copy.start()
                mine.append(copy)
        copies.append(mine)
    for (begin, end), mine in zip(groups, copies):
        for copy in mine:
            copy.wait()
        gate = jnp.dot(h_ref[...], w_ref[:, begin:end], preferred_element_type=F32)
        up = jnp.dot(h_ref[...], w_ref[:, units + begin : units + end], preferred_element_type=F32)
        grad_inner = gi_ref[:, begin:end]
        sig = 1.0 / (1.0 + jnp.exp(-gate))
        act = gate * sig
        inner_ref[:, begin:end] = (act * up).astype(BF16)
        grad_gate = grad_inner * up * (sig * (1.0 + gate * (1.0 - sig)))
        pair_ref[:, begin:end] = grad_gate.astype(BF16)
        pair_ref[:, units + begin : units + end] = (grad_inner * act).astype(BF16)
    for begin in range(0, 2 * depth, 512):
        part = lax.dot_general(
            pair_ref[...], w_ref[begin : begin + 512, :], (((1,), (1,)), ((), ())),
            preferred_element_type=F32,
        )
        part_ref[:, begin : begin + 512] = part.astype(BF16)


def feed_groups(units):
    ends = [128, 384] + list(range(896, units, 512)) + [units]
    return list(zip([0] + ends[:-1], ends))


def spread_heads(row_ref, w_ref, b0, b1, b2, b3, out_ref):
    size = b0.shape[0]
    for j, part in enumerate((b0, b1, b2, b3)):
        spot = pl.multiple_of((row_ref[0] ^ j) * size, size)
        piece = lax.dot_general(
            w_ref[...], part[...], (((1,), (1,)), ((), ())), preferred_element_type=F32
        )
        out_ref[:, pl.ds(spot, size)] = piece.astype(BF16)


def kernel_call(body, out_shape, operands, flops, scratch=(), scalars=0, outside=(), staged=(), mib=48):
    moved = sum(x.size * x.dtype.itemsize for x in operands)
    count = len(operands)
    spaces = [
        pltpu.SMEM if i < scalars else pl.ANY if i in outside or i in staged else pltpu.VMEM
        for i in range(count)
    ]
    if staged:
        held = [pltpu.VMEM(operands[i].shape, operands[i].dtype) for i in staged]
        scratch = [*scratch, *held, pltpu.SemaphoreType.DMA((len(staged),))]

        def whole(*refs):
            refs, buffers, sems = list(refs[: -len(staged) - 1]), refs[-len(staged) - 1 : -1], refs[-1]
            copies = [
                pltpu.make_async_copy(refs[i], buffer, sems.at[n])
                for n, (i, buffer) in enumerate(zip(staged, buffers))
            ]
            for copy in copies:
                copy.start()
            for copy in copies:
                copy.wait()
            for i, buffer in zip(staged, buffers):
                refs[i] = buffer
            body(*refs)
    else:
        whole = body
    out_specs = jax.tree.map(lambda _: pl.BlockSpec(memory_space=pltpu.VMEM), out_shape)
    return pl.pallas_call(
        whole,
        out_shape=out_shape,
        in_specs=[pl.BlockSpec(memory_space=space) for space in spaces],
        out_specs=out_specs,
        scratch_shapes=list(scratch),
        compiler_params=pltpu.CompilerParams(vmem_limit_bytes=mib * 1024 * 1024),
        cost_estimate=pl.CostEstimate(flops=flops, bytes_accessed=moved, transcendentals=0),
    )(*operands)


def rows_call(body, kinds, operands, steps=2):
    rows, width = operands[0].shape
    block = pl.BlockSpec((rows // steps, width), lambda i: (i, 0))
    out_shape = tuple(jax.ShapeDtypeStruct((rows, width), kind) for kind in kinds)
    moved = sum(x.size * x.dtype.itemsize for x in operands)
    return pl.pallas_call(
        body,
        out_shape=out_shape,
        grid=(steps,),
        in_specs=[block] * len(operands),
        out_specs=(block,) * len(kinds),
        cost_estimate=pl.CostEstimate(flops=0, bytes_accessed=moved, transcendentals=0),
    )(*operands)


def on_device(
    tokens_in, segment_ids, attn_gain, w_qkv, w_out, mlp_gain, w_gate, w_up, w_down, cotangent
):
    group = segment_ids.shape[0]
    span = group // 4
    size = span // 4
    units = w_gate.shape[1]
    slots = w_qkv.shape[2] // HD
    heads = slots - 2
    deep, high, row = lax.axis_index("z"), lax.axis_index("xh"), lax.axis_index("y")
    low, core = lax.axis_index("xl"), lax.axis_index("k")
    col = low * 2 + core

    indices = jnp.arange(group, dtype=jnp.int32)
    previous = jnp.concatenate([segment_ids[:1] - 1, segment_ids[:-1]])
    starts = lax.cummax(jnp.where(segment_ids != previous, indices, 0), axis=0)
    bases = [j * span + col * size for j in range(4)]
    my_starts = jnp.concatenate([lax.dynamic_slice_in_dim(starts, b, size, 0) for b in bases])
    lanes = jnp.arange(size, dtype=jnp.int32)
    my_index = jnp.concatenate([lanes + b for b in bases])
    half_dim = HD // 2
    inverse_freq = rope_base ** (-jnp.arange(half_dim, dtype=F32) * 2.0 / HD)
    angles = inverse_freq[:, None] * (my_index - my_starts).astype(F32)[None, :]
    cosine, sine = jnp.cos(angles), jnp.sin(angles)
    key_offset = jnp.concatenate([lanes + (col ^ m) * size for m in range(4)])
    key_offset = jnp.broadcast_to(key_offset[:, None], (span, size))
    qpos, qstart = my_index[None, :], my_starts[None, :]
    cut_at = slots * HD

    flat_qkv = w_qkv.reshape(w_qkv.shape[0], -1)
    qkv_out = jnp.concatenate([(flat_qkv * attn_gain[:, None]).astype(BF16), w_out], axis=1)
    (inputs,), alongside = to_full_width(
        [tokens_in], col, cosine, sine, key_offset, qpos, qstart, *cut(qkv_out, 2, 0)
    )
    cosine, sine, key_offset, qpos, qstart, qkv_out_first, qkv_out_second = alongside
    inputs = inputs.astype(F32)
    normed_one = (inputs * scale_of(inputs)).astype(BF16)
    rows_one = gather_row(normed_one)

    qkv_out_halves = [qkv_out_first, qkv_out_second]
    mine = ring_join(qkv_out_halves, lax.optimization_barrier(ring_send(qkv_out_halves)), low, 0)
    mine = mine.reshape(2, *qkv_out.shape)
    theirs = trade_core(mine)
    (cot_rows,), _ = to_full_width([after(cotangent, mine)], col)
    scaled = lambda v: (v * mlp_gain[:, None]).astype(BF16)
    gate_up = jnp.concatenate([scaled(w_gate), scaled(w_up)], axis=1)
    gu_halves = [after(v, normed_one) for v in cut(gate_up, 2, 0)]
    full_out = jnp.concatenate(
        [mine[0, :, cut_at:], mine[1, :, cut_at:], theirs[0, :, cut_at:], theirs[1, :, cut_at:]],
        axis=1,
    )
    rows_one, gu_halves, full_out, cot_rows = lax.optimization_barrier(
        (rows_one, gu_halves, full_out, cot_rows)
    )

    shape = lambda kind, *dims: jax.ShapeDtypeStruct(dims, kind)
    scratch = lambda kind, *dims: pltpu.VMEM(dims, kind)
    width = inputs.shape[1]
    matmul = lambda rows, depth, columns: 2 * rows * depth * columns
    query, pairs = kernel_call(
        project,
        (shape(BF16, heads * HD, span), shape(BF16, 2 * HD, span)),
        (rows_one, mine, theirs, cosine, sine),
        matmul(span, width, cut_at),
        staged=(0,),
    )
    grad_rows = gather_row(after(cot_rows, query))
    all_pairs = jnp.stack([pairs] + [trade_col(pairs, m) for m in (1, 2, 3)])
    gu_halves = [after(v, all_pairs) for v in gu_halves]
    gu_got = ring_send(gu_halves)

    flops = 2 * matmul(heads * span, HD, group)
    keys_shape = (4, HD, span), (4, span, HD)
    mixed, mixed_low, lse = kernel_call(
        attend,
        (shape(F32, heads * HD, span), shape(BF16, heads * HD, span), shape(F32, heads, span)),
        (query, all_pairs, key_offset, qpos, qstart),
        flops,
        scratch=[scratch(BF16, *keys_shape[i]) for i in (0, 0, 1, 1)],
    )
    mixed_low, grad_rows = lax.optimization_barrier((mixed_low, grad_rows))
    branch = product(mixed_low, full_out, ((0,), (0,)), BF16)
    gu_mine = ring_join(gu_halves, after(gu_got, branch), low, 0)
    down_halves = [after(v, branch, gu_got) for v in cut(w_down, 2, 0)]
    down_got = ring_send(down_halves)
    branch_parts = after(collect_row(row_parts(branch, row)), gu_mine, down_got)
    hidden, normed_two = rows_call(add_and_norm, (F32, BF16), (inputs, *branch_parts))
    down_mine = ring_join(down_halves, after(down_got, hidden), low, 1)
    full_down = jnp.concatenate([down_mine, trade_core(down_mine)], axis=1)
    grad_inner = product(grad_rows, full_down, ((1,), (1,)))
    gu_theirs = trade_core(after(gu_mine, hidden))
    rows_two = gather_row(normed_two)

    side = lambda v, which: v[:, which * width // 2 : (which + 1) * width // 2]
    both_cores = lambda v, axis=0: jnp.concatenate([v, trade_core(v)], axis=axis)
    half_of = lambda v: jnp.concatenate([side(v, 0), trade_core(side(v, 1))])

    def half_by_ring(v):
        blocks = [cut(v, 8, 1)[i] for i in (0, 2, 1, 3, 4, 6, 5, 7)]
        sides = [jnp.concatenate(blocks[:4], axis=1), jnp.concatenate(blocks[4:], axis=1)]
        return jnp.concatenate([sides[0], trade_core(sides[1])])

    token_sum = lambda a, b: product(a, b, ((0,), (0,)), BF16)
    cot_half, heads_both = half_by_ring(after(grad_rows, hidden)), both_cores(after(mixed_low, hidden), 1)
    one_half = half_of(after(rows_one, hidden))
    rows_two, cot_half, heads_both, one_half = lax.optimization_barrier(
        (rows_two, cot_half, heads_both, one_half)
    )
    two_half = half_by_ring(rows_two)
    inner, grad_pair, part_two = kernel_call(
        feed,
        (shape(BF16, span, units), shape(BF16, span, 2 * units), shape(BF16, span, width)),
        (rows_two, grad_inner, gu_mine, gu_theirs),
        2 * matmul(span, width, 2 * units),
        scratch=(scratch(BF16, width, 2 * units), pltpu.SemaphoreType.DMA((len(feed_groups(units)), 4))),
        outside=(2, 3),
    )
    inner_both = both_cores(inner)
    pair_both = both_cores(grad_pair)
    mlp_sums = jnp.concatenate([token_sum(two_half, pair_both), token_sum(cot_half, inner_both)], axis=1)
    grad_n2, mlp_sums = lax.optimization_barrier((sum_row(part_two), mlp_sums))
    mlp_sums = lax.psum_scatter(mlp_sums, ("xh", "xl", "z"), scatter_dimension=0, tiled=True)
    grad_hidden, grad_low = rows_call(norm_back_low, (F32, BF16), (hidden, grad_n2, cot_rows))
    branch_parts = spread_row(grad_low)
    result_parts = row_parts(product(inner, full_down, ((1,), (0,)), BF16), row)
    branch_parts, result_parts = lax.optimization_barrier((branch_parts, result_parts))
    grad_heads = kernel_call(
        spread_heads,
        shape(BF16, heads * HD, span),
        (row.astype(jnp.int32)[None], full_out, *branch_parts),
        matmul(span, width, heads * HD),
        scalars=1,
    )
    pair_shape = shape(BF16, 2 * HD, span)
    known = (query, all_pairs, key_offset, qpos, qstart, mixed, lse, grad_heads, cosine, sine)
    half_heads = shape(BF16, heads * HD // 2, span)
    keys_scratch = [scratch(BF16, *keys_shape[i]) for i in (0, 1, 1)]
    key_sums = (shape(F32, *keys_shape[0]),) * 2
    split = functools.partial(attend_back, count=heads // 2)
    result_near = trade_near(result_parts, trade_row)
    gq_first, *key_grads = kernel_call(
        functools.partial(split, first=0, last_call=False),
        (half_heads,) + key_sums,
        known,
        flops * 5 // 4,
        scratch=keys_scratch,
        staged=(1,),
    )
    key_grads, result_near = lax.optimization_barrier((key_grads, result_near))
    result_far = trade_row(after(result_parts[2], result_near), 2)
    gq_last, *grad_pairs = kernel_call(
        functools.partial(split, first=heads // 2, last_call=True),
        (half_heads,) + (pair_shape,) * 4,
        (*known, *key_grads),
        flops * 5 // 4,
        scratch=keys_scratch + [scratch(F32, *keys_shape[0])] * 2,
        staged=(1,),
    )
    grad_pairs = [grad_pairs[0]] + [trade_col(grad_pairs[m], m) for m in (1, 2, 3)]
    grad_pairs = lax.optimization_barrier(grad_pairs)
    grad_qkv, part_one = kernel_call(
        project_back,
        (shape(BF16, cut_at, span), shape(BF16, span, width)),
        (gq_first, gq_last, *grad_pairs, cosine, sine, mine, theirs),
        matmul(span, width, cut_at),
    )
    qkv_both = both_cores(grad_qkv, 1)
    branch_rows = jnp.concatenate(in_order(after(branch_parts, grad_qkv), row))
    branch_half = half_of(branch_rows)
    qkv_sum = product(one_half, qkv_both, ((0,), (1,)), BF16).reshape(2, width // 4, -1)
    out_sum = product(branch_half, heads_both, ((0,), (1,)), BF16).reshape(2, width // 4, -1)
    both_parts = deep_parts(jnp.concatenate([qkv_sum, out_sum], axis=2), deep)
    both_sums = exchange(both_parts, trade_deep)
    rows_here = mlp_sums.shape[0]
    rows_here = mlp_sums.shape[0]
    own_rows = lambda w: lax.dynamic_slice_in_dim(w, (high * 4 + deep) * rows_here, rows_here, 0)
    own_gain = jnp.sum(own_rows(w_gate) * mlp_sums[:, :units].astype(F32), axis=1, keepdims=True)
    own_gain += jnp.sum(own_rows(w_up) * mlp_sums[:, units : 2 * units].astype(F32), axis=1, keepdims=True)
    own_gain = jnp.broadcast_to(own_gain, (rows_here, 128))
    own_gain = own_gain + trade_row(own_gain, 1)
    own_gain = (own_gain + trade_row(own_gain, 2)).astype(BF16)
    mlp_sums = jnp.concatenate([mlp_sums, own_gain], axis=1)
    mlp_sums, both_sums = lax.optimization_barrier((mlp_sums, both_sums))
    mlp_total = ring_gather(mlp_sums, high)
    both_total = exchange(ring_parts([both_sums], low, high), trade_ring)
    mlp_total, both_total = lax.optimization_barrier((mlp_total, both_total))
    mlp_total = lax.all_gather(mlp_total, "z", axis=0, tiled=True)
    both_total = ring_gather(both_total, high)
    grad_n1 = sum_row(part_one)
    (grad_in,) = rows_call(norm_back_high, (F32,), (inputs, grad_n1, grad_hidden))
    both_total, grad_in, result_far = lax.optimization_barrier((both_total, to_blocks(grad_in, col), result_far))
    both_total = deep_gather(both_total, deep).astype(F32)
    result = (hidden + result_parts[0].astype(F32)) + result_far.astype(F32)
    result = (result + sum(part.astype(F32) for part in result_near)).astype(BF16)
    result = to_blocks(result, col)
    both_total, result = lax.optimization_barrier((both_total, result))
    qkv_total, out_total = both_total[:, :cut_at], both_total[:, cut_at:]
    qkv_gain = jnp.sum(flat_qkv * qkv_total, axis=1)[None]
    qkv_gain = sum([trade_row(qkv_gain, j) for j in (1, 2, 3)], qkv_gain)[0]
    mlp_total = mlp_total.reshape(4, 2, rows_here, -1).swapaxes(0, 1).reshape(mlp_total.shape)
    piece = lambda first: mlp_total[:, first : first + units].astype(F32)
    return (
        result,
        grad_in,
        qkv_gain,
        (qkv_total * attn_gain[:, None]).reshape(w_qkv.shape),
        out_total.T,
        mlp_total[:, 3 * units].astype(F32),
        piece(0) * mlp_gain[:, None],
        piece(units) * mlp_gain[:, None],
        piece(2 * units).T,
    )


def solution(mesh):
    dp, rows, cols = mesh.devices.shape
    fine = Mesh(
        mesh.devices.reshape(dp // 2, 2, rows, cols // 2, 2), ("z", "xh", "y", "xl", "k")
    )
    tokens = P(("z", "xh", "y"), COL)
    in_specs = (
        tokens, P(("z", "xh")), P(COL), P(COL, "y", None), P("y", COL), P(COL),
        P(COL, "y"), P(COL, "y"), P("y", COL), tokens,
    )
    out_specs = (
        tokens, tokens, P(COL), P(COL, "y", None), P("y", COL), P(COL),
        P(COL, "y"), P(COL, "y"), P("y", COL),
    )
    return jax.shard_map(
        on_device, mesh=fine, in_specs=in_specs, out_specs=out_specs, check_vma=False
    )
```

```python
import functools

import jax
import jax.numpy as jnp
from jax import lax
from jax.experimental import pallas as pl
from jax.experimental.pallas import tpu as pltpu
from jax.sharding import Mesh
from jax.sharding import PartitionSpec as P

HD = 64
norm_eps = 1e-05
rope_base = 10000.0
masked = -1e30

COL = ("xl", "k")
RING = ("xh", "xl")
BF16 = jnp.bfloat16
F32 = jnp.float32


def trade(values, axes, mask, size=4):
    return lax.ppermute(values, axes, [(i, i ^ mask) for i in range(size)])


def trade_row(values, mask):
    return trade(values, "y", mask)


def trade_col(values, mask):
    return trade(values, COL, mask)


def trade_core(values):
    return trade(values, "k", 1, 2)


def trade_ring(values, mask):
    return trade(values, RING, mask)


def trade_deep(values, mask):
    return trade(values, "z", mask)


def after(values, *earlier):
    return lax.optimization_barrier((values, earlier))[0]


def pick(bit, zero, one):
    return jnp.where(bit == 0, zero, one)


def in_order(parts, index):
    low, high = index % 2, index // 2
    a, b, c, d = parts
    a, b = pick(low, a, b), pick(low, b, a)
    c, d = pick(low, c, d), pick(low, d, c)
    return [pick(high, a, c), pick(high, b, d), pick(high, c, a), pick(high, d, b)]


def cut(values, count, axis):
    return jnp.split(values, count, axis)


def gather_row(values):
    return lax.all_gather(values, "y", axis=0, tiled=True)


def sum_row(partial):
    return lax.psum_scatter(partial, "y", scatter_dimension=0, tiled=True)


def spread_row(values):
    return [values] + [trade_row(values, j) for j in (1, 2, 3)]


def row_parts(partial, row):
    size = partial.shape[0] // 4
    return [lax.dynamic_slice_in_dim(partial, (row ^ j) * size, size, 0) for j in range(4)]


def collect_row(parts):
    return [parts[0]] + [trade_row(parts[j], j) for j in (1, 2, 3)]


def by_width(parts, low):
    return [
        pick(low, parts[core + 2 * place], parts[core + 2 * (1 - place)])
        for core in range(2)
        for place in range(2)
    ]


def of_width(values, low):
    blocks = cut(values, 4, 1)
    return [
        pick(low, blocks[2 * core + place], blocks[2 * core + 1 - place])
        for place in range(2)
        for core in range(2)
    ]


def to_full_width(values, col, *alongside):
    size = values[0].shape[0] // 4
    send = lambda m: jnp.concatenate(
        [lax.dynamic_slice_in_dim(v, (col ^ m) * size, size, 0) for v in values], axis=1
    )
    parts = [send(0)] + [trade_col(send(m), m) for m in (1, 2, 3)]
    parts, alongside = lax.optimization_barrier((parts, alongside))
    parts = [cut(part, len(values), 1) for part in parts]
    rows = [
        jnp.concatenate(by_width([part[i] for part in parts], col // 2), axis=1)
        for i in range(len(values))
    ]
    return rows, alongside


def to_blocks(values, col):
    parts = of_width(values, col // 2)
    kind = values.dtype
    parts = [parts[0]] + [trade_col(parts[m].astype(BF16), m).astype(kind) for m in (1, 2, 3)]
    return jnp.concatenate(in_order(parts, col), axis=0)


def ring_send(halves):
    return [trade_ring(halves[0], 1), trade_ring(halves[1], 3)]


def ring_join(halves, got, low, axis):
    shard, other = jnp.concatenate(halves), jnp.concatenate(got)
    return jnp.concatenate([pick(low, shard, other), pick(low, other, shard)], axis=axis)


def add_low(*terms):
    total = terms[0].astype(F32)
    for term in terms[1:]:
        total = total + term.astype(F32)
    return total.astype(BF16)


def at(values, index):
    return lax.dynamic_index_in_dim(values, index, 0, keepdims=False)


def ring_parts(blocks, low, high):
    half = blocks[0].shape[1] // 2
    take = lambda place, which: jnp.concatenate(
        [
            lax.dynamic_slice(v, (place, which * half, 0), (1, half, v.shape[2]))[0]
            for v in blocks
        ],
        axis=1,
    )
    return [take(low, high), take(1 - low, high), take(low, 1 - high), take(1 - low, 1 - high)]


def deep_parts(blocks, deep):
    size = blocks.shape[-2] // 4
    return [
        lax.dynamic_slice_in_dim(blocks, (deep ^ j) * size, size, blocks.ndim - 2) for j in range(4)
    ]


def trade_near(parts, trader):
    return [trader(parts[1], 1), trader(parts[3], 3)]


def exchange(parts, trader):
    return add_low(parts[0], *lax.optimization_barrier([trader(parts[j], j) for j in (1, 2, 3)]))


def ring_gather(values, high):
    other = trade_ring(values, 2)
    return jnp.concatenate([pick(high, values, other), pick(high, other, values)], axis=0)


def deep_gather(values, deep):
    parts = lax.optimization_barrier([values] + [trade_deep(values, j) for j in (1, 2, 3)])
    return jnp.concatenate(in_order(parts, deep), axis=0)


def product(left, right, dims, kind=F32):
    return lax.dot_general(left, right, (dims, ((), ())), preferred_element_type=F32).astype(kind)


def scale_of(values):
    return lax.rsqrt(jnp.mean(values * values, axis=1, keepdims=True) + norm_eps)


def add_and_norm(base_ref, p0, p1, p2, p3, hidden_ref, normed_ref):
    hidden = (p0[...].astype(F32) + p1[...].astype(F32)) + (p2[...].astype(F32) + p3[...].astype(F32))
    hidden = base_ref[...] + hidden
    hidden_ref[...] = hidden
    normed_ref[...] = (hidden * scale_of(hidden)).astype(BF16)


def norm_back(values, weighted, passed):
    scale = scale_of(values)
    inner = jnp.mean(weighted * values, axis=1, keepdims=True)
    return passed + (scale * weighted - values * (scale**3 * inner))


def norm_back_low(values_ref, part_ref, passed_ref, grad_ref, low_ref):
    grad = norm_back(values_ref[...], part_ref[...].astype(F32), passed_ref[...].astype(F32))
    grad_ref[...] = grad
    low_ref[...] = grad.astype(BF16)


def norm_back_high(values_ref, part_ref, passed_ref, grad_ref):
    grad_ref[...] = norm_back(values_ref[...], part_ref[...].astype(F32), passed_ref[...])


def turn(first, second, cosine, sine):
    return first * cosine - second * sine, second * cosine + first * sine


def project(x_ref, mine_ref, theirs_ref, cos_ref, sin_ref, q_ref, kv_ref):
    width = mine_ref.shape[1]
    slots = kv_ref.shape[0] + q_ref.shape[0]
    total = None
    for core, weights in enumerate((mine_ref, theirs_ref)):
        for place in range(2):
            spot = (2 * core + place) * width
            term = jnp.dot(
                x_ref[:, spot : spot + width], weights[place, :, :slots], preferred_element_type=F32
            )
            total = term if total is None else total + term
    turned = total.T
    cosine, sine = cos_ref[...], sin_ref[...]
    half = HD // 2
    heads = q_ref.shape[0] // HD
    for head in range(heads + 1):
        spot = head * HD
        first, second = turn(
            turned[spot : spot + half], turned[spot + half : spot + HD], cosine, sine
        )
        if head < heads:
            q_ref[spot : spot + half, :] = (first * HD**-0.5).astype(BF16)
            q_ref[spot + half : spot + HD, :] = (second * HD**-0.5).astype(BF16)
        else:
            kv_ref[:half, :] = first.astype(BF16)
            kv_ref[half:HD, :] = second.astype(BF16)
    kv_ref[HD:, :] = turned[(heads + 1) * HD :].astype(BF16)


def lay_keys(pairs, kt_ref, vt_ref, kn_ref, vn_ref):
    size = pairs.shape[2] // 4
    for block in range(4):
        for m in range(4):
            piece = pairs[m, :, block * size : (block + 1) * size]
            spot = slice(m * size, (m + 1) * size)
            kt_ref[block, :, spot] = piece[:HD]
            if vt_ref is not None:
                vt_ref[block, :, spot] = piece[HD:]
            natural = piece.astype(F32).T.astype(BF16)
            kn_ref[block, spot, :] = natural[:, :HD]
            vn_ref[block, spot, :] = natural[:, HD:]


def side_by_side(ref, first, count, depth, spot, size):
    return jnp.concatenate(
        [ref[head * depth : (head + 1) * depth, spot : spot + size] for head in range(first, first + count)],
        axis=1,
    )


def admitted(koff_ref, start, qpos, qstart, diagonal, count):
    keys = koff_ref[...] + start
    allowed = keys >= qstart
    if diagonal:
        allowed = allowed & (keys <= qpos)
    return jnp.concatenate([allowed] * count, axis=1)


def attend(
    q_ref, pairs_ref, koff_ref, qpos_ref, qstart_ref, o_ref, low_ref, lse_ref, kt_ref, vt_ref, kn_ref, vn_ref
):
    span = kn_ref.shape[1]
    size = span // 4
    heads = q_ref.shape[0] // HD
    lay_keys(pairs_ref, kt_ref, vt_ref, kn_ref, vn_ref)
    for block in range(4):
        spot = block * size
        qpos, qstart = qpos_ref[:, spot : spot + size], qstart_ref[:, spot : spot + size]
        query = side_by_side(q_ref, 0, heads, HD, spot, size)
        top = jnp.full((1, heads * size), masked, F32)
        total = jnp.zeros((1, heads * size), F32)
        accum = jnp.zeros((HD, heads * size), F32)
        for number in (block, *range(block)):
            scores = jnp.dot(kn_ref[number], query, preferred_element_type=F32)
            allowed = admitted(koff_ref, number * span, qpos, qstart, number == block, heads)
            scores = jnp.where(allowed, scores, masked)
            new_top = jnp.maximum(top, jnp.max(scores, axis=0, keepdims=True))
            weights = jnp.exp(scores - new_top)
            shrink = jnp.exp(top - new_top)
            total = total * shrink + jnp.sum(weights, axis=0, keepdims=True)
            accum = accum * shrink + jnp.dot(
                vt_ref[number], weights.astype(BF16), preferred_element_type=F32
            )
            top = new_top
        result = accum / total
        lse = top + jnp.log(total)
        for head in range(heads):
            piece = result[:, head * size : (head + 1) * size]
            rows = slice(head * HD, (head + 1) * HD)
            o_ref[rows, spot : spot + size] = piece
            low_ref[rows, spot : spot + size] = piece.astype(BF16)
            lse_ref[head : head + 1, spot : spot + size] = lse[:, head * size : (head + 1) * size]


def attend_back(
    q_ref, pairs_ref, koff_ref, qpos_ref, qstart_ref, o_ref, lse_ref, go_ref, cos_ref, sin_ref, *refs,
    first, count, last_call,
):
    if last_call:
        gk_in, gv_in, gq_ref, g0, g1, g2, g3, kt_ref, kn_ref, vn_ref, gk_ref, gv_ref = refs
    else:
        gq_ref, gk_ref, gv_ref, kt_ref, kn_ref, vn_ref = refs
    span = kn_ref.shape[1]
    size = span // 4
    lay_keys(pairs_ref, kt_ref, None, kn_ref, vn_ref)
    gk_ref[...] = gk_in[...] if last_call else jnp.zeros_like(gk_ref)
    gv_ref[...] = gv_in[...] if last_call else jnp.zeros_like(gv_ref)
    last = (((1,), (1,)), ((), ()))
    for block in range(4):
        spot = block * size
        here = slice(spot, spot + size)
        qpos, qstart = qpos_ref[:, here], qstart_ref[:, here]
        cosine, sine = cos_ref[:, here], sin_ref[:, here]
        pick_heads = lambda ref, depth: side_by_side(ref, first, count, depth, spot, size)
        query, grad_out = pick_heads(q_ref, HD), pick_heads(go_ref, HD)
        lse = pick_heads(lse_ref, 1)
        delta = jnp.sum(grad_out.astype(F32) * pick_heads(o_ref, HD), axis=0, keepdims=True)
        grad_query = jnp.zeros((HD, count * size), F32)
        for number in (block, *range(block)):
            scores = jnp.dot(kn_ref[number], query, preferred_element_type=F32)
            allowed = admitted(koff_ref, number * span, qpos, qstart, number == block, count)
            probs = jnp.exp(jnp.where(allowed, scores - lse, masked))
            grad_probs = jnp.dot(vn_ref[number], grad_out, preferred_element_type=F32)
            grad_scores = (probs * (grad_probs - delta)).astype(BF16)
            gv_ref[number] += lax.dot_general(
                grad_out, probs.astype(BF16), last, preferred_element_type=F32
            )
            gk_ref[number] += lax.dot_general(query, grad_scores, last, preferred_element_type=F32)
            grad_query = grad_query + jnp.dot(
                kt_ref[number], grad_scores, preferred_element_type=F32
            )
        half = HD // 2
        for head in range(count):
            grad = grad_query[:, head * size : (head + 1) * size] * HD**-0.5
            upper, lower = turn(grad[:half], grad[half:], cosine, -sine)
            gq_ref[head * HD : head * HD + half, here] = upper.astype(BF16)
            gq_ref[head * HD + half : (head + 1) * HD, here] = lower.astype(BF16)
    if last_call:
        for block in range(4):
            for m, ref in enumerate((g0, g1, g2, g3)):
                spot, out = slice(m * size, (m + 1) * size), slice(block * size, (block + 1) * size)
                ref[:HD, out] = gk_ref[block, :, spot].astype(BF16)
                ref[HD:, out] = gv_ref[block, :, spot].astype(BF16)


def project_back(
    gq0, gq1, g0, g1, g2, g3, cos_ref, sin_ref, mine_ref, theirs_ref, gqkv_ref, part_ref
):
    pair = g0[...].astype(F32) + g1[...].astype(F32) + (g2[...].astype(F32) + g3[...].astype(F32))
    half = HD // 2
    first, second = turn(pair[:half], pair[half:HD], cos_ref[...], -sin_ref[...])
    turned = jnp.concatenate(
        [gq0[...].astype(F32), gq1[...].astype(F32), first, second, pair[HD:]], axis=0
    )
    gqkv_ref[...] = turned.astype(BF16)
    natural = turned.T.astype(BF16)
    width = mine_ref.shape[1]
    slots = turned.shape[0]
    for core, weights in enumerate((mine_ref, theirs_ref)):
        for place in range(2):
            spot = (2 * core + place) * width
            part = lax.dot_general(
                natural, weights[place, :, :slots], (((1,), (1,)), ((), ())), preferred_element_type=F32
            )
            part_ref[:, spot : spot + width] = part.astype(BF16)


def feed(h_ref, gi_ref, own_ref, other_ref, inner_ref, pair_ref, part_ref, w_ref, sems):
    units = gi_ref.shape[1]
    depth = own_ref.shape[0]
    groups = feed_groups(units)
    copies = []
    for group, (begin, end) in enumerate(groups):
        mine = []
        for core, ref in enumerate((own_ref, other_ref)):
            for start in (0, units):
                columns = pl.ds(start + begin, end - begin)
                copy = pltpu.make_async_copy(
                    ref.at[:, columns],
                    w_ref.at[pl.ds(core * depth, depth), columns],
                    sems.at[group, len(mine)],
                )
                copy.start()
                mine.append(copy)
        copies.append(mine)
    for (begin, end), mine in zip(groups, copies):
        for copy in mine:
            copy.wait()
        gate = jnp.dot(h_ref[...], w_ref[:, begin:end], preferred_element_type=F32)
        up = jnp.dot(h_ref[...], w_ref[:, units + begin : units + end], preferred_element_type=F32)
        grad_inner = gi_ref[:, begin:end]
        sig = 1.0 / (1.0 + jnp.exp(-gate))
        act = gate * sig
        inner_ref[:, begin:end] = (act * up).astype(BF16)
        grad_gate = grad_inner * up * (sig * (1.0 + gate * (1.0 - sig)))
        pair_ref[:, begin:end] = grad_gate.astype(BF16)
        pair_ref[:, units + begin : units + end] = (grad_inner * act).astype(BF16)
    for begin in range(0, 2 * depth, 512):
        part = lax.dot_general(
            pair_ref[...], w_ref[begin : begin + 512, :], (((1,), (1,)), ((), ())),
            preferred_element_type=F32,
        )
        part_ref[:, begin : begin + 512] = part.astype(BF16)


def feed_groups(units):
    ends = [128, 384] + list(range(896, units, 512)) + [units]
    return list(zip([0] + ends[:-1], ends))


def spread_heads(row_ref, w_ref, b0, b1, b2, b3, out_ref):
    size = b0.shape[0]
    for j, part in enumerate((b0, b1, b2, b3)):
        spot = pl.multiple_of((row_ref[0] ^ j) * size, size)
        piece = lax.dot_general(
            w_ref[...], part[...], (((1,), (1,)), ((), ())), preferred_element_type=F32
        )
        out_ref[:, pl.ds(spot, size)] = piece.astype(BF16)


def kernel_call(body, out_shape, operands, flops, scratch=(), scalars=0, outside=(), staged=(), mib=48):
    moved = sum(x.size * x.dtype.itemsize for x in operands)
    count = len(operands)
    spaces = [
        pltpu.SMEM if i < scalars else pl.ANY if i in outside or i in staged else pltpu.VMEM
        for i in range(count)
    ]
    if staged:
        held = [pltpu.VMEM(operands[i].shape, operands[i].dtype) for i in staged]
        scratch = [*scratch, *held, pltpu.SemaphoreType.DMA((len(staged),))]

        def whole(*refs):
            refs, buffers, sems = list(refs[: -len(staged) - 1]), refs[-len(staged) - 1 : -1], refs[-1]
            copies = [
                pltpu.make_async_copy(refs[i], buffer, sems.at[n])
                for n, (i, buffer) in enumerate(zip(staged, buffers))
            ]
            for copy in copies:
                copy.start()
            for copy in copies:
                copy.wait()
            for i, buffer in zip(staged, buffers):
                refs[i] = buffer
            body(*refs)
    else:
        whole = body
    out_specs = jax.tree.map(lambda _: pl.BlockSpec(memory_space=pltpu.VMEM), out_shape)
    return pl.pallas_call(
        whole,
        out_shape=out_shape,
        in_specs=[pl.BlockSpec(memory_space=space) for space in spaces],
        out_specs=out_specs,
        scratch_shapes=list(scratch),
        compiler_params=pltpu.CompilerParams(vmem_limit_bytes=mib * 1024 * 1024),
        cost_estimate=pl.CostEstimate(flops=flops, bytes_accessed=moved, transcendentals=0),
    )(*operands)


def rows_call(body, kinds, operands, steps=2):
    rows, width = operands[0].shape
    block = pl.BlockSpec((rows // steps, width), lambda i: (i, 0))
    out_shape = tuple(jax.ShapeDtypeStruct((rows, width), kind) for kind in kinds)
    moved = sum(x.size * x.dtype.itemsize for x in operands)
    return pl.pallas_call(
        body,
        out_shape=out_shape,
        grid=(steps,),
        in_specs=[block] * len(operands),
        out_specs=(block,) * len(kinds),
        cost_estimate=pl.CostEstimate(flops=0, bytes_accessed=moved, transcendentals=0),
    )(*operands)


def on_device(
    tokens_in, segment_ids, attn_gain, w_qkv, w_out, mlp_gain, w_gate, w_up, w_down, cotangent
):
    group = segment_ids.shape[0]
    span = group // 4
    size = span // 4
    units = w_gate.shape[1]
    slots = w_qkv.shape[2] // HD
    heads = slots - 2
    deep, high, row = lax.axis_index("z"), lax.axis_index("xh"), lax.axis_index("y")
    low, core = lax.axis_index("xl"), lax.axis_index("k")
    col = low * 2 + core

    indices = jnp.arange(group, dtype=jnp.int32)
    previous = jnp.concatenate([segment_ids[:1] - 1, segment_ids[:-1]])
    starts = lax.cummax(jnp.where(segment_ids != previous, indices, 0), axis=0)
    bases = [j * span + col * size for j in range(4)]
    my_starts = jnp.concatenate([lax.dynamic_slice_in_dim(starts, b, size, 0) for b in bases])
    lanes = jnp.arange(size, dtype=jnp.int32)
    my_index = jnp.concatenate([lanes + b for b in bases])
    half_dim = HD // 2
    inverse_freq = rope_base ** (-jnp.arange(half_dim, dtype=F32) * 2.0 / HD)
    angles = inverse_freq[:, None] * (my_index - my_starts).astype(F32)[None, :]
    cosine, sine = jnp.cos(angles), jnp.sin(angles)
    key_offset = jnp.concatenate([lanes + (col ^ m) * size for m in range(4)])
    key_offset = jnp.broadcast_to(key_offset[:, None], (span, size))
    qpos, qstart = my_index[None, :], my_starts[None, :]
    cut_at = slots * HD

    flat_qkv = w_qkv.reshape(w_qkv.shape[0], -1)
    qkv_out = jnp.concatenate([(flat_qkv * attn_gain[:, None]).astype(BF16), w_out], axis=1)
    (inputs,), alongside = to_full_width(
        [tokens_in], col, cosine, sine, key_offset, qpos, qstart, *cut(qkv_out, 2, 0)
    )
    cosine, sine, key_offset, qpos, qstart, qkv_out_first, qkv_out_second = alongside
    inputs = inputs.astype(F32)
    normed_one = (inputs * scale_of(inputs)).astype(BF16)
    rows_one = gather_row(normed_one)

    qkv_out_halves = [qkv_out_first, qkv_out_second]
    mine = ring_join(qkv_out_halves, lax.optimization_barrier(ring_send(qkv_out_halves)), low, 0)
    mine = mine.reshape(2, *qkv_out.shape)
    theirs = trade_core(mine)
    (cot_rows,), _ = to_full_width([after(cotangent, mine)], col)
    scaled = lambda v: (v * mlp_gain[:, None]).astype(BF16)
    gate_up = jnp.concatenate([scaled(w_gate), scaled(w_up)], axis=1)
    gu_halves = [after(v, normed_one) for v in cut(gate_up, 2, 0)]
    full_out = jnp.concatenate(
        [mine[0, :, cut_at:], mine[1, :, cut_at:], theirs[0, :, cut_at:], theirs[1, :, cut_at:]],
        axis=1,
    )
    rows_one, gu_halves, full_out, cot_rows = lax.optimization_barrier(
        (rows_one, gu_halves, full_out, cot_rows)
    )

    shape = lambda kind, *dims: jax.ShapeDtypeStruct(dims, kind)
    scratch = lambda kind, *dims: pltpu.VMEM(dims, kind)
    width = inputs.shape[1]
    matmul = lambda rows, depth, columns: 2 * rows * depth * columns
    query, pairs = kernel_call(
        project,
        (shape(BF16, heads * HD, span), shape(BF16, 2 * HD, span)),
        (rows_one, mine, theirs, cosine, sine),
        matmul(span, width, cut_at),
        staged=(0,),
    )
    grad_rows = gather_row(after(cot_rows, query))
    all_pairs = jnp.stack([pairs] + [trade_col(pairs, m) for m in (1, 2, 3)])
    gu_halves = [after(v, all_pairs) for v in gu_halves]
    gu_got = ring_send(gu_halves)

    flops = 2 * matmul(heads * span, HD, group)
    keys_shape = (4, HD, span), (4, span, HD)
    mixed, mixed_low, lse = kernel_call(
        attend,
        (shape(F32, heads * HD, span), shape(BF16, heads * HD, span), shape(F32, heads, span)),
        (query, all_pairs, key_offset, qpos, qstart),
        flops,
        scratch=[scratch(BF16, *keys_shape[i]) for i in (0, 0, 1, 1)],
    )
    mixed_low, grad_rows = lax.optimization_barrier((mixed_low, grad_rows))
    branch = product(mixed_low, full_out, ((0,), (0,)), BF16)
    branch_parts = collect_row(row_parts(branch, row))
    gu_mine = ring_join(gu_halves, after(gu_got, branch), low, 0)
    down_halves = [after(v, branch_parts[1]) for v in cut(w_down, 2, 0)]
    down_got = ring_send(down_halves)
    branch_parts = after(branch_parts, gu_mine)
    hidden, normed_two = rows_call(add_and_norm, (F32, BF16), (inputs, *branch_parts))
    down_mine = ring_join(down_halves, after(down_got, hidden), low, 1)
    full_down = jnp.concatenate([down_mine, trade_core(down_mine)], axis=1)
    grad_inner = product(grad_rows, full_down, ((1,), (1,)))
    gu_theirs = trade_core(after(gu_mine, hidden))
    rows_two = gather_row(normed_two)

    side = lambda v, which: v[:, which * width // 2 : (which + 1) * width // 2]
    both_cores = lambda v, axis=0: jnp.concatenate([v, trade_core(v)], axis=axis)
    half_of = lambda v: jnp.concatenate([side(v, 0), trade_core(side(v, 1))])

    def half_by_ring(v):
        blocks = [cut(v, 8, 1)[i] for i in (0, 2, 1, 3, 4, 6, 5, 7)]
        sides = [jnp.concatenate(blocks[:4], axis=1), jnp.concatenate(blocks[4:], axis=1)]
        return jnp.concatenate([sides[0], trade_core(sides[1])])

    token_sum = lambda a, b: product(a, b, ((0,), (0,)), BF16)
    cot_half, heads_both = half_by_ring(after(grad_rows, hidden)), both_cores(after(mixed_low, hidden), 1)
    one_half = half_of(after(rows_one, hidden))
    rows_two, cot_half, heads_both, one_half = lax.optimization_barrier(
        (rows_two, cot_half, heads_both, one_half)
    )
    two_half = half_by_ring(rows_two)
    inner, grad_pair, part_two = kernel_call(
        feed,
        (shape(BF16, span, units), shape(BF16, span, 2 * units), shape(BF16, span, width)),
        (rows_two, grad_inner, gu_mine, gu_theirs),
        2 * matmul(span, width, 2 * units),
        scratch=(scratch(BF16, width, 2 * units), pltpu.SemaphoreType.DMA((len(feed_groups(units)), 4))),
        outside=(2, 3),
    )
    inner_both = both_cores(inner)
    pair_both = both_cores(grad_pair)
    mlp_sums = jnp.concatenate([token_sum(two_half, pair_both), token_sum(cot_half, inner_both)], axis=1)
    grad_n2, mlp_sums = lax.optimization_barrier((sum_row(part_two), mlp_sums))
    mlp_sums = lax.psum_scatter(mlp_sums, ("xh", "xl", "z"), scatter_dimension=0, tiled=True)
    grad_hidden, grad_low = rows_call(norm_back_low, (F32, BF16), (hidden, grad_n2, cot_rows))
    branch_parts = spread_row(grad_low)
    result_parts = row_parts(product(inner, full_down, ((1,), (0,)), BF16), row)
    branch_parts, result_parts = lax.optimization_barrier((branch_parts, result_parts))
    grad_heads = kernel_call(
        spread_heads,
        shape(BF16, heads * HD, span),
        (row.astype(jnp.int32)[None], full_out, *branch_parts),
        matmul(span, width, heads * HD),
        scalars=1,
    )
    pair_shape = shape(BF16, 2 * HD, span)
    known = (query, all_pairs, key_offset, qpos, qstart, mixed, lse, grad_heads, cosine, sine)
    half_heads = shape(BF16, heads * HD // 2, span)
    keys_scratch = [scratch(BF16, *keys_shape[i]) for i in (0, 1, 1)]
    key_sums = (shape(F32, *keys_shape[0]),) * 2
    split = functools.partial(attend_back, count=heads // 2)
    result_near = trade_near(result_parts, trade_row)
    gq_first, *key_grads = kernel_call(
        functools.partial(split, first=0, last_call=False),
        (half_heads,) + key_sums,
        known,
        flops * 5 // 4,
        scratch=keys_scratch,
        staged=(1,),
    )
    key_grads, result_near = lax.optimization_barrier((key_grads, result_near))
    result_far = trade_row(after(result_parts[2], result_near), 2)
    gq_last, *grad_pairs = kernel_call(
        functools.partial(split, first=heads // 2, last_call=True),
        (half_heads,) + (pair_shape,) * 4,
        (*known, *key_grads),
        flops * 5 // 4,
        scratch=keys_scratch + [scratch(F32, *keys_shape[0])] * 2,
        staged=(1,),
    )
    grad_pairs = [grad_pairs[0]] + [trade_col(grad_pairs[m], m) for m in (1, 2, 3)]
    grad_pairs = lax.optimization_barrier(grad_pairs)
    grad_qkv, part_one = kernel_call(
        project_back,
        (shape(BF16, cut_at, span), shape(BF16, span, width)),
        (gq_first, gq_last, *grad_pairs, cosine, sine, mine, theirs),
        matmul(span, width, cut_at),
    )
    qkv_both = both_cores(grad_qkv, 1)
    branch_rows = jnp.concatenate(in_order(after(branch_parts, grad_qkv), row))
    branch_half = half_of(branch_rows)
    qkv_sum = product(one_half, qkv_both, ((0,), (1,)), BF16).reshape(2, width // 4, -1)
    out_sum = product(branch_half, heads_both, ((0,), (1,)), BF16).reshape(2, width // 4, -1)
    both_parts = deep_parts(jnp.concatenate([qkv_sum, out_sum], axis=2), deep)
    both_sums = exchange(both_parts, trade_deep)
    rows_here = mlp_sums.shape[0]
    rows_here = mlp_sums.shape[0]
    own_rows = lambda w: lax.dynamic_slice_in_dim(w, (high * 4 + deep) * rows_here, rows_here, 0)
    own_gain = jnp.sum(own_rows(w_gate) * mlp_sums[:, :units].astype(F32), axis=1, keepdims=True)
    own_gain += jnp.sum(own_rows(w_up) * mlp_sums[:, units : 2 * units].astype(F32), axis=1, keepdims=True)
    own_gain = jnp.broadcast_to(own_gain, (rows_here, 128))
    own_gain = own_gain + trade_row(own_gain, 1)
    own_gain = (own_gain + trade_row(own_gain, 2)).astype(BF16)
    mlp_sums = jnp.concatenate([mlp_sums, own_gain], axis=1)
    mlp_sums, both_sums = lax.optimization_barrier((mlp_sums, both_sums))
    mlp_total = ring_gather(mlp_sums, high)
    both_total = exchange(ring_parts([both_sums], low, high), trade_ring)
    mlp_total, both_total = lax.optimization_barrier((mlp_total, both_total))
    mlp_total = lax.all_gather(mlp_total, "z", axis=0, tiled=True)
    both_total = ring_gather(both_total, high)
    grad_n1 = sum_row(part_one)
    (grad_in,) = rows_call(norm_back_high, (F32,), (inputs, grad_n1, grad_hidden))
    both_total, grad_in, result_far = lax.optimization_barrier((both_total, to_blocks(grad_in, col), result_far))
    both_total = deep_gather(both_total, deep).astype(F32)
    result = (hidden + result_parts[0].astype(F32)) + result_far.astype(F32)
    result = (result + sum(part.astype(F32) for part in result_near)).astype(BF16)
    result = to_blocks(result, col)
    both_total, result = lax.optimization_barrier((both_total, result))
    qkv_total, out_total = both_total[:, :cut_at], both_total[:, cut_at:]
    qkv_gain = jnp.sum(flat_qkv * qkv_total, axis=1)[None]
    qkv_gain = sum([trade_row(qkv_gain, j) for j in (1, 2, 3)], qkv_gain)[0]
    mlp_total = mlp_total.reshape(4, 2, rows_here, -1).swapaxes(0, 1).reshape(mlp_total.shape)
    piece = lambda first: mlp_total[:, first : first + units].astype(F32)
    return (
        result,
        grad_in,
        qkv_gain,
        (qkv_total * attn_gain[:, None]).reshape(w_qkv.shape),
        out_total.T,
        mlp_total[:, 3 * units].astype(F32),
        piece(0) * mlp_gain[:, None],
        piece(units) * mlp_gain[:, None],
        piece(2 * units).T,
    )


def solution(mesh):
    dp, rows, cols = mesh.devices.shape
    fine = Mesh(
        mesh.devices.reshape(dp // 2, 2, rows, cols // 2, 2), ("z", "xh", "y", "xl", "k")
    )
    tokens = P(("z", "xh", "y"), COL)
    in_specs = (
        tokens, P(("z", "xh")), P(COL), P(COL, "y", None), P("y", COL), P(COL),
        P(COL, "y"), P(COL, "y"), P("y", COL), tokens,
    )
    out_specs = (
        tokens, tokens, P(COL), P(COL, "y", None), P("y", COL), P(COL),
        P(COL, "y"), P(COL, "y"), P("y", COL),
    )
    return jax.shard_map(
        on_device, mesh=fine, in_specs=in_specs, out_specs=out_specs, check_vma=False
    )
```

```python
import functools

import jax
import jax.numpy as jnp
from jax import lax
from jax.experimental import pallas as pl
from jax.experimental.pallas import tpu as pltpu
from jax.sharding import Mesh
from jax.sharding import PartitionSpec as P

HD = 64
norm_eps = 1e-05
rope_base = 10000.0
masked = -1e30

COL = ("xl", "k")
RING = ("xh", "xl")
BF16 = jnp.bfloat16
F32 = jnp.float32


def trade(values, axes, mask, size=4):
    return lax.ppermute(values, axes, [(i, i ^ mask) for i in range(size)])


def trade_row(values, mask):
    return trade(values, "y", mask)


def trade_col(values, mask):
    return trade(values, COL, mask)


def trade_core(values):
    return trade(values, "k", 1, 2)


def trade_ring(values, mask):
    return trade(values, RING, mask)


def trade_deep(values, mask):
    return trade(values, "z", mask)


def after(values, *earlier):
    return lax.optimization_barrier((values, earlier))[0]


def pick(bit, zero, one):
    return jnp.where(bit == 0, zero, one)


def in_order(parts, index):
    low, high = index % 2, index // 2
    a, b, c, d = parts
    a, b = pick(low, a, b), pick(low, b, a)
    c, d = pick(low, c, d), pick(low, d, c)
    return [pick(high, a, c), pick(high, b, d), pick(high, c, a), pick(high, d, b)]


def cut(values, count, axis):
    return jnp.split(values, count, axis)


def gather_row(values):
    return lax.all_gather(values, "y", axis=0, tiled=True)


def sum_row(partial):
    return lax.psum_scatter(partial, "y", scatter_dimension=0, tiled=True)


def spread_row(values):
    return [values] + [trade_row(values, j) for j in (1, 2, 3)]


def row_parts(partial, row):
    size = partial.shape[0] // 4
    return [lax.dynamic_slice_in_dim(partial, (row ^ j) * size, size, 0) for j in range(4)]


def collect_row(parts):
    return [parts[0]] + [trade_row(parts[j], j) for j in (1, 2, 3)]


def by_width(parts, low):
    return [
        pick(low, parts[core + 2 * place], parts[core + 2 * (1 - place)])
        for core in range(2)
        for place in range(2)
    ]


def of_width(values, low):
    blocks = cut(values, 4, 1)
    return [
        pick(low, blocks[2 * core + place], blocks[2 * core + 1 - place])
        for place in range(2)
        for core in range(2)
    ]


def to_full_width(values, col, *alongside):
    size = values[0].shape[0] // 4
    send = lambda m: jnp.concatenate(
        [lax.dynamic_slice_in_dim(v, (col ^ m) * size, size, 0) for v in values], axis=1
    )
    parts = [send(0)] + [trade_col(send(m), m) for m in (1, 2, 3)]
    parts, alongside = lax.optimization_barrier((parts, alongside))
    parts = [cut(part, len(values), 1) for part in parts]
    rows = [
        jnp.concatenate(by_width([part[i] for part in parts], col // 2), axis=1)
        for i in range(len(values))
    ]
    return rows, alongside


def to_blocks(values, col):
    parts = of_width(values, col // 2)
    kind = values.dtype
    parts = [parts[0]] + [trade_col(parts[m].astype(BF16), m).astype(kind) for m in (1, 2, 3)]
    return jnp.concatenate(in_order(parts, col), axis=0)


def ring_send(halves):
    return [trade_ring(halves[0], 1), trade_ring(halves[1], 3)]


def ring_join(halves, got, low, axis):
    shard, other = jnp.concatenate(halves), jnp.concatenate(got)
    return jnp.concatenate([pick(low, shard, other), pick(low, other, shard)], axis=axis)


def add_low(*terms):
    total = terms[0].astype(F32)
    for term in terms[1:]:
        total = total + term.astype(F32)
    return total.astype(BF16)


def at(values, index):
    return lax.dynamic_index_in_dim(values, index, 0, keepdims=False)


def ring_parts(blocks, low, high):
    half = blocks[0].shape[1] // 2
    take = lambda place, which: jnp.concatenate(
        [
            lax.dynamic_slice(v, (place, which * half, 0), (1, half, v.shape[2]))[0]
            for v in blocks
        ],
        axis=1,
    )
    return [take(low, high), take(1 - low, high), take(low, 1 - high), take(1 - low, 1 - high)]


def deep_parts(blocks, deep):
    size = blocks.shape[-2] // 4
    return [
        lax.dynamic_slice_in_dim(blocks, (deep ^ j) * size, size, blocks.ndim - 2) for j in range(4)
    ]


def trade_near(parts, trader):
    return [trader(parts[1], 1), trader(parts[3], 3)]


def exchange(parts, trader):
    return add_low(parts[0], *lax.optimization_barrier([trader(parts[j], j) for j in (1, 2, 3)]))


def ring_gather(values, high):
    other = trade_ring(values, 2)
    return jnp.concatenate([pick(high, values, other), pick(high, other, values)], axis=0)


def deep_gather(values, deep):
    parts = lax.optimization_barrier([values] + [trade_deep(values, j) for j in (1, 2, 3)])
    return jnp.concatenate(in_order(parts, deep), axis=0)


def product(left, right, dims, kind=F32):
    return lax.dot_general(left, right, (dims, ((), ())), preferred_element_type=F32).astype(kind)


def scale_of(values):
    return lax.rsqrt(jnp.mean(values * values, axis=1, keepdims=True) + norm_eps)


def add_and_norm(base_ref, p0, p1, p2, p3, hidden_ref, normed_ref):
    hidden = (p0[...].astype(F32) + p1[...].astype(F32)) + (p2[...].astype(F32) + p3[...].astype(F32))
    hidden = base_ref[...] + hidden
    hidden_ref[...] = hidden
    normed_ref[...] = (hidden * scale_of(hidden)).astype(BF16)


def norm_back(values, weighted, passed):
    scale = scale_of(values)
    inner = jnp.mean(weighted * values, axis=1, keepdims=True)
    return passed + (scale * weighted - values * (scale**3 * inner))


def norm_back_low(values_ref, part_ref, passed_ref, grad_ref, low_ref):
    grad = norm_back(values_ref[...], part_ref[...].astype(F32), passed_ref[...].astype(F32))
    grad_ref[...] = grad
    low_ref[...] = grad.astype(BF16)


def norm_back_high(values_ref, part_ref, passed_ref, grad_ref):
    grad_ref[...] = norm_back(values_ref[...], part_ref[...].astype(F32), passed_ref[...])


def turn(first, second, cosine, sine):
    return first * cosine - second * sine, second * cosine + first * sine


def project(x_ref, mine_ref, theirs_ref, cos_ref, sin_ref, q_ref, kv_ref):
    width = mine_ref.shape[1]
    slots = kv_ref.shape[0] + q_ref.shape[0]
    total = None
    for core, weights in enumerate((mine_ref, theirs_ref)):
        for place in range(2):
            spot = (2 * core + place) * width
            term = jnp.dot(
                x_ref[:, spot : spot + width], weights[place, :, :slots], preferred_element_type=F32
            )
            total = term if total is None else total + term
    turned = total.T
    cosine, sine = cos_ref[...], sin_ref[...]
    half = HD // 2
    heads = q_ref.shape[0] // HD
    for head in range(heads + 1):
        spot = head * HD
        first, second = turn(
            turned[spot : spot + half], turned[spot + half : spot + HD], cosine, sine
        )
        if head < heads:
            q_ref[spot : spot + half, :] = (first * HD**-0.5).astype(BF16)
            q_ref[spot + half : spot + HD, :] = (second * HD**-0.5).astype(BF16)
        else:
            kv_ref[:half, :] = first.astype(BF16)
            kv_ref[half:HD, :] = second.astype(BF16)
    kv_ref[HD:, :] = turned[(heads + 1) * HD :].astype(BF16)


def lay_keys(pairs, kt_ref, vt_ref, kn_ref, vn_ref):
    size = pairs.shape[2] // 4
    for block in range(4):
        for m in range(4):
            piece = pairs[m, :, block * size : (block + 1) * size]
            spot = slice(m * size, (m + 1) * size)
            kt_ref[block, :, spot] = piece[:HD]
            if vt_ref is not None:
                vt_ref[block, :, spot] = piece[HD:]
            natural = piece.astype(F32).T.astype(BF16)
            kn_ref[block, spot, :] = natural[:, :HD]
            vn_ref[block, spot, :] = natural[:, HD:]


def side_by_side(ref, first, count, depth, spot, size):
    return jnp.concatenate(
        [ref[head * depth : (head + 1) * depth, spot : spot + size] for head in range(first, first + count)],
        axis=1,
    )


def admitted(koff_ref, start, qpos, qstart, diagonal, count):
    keys = koff_ref[...] + start
    allowed = keys >= qstart
    if diagonal:
        allowed = allowed & (keys <= qpos)
    return jnp.concatenate([allowed] * count, axis=1)


def attend(
    q_ref, pairs_ref, koff_ref, qpos_ref, qstart_ref, o_ref, low_ref, lse_ref, kt_ref, vt_ref, kn_ref, vn_ref
):
    span = kn_ref.shape[1]
    size = span // 4
    heads = q_ref.shape[0] // HD
    lay_keys(pairs_ref, kt_ref, vt_ref, kn_ref, vn_ref)
    for block in range(4):
        spot = block * size
        qpos, qstart = qpos_ref[:, spot : spot + size], qstart_ref[:, spot : spot + size]
        query = side_by_side(q_ref, 0, heads, HD, spot, size)
        top = jnp.full((1, heads * size), masked, F32)
        total = jnp.zeros((1, heads * size), F32)
        accum = jnp.zeros((HD, heads * size), F32)
        for number in (block, *range(block)):
            scores = jnp.dot(kn_ref[number], query, preferred_element_type=F32)
            allowed = admitted(koff_ref, number * span, qpos, qstart, number == block, heads)
            scores = jnp.where(allowed, scores, masked)
            new_top = jnp.maximum(top, jnp.max(scores, axis=0, keepdims=True))
            weights = jnp.exp(scores - new_top)
            shrink = jnp.exp(top - new_top)
            total = total * shrink + jnp.sum(weights, axis=0, keepdims=True)
            accum = accum * shrink + jnp.dot(
                vt_ref[number], weights.astype(BF16), preferred_element_type=F32
            )
            top = new_top
        result = accum / total
        lse = top + jnp.log(total)
        for head in range(heads):
            piece = result[:, head * size : (head + 1) * size]
            rows = slice(head * HD, (head + 1) * HD)
            o_ref[rows, spot : spot + size] = piece
            low_ref[rows, spot : spot + size] = piece.astype(BF16)
            lse_ref[head : head + 1, spot : spot + size] = lse[:, head * size : (head + 1) * size]


def attend_back(
    q_ref, pairs_ref, koff_ref, qpos_ref, qstart_ref, o_ref, lse_ref, go_ref, cos_ref, sin_ref, *refs,
    first, count, last_call,
):
    if last_call:
        gk_in, gv_in, gq_ref, g0, g1, g2, g3, kt_ref, kn_ref, vn_ref, gk_ref, gv_ref = refs
    else:
        gq_ref, gk_ref, gv_ref, kt_ref, kn_ref, vn_ref = refs
    span = kn_ref.shape[1]
    size = span // 4
    lay_keys(pairs_ref, kt_ref, None, kn_ref, vn_ref)
    gk_ref[...] = gk_in[...] if last_call else jnp.zeros_like(gk_ref)
    gv_ref[...] = gv_in[...] if last_call else jnp.zeros_like(gv_ref)
    last = (((1,), (1,)), ((), ()))
    for block in range(4):
        spot = block * size
        here = slice(spot, spot + size)
        qpos, qstart = qpos_ref[:, here], qstart_ref[:, here]
        cosine, sine = cos_ref[:, here], sin_ref[:, here]
        pick_heads = lambda ref, depth: side_by_side(ref, first, count, depth, spot, size)
        query, grad_out = pick_heads(q_ref, HD), pick_heads(go_ref, HD)
        lse = pick_heads(lse_ref, 1)
        delta = jnp.sum(grad_out.astype(F32) * pick_heads(o_ref, HD), axis=0, keepdims=True)
        grad_query = jnp.zeros((HD, count * size), F32)
        for number in (block, *range(block)):
            scores = jnp.dot(kn_ref[number], query, preferred_element_type=F32)
            allowed = admitted(koff_ref, number * span, qpos, qstart, number == block, count)
            probs = jnp.exp(jnp.where(allowed, scores - lse, masked))
            grad_probs = jnp.dot(vn_ref[number], grad_out, preferred_element_type=F32)
            grad_scores = (probs * (grad_probs - delta)).astype(BF16)
            gv_ref[number] += lax.dot_general(
                grad_out, probs.astype(BF16), last, preferred_element_type=F32
            )
            gk_ref[number] += lax.dot_general(query, grad_scores, last, preferred_element_type=F32)
            grad_query = grad_query + jnp.dot(
                kt_ref[number], grad_scores, preferred_element_type=F32
            )
        half = HD // 2
        for head in range(count):
            grad = grad_query[:, head * size : (head + 1) * size] * HD**-0.5
            upper, lower = turn(grad[:half], grad[half:], cosine, -sine)
            gq_ref[head * HD : head * HD + half, here] = upper.astype(BF16)
            gq_ref[head * HD + half : (head + 1) * HD, here] = lower.astype(BF16)
    if last_call:
        for block in range(4):
            for m, ref in enumerate((g0, g1, g2, g3)):
                spot, out = slice(m * size, (m + 1) * size), slice(block * size, (block + 1) * size)
                ref[:HD, out] = gk_ref[block, :, spot].astype(BF16)
                ref[HD:, out] = gv_ref[block, :, spot].astype(BF16)


def project_back(
    gq0, gq1, g0, g1, g2, g3, cos_ref, sin_ref, mine_ref, theirs_ref, gqkv_ref, part_ref
):
    pair = g0[...].astype(F32) + g1[...].astype(F32) + (g2[...].astype(F32) + g3[...].astype(F32))
    half = HD // 2
    first, second = turn(pair[:half], pair[half:HD], cos_ref[...], -sin_ref[...])
    turned = jnp.concatenate(
        [gq0[...].astype(F32), gq1[...].astype(F32), first, second, pair[HD:]], axis=0
    )
    gqkv_ref[...] = turned.astype(BF16)
    natural = turned.T.astype(BF16)
    width = mine_ref.shape[1]
    slots = turned.shape[0]
    for core, weights in enumerate((mine_ref, theirs_ref)):
        for place in range(2):
            spot = (2 * core + place) * width
            part = lax.dot_general(
                natural, weights[place, :, :slots], (((1,), (1,)), ((), ())), preferred_element_type=F32
            )
            part_ref[:, spot : spot + width] = part.astype(BF16)


def feed(h_ref, gi_ref, own_ref, other_ref, inner_ref, pair_ref, part_ref, w_ref, sems):
    units = gi_ref.shape[1]
    depth = own_ref.shape[0]
    groups = feed_groups(units)
    copies = []
    for group, (begin, end) in enumerate(groups):
        mine = []
        for core, ref in enumerate((own_ref, other_ref)):
            for start in (0, units):
                columns = pl.ds(start + begin, end - begin)
                copy = pltpu.make_async_copy(
                    ref.at[:, columns],
                    w_ref.at[pl.ds(core * depth, depth), columns],
                    sems.at[group, len(mine)],
                )
                copy.start()
                mine.append(copy)
        copies.append(mine)
    for (begin, end), mine in zip(groups, copies):
        for copy in mine:
            copy.wait()
        gate = jnp.dot(h_ref[...], w_ref[:, begin:end], preferred_element_type=F32)
        up = jnp.dot(h_ref[...], w_ref[:, units + begin : units + end], preferred_element_type=F32)
        grad_inner = gi_ref[:, begin:end]
        sig = 1.0 / (1.0 + jnp.exp(-gate))
        act = gate * sig
        inner_ref[:, begin:end] = (act * up).astype(BF16)
        grad_gate = grad_inner * up * (sig * (1.0 + gate * (1.0 - sig)))
        pair_ref[:, begin:end] = grad_gate.astype(BF16)
        pair_ref[:, units + begin : units + end] = (grad_inner * act).astype(BF16)
    for begin in range(0, 2 * depth, 512):
        part = lax.dot_general(
            pair_ref[...], w_ref[begin : begin + 512, :], (((1,), (1,)), ((), ())),
            preferred_element_type=F32,
        )
        part_ref[:, begin : begin + 512] = part.astype(BF16)


def feed_groups(units):
    ends = [128, 384] + list(range(896, units, 512)) + [units]
    return list(zip([0] + ends[:-1], ends))


def spread_heads(row_ref, w_ref, b0, b1, b2, b3, out_ref):
    size = b0.shape[0]
    for j, part in enumerate((b0, b1, b2, b3)):
        spot = pl.multiple_of((row_ref[0] ^ j) * size, size)
        piece = lax.dot_general(
            w_ref[...], part[...], (((1,), (1,)), ((), ())), preferred_element_type=F32
        )
        out_ref[:, pl.ds(spot, size)] = piece.astype(BF16)


def kernel_call(body, out_shape, operands, flops, scratch=(), scalars=0, outside=(), staged=(), mib=48):
    moved = sum(x.size * x.dtype.itemsize for x in operands)
    count = len(operands)
    spaces = [
        pltpu.SMEM if i < scalars else pl.ANY if i in outside or i in staged else pltpu.VMEM
        for i in range(count)
    ]
    if staged:
        held = [pltpu.VMEM(operands[i].shape, operands[i].dtype) for i in staged]
        scratch = [*scratch, *held, pltpu.SemaphoreType.DMA((len(staged),))]

        def whole(*refs):
            refs, buffers, sems = list(refs[: -len(staged) - 1]), refs[-len(staged) - 1 : -1], refs[-1]
            copies = [
                pltpu.make_async_copy(refs[i], buffer, sems.at[n])
                for n, (i, buffer) in enumerate(zip(staged, buffers))
            ]
            for copy in copies:
                copy.start()
            for copy in copies:
                copy.wait()
            for i, buffer in zip(staged, buffers):
                refs[i] = buffer
            body(*refs)
    else:
        whole = body
    out_specs = jax.tree.map(lambda _: pl.BlockSpec(memory_space=pltpu.VMEM), out_shape)
    return pl.pallas_call(
        whole,
        out_shape=out_shape,
        in_specs=[pl.BlockSpec(memory_space=space) for space in spaces],
        out_specs=out_specs,
        scratch_shapes=list(scratch),
        compiler_params=pltpu.CompilerParams(vmem_limit_bytes=mib * 1024 * 1024),
        cost_estimate=pl.CostEstimate(flops=flops, bytes_accessed=moved, transcendentals=0),
    )(*operands)


def rows_call(body, kinds, operands, steps=2):
    rows, width = operands[0].shape
    block = pl.BlockSpec((rows // steps, width), lambda i: (i, 0))
    out_shape = tuple(jax.ShapeDtypeStruct((rows, width), kind) for kind in kinds)
    moved = sum(x.size * x.dtype.itemsize for x in operands)
    return pl.pallas_call(
        body,
        out_shape=out_shape,
        grid=(steps,),
        in_specs=[block] * len(operands),
        out_specs=(block,) * len(kinds),
        cost_estimate=pl.CostEstimate(flops=0, bytes_accessed=moved, transcendentals=0),
    )(*operands)


def on_device(
    tokens_in, segment_ids, attn_gain, w_qkv, w_out, mlp_gain, w_gate, w_up, w_down, cotangent
):
    group = segment_ids.shape[0]
    span = group // 4
    size = span // 4
    units = w_gate.shape[1]
    slots = w_qkv.shape[2] // HD
    heads = slots - 2
    deep, high, row = lax.axis_index("z"), lax.axis_index("xh"), lax.axis_index("y")
    low, core = lax.axis_index("xl"), lax.axis_index("k")
    col = low * 2 + core

    indices = jnp.arange(group, dtype=jnp.int32)
    previous = jnp.concatenate([segment_ids[:1] - 1, segment_ids[:-1]])
    starts = lax.cummax(jnp.where(segment_ids != previous, indices, 0), axis=0)
    bases = [j * span + col * size for j in range(4)]
    my_starts = jnp.concatenate([lax.dynamic_slice_in_dim(starts, b, size, 0) for b in bases])
    lanes = jnp.arange(size, dtype=jnp.int32)
    my_index = jnp.concatenate([lanes + b for b in bases])
    half_dim = HD // 2
    inverse_freq = rope_base ** (-jnp.arange(half_dim, dtype=F32) * 2.0 / HD)
    angles = inverse_freq[:, None] * (my_index - my_starts).astype(F32)[None, :]
    cosine, sine = jnp.cos(angles), jnp.sin(angles)
    key_offset = jnp.concatenate([lanes + (col ^ m) * size for m in range(4)])
    key_offset = jnp.broadcast_to(key_offset[:, None], (span, size))
    qpos, qstart = my_index[None, :], my_starts[None, :]
    cut_at = slots * HD

    flat_qkv = w_qkv.reshape(w_qkv.shape[0], -1)
    qkv_out = jnp.concatenate([(flat_qkv * attn_gain[:, None]).astype(BF16), w_out], axis=1)
    (inputs,), alongside = to_full_width(
        [tokens_in], col, cosine, sine, key_offset, qpos, qstart, *cut(qkv_out, 2, 0)
    )
    cosine, sine, key_offset, qpos, qstart, qkv_out_first, qkv_out_second = alongside
    inputs = inputs.astype(F32)
    normed_one = (inputs * scale_of(inputs)).astype(BF16)
    rows_one = gather_row(normed_one)

    qkv_out_halves = [qkv_out_first, qkv_out_second]
    mine = ring_join(qkv_out_halves, lax.optimization_barrier(ring_send(qkv_out_halves)), low, 0)
    mine = mine.reshape(2, *qkv_out.shape)
    theirs = trade_core(mine)
    (cot_rows,), _ = to_full_width([after(cotangent, mine)], col)
    scaled = lambda v: (v * mlp_gain[:, None]).astype(BF16)
    gate_up = jnp.concatenate([scaled(w_gate), scaled(w_up)], axis=1)
    gu_halves = [after(v, normed_one) for v in cut(gate_up, 2, 0)]
    full_out = jnp.concatenate(
        [mine[0, :, cut_at:], mine[1, :, cut_at:], theirs[0, :, cut_at:], theirs[1, :, cut_at:]],
        axis=1,
    )
    rows_one, gu_halves, full_out, cot_rows = lax.optimization_barrier(
        (rows_one, gu_halves, full_out, cot_rows)
    )
    gu_got = ring_send(gu_halves)

    shape = lambda kind, *dims: jax.ShapeDtypeStruct(dims, kind)
    scratch = lambda kind, *dims: pltpu.VMEM(dims, kind)
    width = inputs.shape[1]
    matmul = lambda rows, depth, columns: 2 * rows * depth * columns
    query, pairs = kernel_call(
        project,
        (shape(BF16, heads * HD, span), shape(BF16, 2 * HD, span)),
        (rows_one, mine, theirs, cosine, sine),
        matmul(span, width, cut_at),
        staged=(0,),
    )
    grad_rows = gather_row(after(cot_rows, query))
    all_pairs = jnp.stack([pairs] + [trade_col(pairs, m) for m in (1, 2, 3)])

    flops = 2 * matmul(heads * span, HD, group)
    keys_shape = (4, HD, span), (4, span, HD)
    mixed, mixed_low, lse = kernel_call(
        attend,
        (shape(F32, heads * HD, span), shape(BF16, heads * HD, span), shape(F32, heads, span)),
        (query, all_pairs, key_offset, qpos, qstart),
        flops,
        scratch=[scratch(BF16, *keys_shape[i]) for i in (0, 0, 1, 1)],
    )
    branch = product(mixed_low, full_out, ((0,), (0,)), BF16)
    gu_mine = ring_join(gu_halves, after(gu_got, branch), low, 0)
    down_halves = [after(v, branch, gu_got) for v in cut(w_down, 2, 0)]
    down_got = ring_send(down_halves)
    down_mine = ring_join(down_halves, down_got, low, 1)
    branch_parts = after(collect_row(row_parts(branch, row)), gu_mine, down_mine)
    hidden, normed_two = rows_call(add_and_norm, (F32, BF16), (inputs, *branch_parts))
    down_mine = after(down_mine, hidden)
    full_down = jnp.concatenate([down_mine, trade_core(down_mine)], axis=1)
    grad_inner = product(grad_rows, full_down, ((1,), (1,)))
    gu_theirs = trade_core(after(gu_mine, hidden))
    rows_two = gather_row(normed_two)

    side = lambda v, which: v[:, which * width // 2 : (which + 1) * width // 2]
    both_cores = lambda v, axis=0: jnp.concatenate([v, trade_core(v)], axis=axis)
    half_of = lambda v: jnp.concatenate([side(v, 0), trade_core(side(v, 1))])

    def half_by_ring(v):
        blocks = [cut(v, 8, 1)[i] for i in (0, 2, 1, 3, 4, 6, 5, 7)]
        sides = [jnp.concatenate(blocks[:4], axis=1), jnp.concatenate(blocks[4:], axis=1)]
        return jnp.concatenate([sides[0], trade_core(sides[1])])

    token_sum = lambda a, b: product(a, b, ((0,), (0,)), BF16)
    cot_half, heads_both = half_by_ring(after(grad_rows, hidden)), both_cores(after(mixed_low, hidden), 1)
    one_half = half_of(after(rows_one, hidden))
    rows_two, cot_half, heads_both, one_half = lax.optimization_barrier(
        (rows_two, cot_half, heads_both, one_half)
    )
    two_half = half_by_ring(rows_two)
    inner, grad_pair, part_two = kernel_call(
        feed,
        (shape(BF16, span, units), shape(BF16, span, 2 * units), shape(BF16, span, width)),
        (rows_two, grad_inner, gu_mine, gu_theirs),
        2 * matmul(span, width, 2 * units),
        scratch=(scratch(BF16, width, 2 * units), pltpu.SemaphoreType.DMA((len(feed_groups(units)), 4))),
        outside=(2, 3),
    )
    inner_both = both_cores(inner)
    pair_both = both_cores(grad_pair)
    mlp_sums = jnp.concatenate([token_sum(two_half, pair_both), token_sum(cot_half, inner_both)], axis=1)
    grad_n2, mlp_sums = lax.optimization_barrier((sum_row(part_two), mlp_sums))
    mlp_sums = lax.psum_scatter(mlp_sums, ("xh", "xl", "z"), scatter_dimension=0, tiled=True)
    grad_hidden, grad_low = rows_call(norm_back_low, (F32, BF16), (hidden, grad_n2, cot_rows))
    branch_parts = spread_row(grad_low)
    result_parts = row_parts(product(inner, full_down, ((1,), (0,)), BF16), row)
    branch_parts, result_parts = lax.optimization_barrier((branch_parts, result_parts))
    grad_heads = kernel_call(
        spread_heads,
        shape(BF16, heads * HD, span),
        (row.astype(jnp.int32)[None], full_out, *branch_parts),
        matmul(span, width, heads * HD),
        scalars=1,
    )
    pair_shape = shape(BF16, 2 * HD, span)
    known = (query, all_pairs, key_offset, qpos, qstart, mixed, lse, grad_heads, cosine, sine)
    half_heads = shape(BF16, heads * HD // 2, span)
    keys_scratch = [scratch(BF16, *keys_shape[i]) for i in (0, 1, 1)]
    key_sums = (shape(F32, *keys_shape[0]),) * 2
    split = functools.partial(attend_back, count=heads // 2)
    result_near = trade_near(result_parts, trade_row)
    gq_first, *key_grads = kernel_call(
        functools.partial(split, first=0, last_call=False),
        (half_heads,) + key_sums,
        known,
        flops * 5 // 4,
        scratch=keys_scratch,
        staged=(1,),
    )
    key_grads, result_near = lax.optimization_barrier((key_grads, result_near))
    result_far = trade_row(after(result_parts[2], result_near), 2)
    gq_last, *grad_pairs = kernel_call(
        functools.partial(split, first=heads // 2, last_call=True),
        (half_heads,) + (pair_shape,) * 4,
        (*known, *key_grads),
        flops * 5 // 4,
        scratch=keys_scratch + [scratch(F32, *keys_shape[0])] * 2,
        staged=(1,),
    )
    grad_pairs = [grad_pairs[0]] + [trade_col(grad_pairs[m], m) for m in (1, 2, 3)]
    grad_pairs = lax.optimization_barrier(grad_pairs)
    grad_qkv, part_one = kernel_call(
        project_back,
        (shape(BF16, cut_at, span), shape(BF16, span, width)),
        (gq_first, gq_last, *grad_pairs, cosine, sine, mine, theirs),
        matmul(span, width, cut_at),
    )
    qkv_both = both_cores(grad_qkv, 1)
    branch_rows = jnp.concatenate(in_order(after(branch_parts, grad_qkv), row))
    branch_half = half_of(branch_rows)
    qkv_sum = product(one_half, qkv_both, ((0,), (1,)), BF16).reshape(2, width // 4, -1)
    out_sum = product(branch_half, heads_both, ((0,), (1,)), BF16).reshape(2, width // 4, -1)
    both_parts = deep_parts(jnp.concatenate([qkv_sum, out_sum], axis=2), deep)
    both_sums = exchange(both_parts, trade_deep)
    rows_here = mlp_sums.shape[0]
    rows_here = mlp_sums.shape[0]
    own_rows = lambda w: lax.dynamic_slice_in_dim(w, (high * 4 + deep) * rows_here, rows_here, 0)
    own_gain = jnp.sum(own_rows(w_gate) * mlp_sums[:, :units].astype(F32), axis=1, keepdims=True)
    own_gain += jnp.sum(own_rows(w_up) * mlp_sums[:, units : 2 * units].astype(F32), axis=1, keepdims=True)
    own_gain = jnp.broadcast_to(own_gain, (rows_here, 128))
    own_gain = own_gain + trade_row(own_gain, 1)
    own_gain = (own_gain + trade_row(own_gain, 2)).astype(BF16)
    mlp_sums = jnp.concatenate([mlp_sums, own_gain], axis=1)
    mlp_sums, both_sums = lax.optimization_barrier((mlp_sums, both_sums))
    mlp_total = ring_gather(mlp_sums, high)
    both_total = exchange(ring_parts([both_sums], low, high), trade_ring)
    mlp_total, both_total = lax.optimization_barrier((mlp_total, both_total))
    mlp_total = lax.all_gather(mlp_total, "z", axis=0, tiled=True)
    both_total = ring_gather(both_total, high)
    grad_n1 = sum_row(part_one)
    (grad_in,) = rows_call(norm_back_high, (F32,), (inputs, grad_n1, grad_hidden))
    both_total, grad_in, result_far = lax.optimization_barrier((both_total, to_blocks(grad_in, col), result_far))
    both_total = deep_gather(both_total, deep).astype(F32)
    result = (hidden + result_parts[0].astype(F32)) + result_far.astype(F32)
    result = (result + sum(part.astype(F32) for part in result_near)).astype(BF16)
    result = to_blocks(result, col)
    both_total, result = lax.optimization_barrier((both_total, result))
    qkv_total, out_total = both_total[:, :cut_at], both_total[:, cut_at:]
    qkv_gain = jnp.sum(flat_qkv * qkv_total, axis=1)[None]
    qkv_gain = sum([trade_row(qkv_gain, j) for j in (1, 2, 3)], qkv_gain)[0]
    mlp_total = mlp_total.reshape(4, 2, rows_here, -1).swapaxes(0, 1).reshape(mlp_total.shape)
    piece = lambda first: mlp_total[:, first : first + units].astype(F32)
    return (
        result,
        grad_in,
        qkv_gain,
        (qkv_total * attn_gain[:, None]).reshape(w_qkv.shape),
        out_total.T,
        mlp_total[:, 3 * units].astype(F32),
        piece(0) * mlp_gain[:, None],
        piece(units) * mlp_gain[:, None],
        piece(2 * units).T,
    )


def solution(mesh):
    dp, rows, cols = mesh.devices.shape
    fine = Mesh(
        mesh.devices.reshape(dp // 2, 2, rows, cols // 2, 2), ("z", "xh", "y", "xl", "k")
    )
    tokens = P(("z", "xh", "y"), COL)
    in_specs = (
        tokens, P(("z", "xh")), P(COL), P(COL, "y", None), P("y", COL), P(COL),
        P(COL, "y"), P(COL, "y"), P("y", COL), tokens,
    )
    out_specs = (
        tokens, tokens, P(COL), P(COL, "y", None), P("y", COL), P(COL),
        P(COL, "y"), P(COL, "y"), P("y", COL),
    )
    return jax.shard_map(
        on_device, mesh=fine, in_specs=in_specs, out_specs=out_specs, check_vma=False
    )
```
